256 devices in a mesh: gx: 8 (over x, y_lo), gy: 4 (over y_hi, core), ka: 8 (over z).
Axes of the slice: x: 4, y: 4 (y_hi: 2, y_lo: 2; y = y_hi * 2 + y_lo), z: 8, core: 2. Of those that a mesh axis runs over, the one named last changes fastest.
Arguments:
- fractional_placements: float32 [3, 65536], P(None, ('gx', 'gy', 'ka')), may hold values from 0 to 1, as said below
- particle_speeds: float32 [3, 65536], P(None, ('gx', 'gy', 'ka')), may hold values from -3 to 3
- element_kinds: int32 [65536], P(('gx', 'gy', 'ka')), may hold values from 0 to 5
- adjacent_padded_indices: int32 [65536, 64], P(('gx', 'gy', 'ka')), may hold values from 0 to 4095, as said below
- adjacent_valid_tally: int32 [65536], P(('gx', 'gy', 'ka')), may hold values from 16 to 64, as said below
- border_particle_rows: int32 [16, 8, 128], P('gx', 'gy'), may hold values from 0 to 2047
- reciprocal_integer_triples: int32 [3, 16384], P(None, 'ka'), may hold values from -16 to 16, as said below
- cell_edge_sizes: float32 [3], replicated, may hold values from 20 to 40
- friction_random_kicks: float32 [3, 65536], P(None, ('gx', 'gy', 'ka')), may hold values from -6 to 6
- element_feature_vectors: float32 [6, 128], replicated, may hold values from -5 to 5
- distance_net_initial_weights: float32 [8, 64], replicated, may hold values from -2 to 2
- distance_net_final_weights: float32 [64, 128], replicated, may hold values from -0.75 to 0.75
- message_blend_matrix: float32 [128, 128], replicated, may hold values from -0.5 to 0.5
- energy_head_initial_weights: float32 [128, 16], replicated, may hold values from -0.5 to 0.5
- energy_head_final_weights: float32 [16], replicated, may hold values from -1.5 to 1.5
- hidden_electric_projection: float32 [128, 8], replicated, may hold values from -0.5 to 0.5
Outputs:
- forces: float32 [3, 65536], P(None, ('gx', 'gy', 'ka'))
- new_positions: float32 [3, 65536], P(None, ('gx', 'gy', 'ka'))
- new_velocities: float32 [3, 65536], P(None, ('gx', 'gy', 'ka'))
The draws below stay inside these ranges and needn't reach their ends.
Inputs may be any that keep to these rules, and one draw needn't show every extreme that they name: `fractional_placements`: domain (X, Y) has first coordinates in [X / 8, (X + 1) / 8) and second ones in [Y / 4, (Y + 1) / 4). `adjacent_padded_indices`: an entry names another atom of the domain or a slot of one of the 12 outer ghost cells, never the atom itself or the 4 inner cells. `adjacent_valid_tally`: on every device some atom has all 64 slots live. `reciprocal_integer_triples`: no triple is all zeros.
All inputs are finite; a program needn't handle non-finite values.
Results may differ from the reference program's by a relative error of at most 0.0003.
Values sent between devices are 32-bit elements; how exact they have to be, the bound alone decides.
No kernel may reach another device: no remote copies, remote signals or barrier semaphores. Data moves between devices by JAX's collectives and lax.ppermute only.
A program may use at most 64 MiB of HBM per device.

```python
import math
import jax
import jax.numpy as jnp
import numpy as np
from jax import lax

ATOM_DEV = 256
MAXN = 64
GHOSTS = 128
C = 128
NB = 8
RH = 64
RO = 16
LATENT = 8
SPECIES = 6
K = 16384
DOM_X = 8
DOM_Y = 4
DOM_ATOMS = 2048
ATOMS = 65536


outer_cells = np.array([0, 1, 2, 3, 4, 7, 8, 11, 12, 13, 14, 15], dtype=np.int32)


def draw_fractional_placements(key, part):
    key = jax.random.fold_in(key, 11)
    atom_ids = jnp.arange(ATOMS, dtype=jnp.int32)
    domain_ids = atom_ids // DOM_ATOMS
    first_index = (domain_ids // DOM_Y).astype(jnp.float32)
    second_index = (domain_ids % DOM_Y).astype(jnp.float32)
    spread = jax.random.uniform(key, (3, ATOMS), jnp.float32)
    return jnp.stack([(first_index + spread[0]) / DOM_X, (second_index + spread[1]) / DOM_Y, spread[2]], 0)


def draw_adjacent_padded_indices(key, part):
    key = jax.random.fold_in(key, 12)
    atom_ids = jnp.arange(ATOMS, dtype=jnp.int32)
    own_slot = (atom_ids % DOM_ATOMS)[:, None]
    picked = jax.random.randint(key, (ATOMS, MAXN), 0, DOM_ATOMS - 1 + 12 * GHOSTS, dtype=jnp.int32)
    inside = picked + (picked >= own_slot).astype(jnp.int32)
    remainder = jnp.maximum(picked - (DOM_ATOMS - 1), 0)
    ghost_entry = DOM_ATOMS + jnp.asarray(outer_cells)[remainder // GHOSTS] * GHOSTS + remainder % GHOSTS
    return jnp.where(picked < DOM_ATOMS - 1, inside, ghost_entry)


def draw_adjacent_valid_tally(key, part):
    key = jax.random.fold_in(key, 13)
    atom_ids = jnp.arange(ATOMS, dtype=jnp.int32)
    counted = jax.random.randint(key, (ATOMS,), MAXN // 4, MAXN + 1, dtype=jnp.int32)
    return jnp.where(atom_ids % ATOM_DEV == 0, MAXN, counted)


def draw_reciprocal_integer_triples(key, part):
    key = jax.random.fold_in(key, 14)
    triples = jax.random.randint(key, (3, K), -16, 17, dtype=jnp.int32)
    vacant = jnp.all(triples == 0, axis=0)
    return triples.at[2].set(jnp.where(vacant, 1, triples[2]))


def touch_ends(values, stream_key, low, largest):
    dims = values.shape
    spot = [jax.random.randint(jax.random.fold_in(stream_key, axis), (), 0, dims[axis]) for axis in range(len(dims))]
    values = values.at[tuple(spot)].set(low)
    longest = dims.index(max(dims))
    spot[longest] = (spot[longest] + 1) % dims[longest]
    return values.at[tuple(spot)].set(largest)


def steps_of(stream_key, shape, cuts, least, top_value):
    loudness, own = 1.0, jax.random.fold_in(stream_key, 6)
    for dim, shards_of in cuts:
        steps = jnp.exp(jax.random.uniform(jax.random.fold_in(own, dim), (shards_of,), jnp.float32, least / len(cuts), top_value / len(cuts)))
        loudness = loudness * jnp.repeat(steps, shape[dim] // shards_of).reshape([-1 if axis == dim else 1 for axis in range(len(shape))])
    return loudness


def centred(own_key, shape, scale, bound, cuts=(), kind=jnp.bfloat16):
    entries = jax.random.normal(own_key, shape, jnp.float32) * scale
    if len(cuts) > 0:
        entries = steps_of(own_key, shape, cuts, -0.22, 0.18) * entries
    return jnp.clip(entries, min=-bound, max=bound).astype(kind)


def setup_inputs(seed: int = 0) -> dict:
    splits = jax.random.split(jax.random.key(seed), 17)
    fractional_placements = draw_fractional_placements(jax.random.fold_in(splits[16], 71), 0)
    particle_speeds = centred(splits[1], (3, ATOMS), 0.5, 3.0, ((1, 256),), jnp.float32)
    element_kinds = touch_ends(jax.random.randint(splits[2], (ATOMS,), 0, SPECIES), jax.random.fold_in(splits[2], 1), 0, SPECIES - 1).astype(jnp.int32)
    adjacent_padded_indices = draw_adjacent_padded_indices(jax.random.fold_in(splits[16], 71), 0)
    adjacent_valid_tally = draw_adjacent_valid_tally(jax.random.fold_in(splits[16], 71), 0)
    border_particle_rows = touch_ends(jax.random.randint(splits[5], (2 * DOM_X, 2 * DOM_Y, GHOSTS), 0, DOM_ATOMS), jax.random.fold_in(splits[5], 1), 0, DOM_ATOMS - 1).astype(jnp.int32)
    reciprocal_integer_triples = draw_reciprocal_integer_triples(jax.random.fold_in(splits[16], 71), 0)
    cell_edge_sizes = jnp.clip(jax.random.uniform(splits[7], (3,), jnp.float32, 20.0, 40.0), 20.0, 40.0)
    friction_random_kicks = centred(splits[8], (3, ATOMS), 1.0, 6.0, ((1, 256),), jnp.float32)
    element_feature_vectors = centred(splits[9], (SPECIES, C), 1.0, 5.0, (), jnp.float32)
    distance_net_initial_weights = centred(splits[10], (NB, RH), NB ** -0.5, 2.0, (), jnp.float32)
    distance_net_final_weights = centred(splits[11], (RH, C), RH ** -0.5, 0.75, (), jnp.float32)
    message_blend_matrix = centred(splits[12], (C, C), C ** -0.5, 0.5, (), jnp.float32)
    energy_head_initial_weights = centred(splits[13], (C, RO), C ** -0.5, 0.5, (), jnp.float32)
    energy_head_final_weights = centred(splits[14], (RO,), RO ** -0.5, 1.5, (), jnp.float32)
    hidden_electric_projection = centred(splits[15], (C, LATENT), C ** -0.5, 0.5, (), jnp.float32)
    return {"fractional_placements": fractional_placements, "particle_speeds": particle_speeds, "element_kinds": element_kinds, "adjacent_padded_indices": adjacent_padded_indices, "adjacent_valid_tally": adjacent_valid_tally, "border_particle_rows": border_particle_rows, "reciprocal_integer_triples": reciprocal_integer_triples, "cell_edge_sizes": cell_edge_sizes, "friction_random_kicks": friction_random_kicks, "element_feature_vectors": element_feature_vectors, "distance_net_initial_weights": distance_net_initial_weights, "distance_net_final_weights": distance_net_final_weights, "message_blend_matrix": message_blend_matrix, "energy_head_initial_weights": energy_head_initial_weights, "energy_head_final_weights": energy_head_final_weights, "hidden_electric_projection": hidden_electric_projection}


highest = lax.Precision.HIGHEST
masses_table = (1.008, 12.011, 15.999, 6.94, 30.974, 18.998)
radial_widths = (2.0, 4.0, 6.0, 8.0, 10.0, 12.0, 14.0, 16.0)
time_step = 0.5
friction = 0.2
gauss_width = 0.3
species_kinds = 6

def product(left_side, right_side):
    return jnp.dot(left_side, right_side, precision=highest, preferred_element_type=jnp.float32)

def one_hot_rows(labels):
    levels = jnp.arange(species_kinds).astype(labels.dtype)
    return (labels[None, :] == levels[:, None]).astype(jnp.float32)

def to_blocks(tensor, position_axis, block_rows):
    dims_of = tensor.shape
    pieces = dims_of[position_axis] // block_rows
    divided = tensor.reshape(dims_of[:position_axis] + (pieces, block_rows) + dims_of[position_axis + 1:])
    return jnp.moveaxis(divided, position_axis, 0)

def from_blocks(tensor, position_axis):
    merged = jnp.moveaxis(tensor, 0, position_axis)
    dims_of = merged.shape
    return merged.reshape(dims_of[:position_axis] + (dims_of[position_axis] * dims_of[position_axis + 1],) + dims_of[position_axis + 2:])

def displacements(extended, listing, centres, cell_edge_sizes):
    nearby = extended[:, listing]
    offsets = nearby[:3] - centres[:, :, None]
    offsets = offsets - jnp.floor(offsets + 0.5)
    return (offsets * cell_edge_sizes[:, None, None], nearby[3])

def pair_messages(displace, labels, live_pairs, element_feature_vectors, distance_net_initial_weights, distance_net_final_weights):
    atom_rows = displace.shape[1]
    list_width = displace.shape[2]
    spacing = jnp.sqrt(lax.optimization_barrier(jnp.sum(displace * displace, axis=0))).reshape(-1)
    scales = jnp.asarray(radial_widths, dtype=jnp.float32)[:, None]
    radial_basis = jnp.exp(-jnp.square(spacing[None, :] / scales))
    hidden = jax.nn.silu(product(distance_net_initial_weights.T, radial_basis))
    radial = product(distance_net_final_weights.T, hidden)
    partner = product(element_feature_vectors.T, one_hot_rows(labels.reshape(-1)))
    weighted = radial * partner * live_pairs.reshape(-1)[None, :]
    return lax.optimization_barrier(jnp.sum(weighted.reshape(-1, atom_rows, list_width), axis=2)) / list_width

def blocked_messages(displace, labels, live_pairs, weights):
    block_rows = min(128, displace.shape[1])

    def one_block(block_items):
        return pair_messages(block_items[0], block_items[1], block_items[2], weights[0], weights[1], weights[2])
    outputs = lax.map(one_block, (to_blocks(displace, 1, block_rows), to_blocks(labels, 0, block_rows), to_blocks(live_pairs, 0, block_rows)))
    return from_blocks(outputs, 1)

def blocked_pullback(displace, labels, live_pairs, upstream, weights):
    block_rows = min(128, displace.shape[1])

    def one_block(block_items):

        def local_map(offsets_in):
            return pair_messages(offsets_in, block_items[1], block_items[2], weights[0], weights[1], weights[2])
        _, backward = jax.vjp(local_map, block_items[0])
        return backward(block_items[3])[0]
    gradients = lax.map(one_block, (to_blocks(displace, 1, block_rows), to_blocks(labels, 0, block_rows), to_blocks(live_pairs, 0, block_rows), to_blocks(upstream, 1, block_rows)))
    return from_blocks(gradients, 1)

def phases(kblock, coords):
    phase_angle = kblock[0][:, None] * coords[0][None, :] + kblock[1][:, None] * coords[1][None, :] + kblock[2][:, None] * coords[2][None, :]
    phase_angle = 2.0 * math.pi * phase_angle
    return (jnp.cos(phase_angle), jnp.sin(phase_angle))

def structure(coords, charges, reciprocal_real_triples, block_cols):

    def one_block(kblock):
        cosine, sine_part = phases(kblock, coords)
        return jnp.stack([product(charges, cosine.T), product(charges, sine_part.T)], 0)
    blockwise = lax.map(one_block, to_blocks(reciprocal_real_triples, 1, block_cols))
    return from_blocks(blockwise, 2)

def kspace_terms(coords, reciprocal_real_triples, cos_weight, sin_weight, block_cols):

    def one_step(running, block_items):
        kblock, first_part, second_part = block_items
        cosine, sine_part = phases(kblock, coords)
        cos_coef = jnp.concatenate([first_part, kblock[0][None] * second_part, kblock[1][None] * second_part, kblock[2][None] * second_part], 0)
        sin_coef = jnp.concatenate([second_part, -kblock[0][None] * first_part, -kblock[1][None] * first_part, -kblock[2][None] * first_part], 0)
        return (running + product(cos_coef, cosine) + product(sin_coef, sine_part), None)
    initial = jnp.zeros((4 * cos_weight.shape[0], coords.shape[1]), jnp.float32)
    running, _ = lax.scan(one_step, initial, (to_blocks(reciprocal_real_triples, 1, block_cols), to_blocks(cos_weight, 1, block_cols), to_blocks(sin_weight, 1, block_cols)))
    return running

def kspace_weights(reciprocal_real_triples, cell_edge_sizes, atoms_total):
    wavevector = 2.0 * math.pi * reciprocal_real_triples / cell_edge_sizes[:, None]
    squared = lax.optimization_barrier(jnp.sum(wavevector * wavevector, axis=0))
    return 2.0 * math.pi / atoms_total * jnp.exp(-0.5 * gauss_width * gauss_width * squared) / squared

def feature_gradient(features, potential, energy_head_initial_weights, energy_head_final_weights, hidden_electric_projection):
    activation = product(energy_head_initial_weights.T, features)
    sigmoid_part = jax.nn.sigmoid(activation)
    slope_term = energy_head_final_weights[:, None] * sigmoid_part * (1.0 + activation * (1.0 - sigmoid_part))
    return product(energy_head_initial_weights, slope_term) + product(hidden_electric_projection, potential)

def langevin(fractional_placements, particle_speeds, element_kinds, forces, cell_edge_sizes, friction_random_kicks):
    masses = lax.optimization_barrier(jnp.sum(jnp.asarray(masses_table, dtype=jnp.float32)[:, None] * one_hot_rows(element_kinds), axis=0))
    halfway = particle_speeds + 0.5 * time_step * forces / masses
    retain = math.exp(-friction * time_step)
    updated = retain * halfway + jnp.sqrt((1.0 - retain * retain) / masses) * friction_random_kicks
    new_positions = fractional_placements + 0.5 * time_step * (halfway + updated) / cell_edge_sizes[:, None]
    return (new_positions, updated)

def reference(fractional_placements, particle_speeds, element_kinds, adjacent_padded_indices, adjacent_valid_tally, border_particle_rows, reciprocal_integer_triples, cell_edge_sizes, friction_random_kicks, element_feature_vectors, distance_net_initial_weights, distance_net_final_weights, message_blend_matrix, energy_head_initial_weights, energy_head_final_weights, hidden_electric_projection):
    weights = (element_feature_vectors, distance_net_initial_weights, distance_net_final_weights)
    domains = DOM_X * DOM_Y
    slot_count = GHOSTS
    packed = jnp.concatenate([fractional_placements, element_kinds[None, :].astype(jnp.float32)], 0)
    packed_dom = jnp.moveaxis(packed.reshape(4, domains, DOM_ATOMS), 1, 0)
    listing = border_particle_rows.reshape(DOM_X, 2, DOM_Y, 2, slot_count).transpose(0, 2, 1, 3, 4).reshape(domains, 4 * slot_count)
    sending = jax.vmap(lambda domain_block, row_list: domain_block[:, row_list])(packed_dom, listing)
    cell_grid = sending.reshape(DOM_X, DOM_Y, 4, 2, 2, slot_count).transpose(0, 3, 1, 4, 2, 5).reshape(2 * DOM_X, 2 * DOM_Y, 4, slot_count)
    padded = jnp.pad(cell_grid, ((1, 1), (1, 1), (0, 0), (0, 0)), mode='wrap')

    def window(domain_index):
        row_index = domain_index // DOM_Y
        col_index = domain_index % DOM_Y
        zero_start = domain_index * 0
        window_cells = lax.dynamic_slice(padded, (2 * row_index, 2 * col_index, zero_start, zero_start), (4, 4, 4, slot_count))
        return window_cells.transpose(2, 0, 1, 3).reshape(4, 16 * slot_count)
    ghosts = jax.vmap(window)(jnp.arange(domains).astype(jnp.int32))
    extended = jnp.concatenate([packed_dom, ghosts], 2)
    near_lists = adjacent_padded_indices.reshape(domains, DOM_ATOMS, MAXN)
    live_pairs = (jnp.arange(MAXN).astype(jnp.int32)[None, :] < adjacent_valid_tally[:, None]).astype(jnp.float32).reshape(domains, DOM_ATOMS, MAXN)
    centres = packed_dom[:, :3]
    kind_rows = element_kinds.reshape(domains, DOM_ATOMS)

    def forward(block_items):
        surround, near_rows, own_live, centre, own_kinds = block_items
        displace, labels = displacements(surround, near_rows, centre, cell_edge_sizes)
        message = blocked_messages(displace, labels, own_live, weights)
        return product(element_feature_vectors.T, one_hot_rows(own_kinds)) + product(message_blend_matrix.T, message)
    features = lax.map(forward, (extended, near_lists, live_pairs, centres, kind_rows))
    charges = jnp.einsum('cl,dcn->dln', hidden_electric_projection, features, precision=highest)
    charges_all = jnp.moveaxis(charges, 0, 1).reshape(LATENT, ATOMS)
    reciprocal_real_triples = reciprocal_integer_triples.astype(jnp.float32)
    spectrum = structure(fractional_placements, charges_all, reciprocal_real_triples, 256)
    kweight = kspace_weights(reciprocal_real_triples, cell_edge_sizes, ATOMS)
    kspace_out = kspace_terms(fractional_placements, reciprocal_real_triples, kweight * spectrum[0], kweight * spectrum[1], 256)
    potential = kspace_out[:LATENT]
    gradient_terms = kspace_out[LATENT:].reshape(3, LATENT, ATOMS)
    long_range = (2.0 * math.pi / cell_edge_sizes)[:, None] * lax.optimization_barrier(jnp.sum(charges_all[None] * gradient_terms, axis=1))
    potential_dom = jnp.moveaxis(potential.reshape(LATENT, domains, DOM_ATOMS), 1, 0)

    def backward_pass(block_items):
        surround, near_rows, own_live, centre, own_features, own_potential = block_items
        displace, labels = displacements(surround, near_rows, centre, cell_edge_sizes)
        upstream = product(message_blend_matrix, feature_gradient(own_features, own_potential, energy_head_initial_weights, energy_head_final_weights, hidden_electric_projection))
        grad_pairs = blocked_pullback(displace, labels, own_live, upstream, weights)
        direct = -lax.optimization_barrier(jnp.sum(grad_pairs, axis=2))
        scattered = jnp.zeros((3, surround.shape[1]), jnp.float32).at[:, near_rows.reshape(-1)].add(grad_pairs.reshape(3, -1))
        return (direct, scattered)
    direct, scattered = lax.map(backward_pass, (extended, near_lists, live_pairs, centres, features, potential_dom))
    ghost_part = scattered[:, :, DOM_ATOMS:].reshape(DOM_X, DOM_Y, 3, 4, 4, slot_count)
    returned = jnp.zeros((DOM_X, DOM_Y, 2, 2, 3, slot_count), jnp.float32)
    for row_cell in range(4):
        for col_cell in range(4):
            if row_cell in (1, 2) and col_cell in (1, 2):
                continue
            shifted = jnp.roll(ghost_part[:, :, :, row_cell, col_cell], ((row_cell - 1) // 2, (col_cell - 1) // 2), axis=(0, 1))
            returned = returned.at[:, :, (row_cell - 1) % 2, (col_cell - 1) % 2].add(shifted)
    returned = returned.transpose(0, 1, 4, 2, 3, 5).reshape(domains, 3, 4 * slot_count)
    gathered_back = jax.vmap(lambda target, row_list, addend: target.at[:, row_list].add(addend))(scattered[:, :, :DOM_ATOMS], listing, returned)
    short_range = direct + gathered_back
    gradient = jnp.moveaxis(short_range, 0, 1).reshape(3, ATOMS) + long_range
    forces = -gradient
    new_positions, updated = langevin(fractional_placements, particle_speeds, element_kinds, forces, cell_edge_sizes, friction_random_kicks)
    return (forces, new_positions, updated)
```

```python
import math

import jax
import jax.numpy as jnp
from jax import lax
from jax.experimental import pallas as pl
from jax.experimental.pallas import tpu as pltpu
from jax.sharding import PartitionSpec as P

f32 = jnp.float32
bf16 = jnp.bfloat16
i32 = jnp.int32
masses_table = (1.008, 12.011, 15.999, 6.94, 30.974, 18.998)
radial_widths = (2.0, 4.0, 6.0, 8.0, 10.0, 12.0, 14.0, 16.0)
time_step = 0.5
friction = 0.2
gauss_width = 0.3
kinds = 6
slots = 64
hidden = 64
chunk = 8
chunks = slots // chunk
own = 256
ranks = 8
atoms_all = 65536
top = 16
span = 2 * top + 1
plane_own = 69
plane_rows = 72
waves = 2 * plane_rows
tau = 2.0 * math.pi
outer = [(u, v) for u in range(4) for v in range(4) if not (u in (1, 2) and v in (1, 2))]
vmem = pl.BlockSpec(memory_space=pltpu.VMEM)
smem = pl.BlockSpec(memory_space=pltpu.SMEM)
params = pltpu.CompilerParams(vmem_limit_bytes=24 * 1024 * 1024)


def call(kernel, outs, specs, scratch=(), cost=None):
    shapes = [jax.ShapeDtypeStruct(s, d) for s, d in outs]
    return pl.pallas_call(
        kernel,
        out_shape=shapes,
        in_specs=specs,
        out_specs=[vmem] * len(shapes),
        scratch_shapes=list(scratch),
        compiler_params=params,
        cost_estimate=cost,
    )


def dot_n(a, b):
    return lax.dot_general(a, b, (((1,), (0,)), ((), ())), preferred_element_type=f32)


def dot_t(a, b):
    return lax.dot_general(a, b, (((1,), (1,)), ((), ())), preferred_element_type=f32)


def dot_c(a, b):
    return lax.dot_general(
        a, b, (((0,), (0,)), ((), ())), precision=lax.Precision.HIGHEST, preferred_element_type=f32
    )


def split(x):
    high = x.astype(bf16)
    return high, (x - high.astype(f32)).astype(bf16)


def dot3(a, b):
    ah, al = split(a)
    bh, bl = split(b)
    return dot_n(ah, bh) + (dot_n(al, bh) + dot_n(ah, bl))


def lane_pick(row, where):
    return jnp.take_along_axis(
        jnp.broadcast_to(row, where.shape), where, axis=1, mode="promise_in_bounds"
    )


def sine_turns(w):
    square = w * w
    total = jnp.full_like(w, -(tau**11) / math.factorial(11))
    for power in (9, 7, 5, 3, 1):
        sign = -1.0 if power % 4 == 3 else 1.0
        total = total * square + sign * tau**power / math.factorial(power)
    return total * w


def circle(turns):
    t = turns - jnp.floor(turns + 0.5)
    cosine = sine_turns(0.25 - jnp.abs(t))
    folded = jnp.where(t > 0.25, 0.5 - t, jnp.where(t < -0.25, -0.5 - t, t))
    return cosine, sine_turns(folded)


def plane_of(rank, shape, axis):
    index = (lax.broadcasted_iota(i32, shape, axis) + rank * plane_own).astype(f32)
    first = jnp.floor((index + (top + 0.5)) * (1.0 / span))
    return first, index - span * first


def pack_kernel(place, kind, out):
    rows = []
    for c in range(3):
        rows += [place[c : c + 1, 0:128], place[c : c + 1, 128:256]]
    species = kind[...].astype(f32)
    rows += [species[:, 0:128], species[:, 128:256]]
    tile = jnp.concatenate(rows, axis=0)
    for z in range(ranks):
        out[z] = tile


def border_kernel(table, rows, cell0, cell1):
    index = jnp.concatenate([rows[0], rows[1], rows[0], rows[1]], axis=0)
    low, high = index & 127, lax.shift_right_logical(index, 7)
    for c in range(4):
        found = jnp.zeros((8, 128), f32)
        for h in range(16):
            row = table[h // 2, 2 * c + h % 2 : 2 * c + h % 2 + 1, :]
            found = jnp.where(high == h, lane_pick(row, low), found)
        for j in range(2):
            cell0[j * 4 + c : j * 4 + c + 1, :] = found[j : j + 1]
            cell1[j * 4 + c : j * 4 + c + 1, :] = found[2 + j : 3 + j]


def columns_kernel(left, cell0, cell1, right, head, tail):
    for u, ref in enumerate((left, cell0, cell1, right)):
        head[u * 4 : u * 4 + 4, :] = ref[0:4, :]
        tail[u * 4 : u * 4 + 4, :] = ref[4:8, :]


def own_gather_kernel(table, listing, near):
    def step(j, carry):
        at = pl.ds(pl.multiple_of(j * chunk, chunk), chunk)
        for half in range(2):
            lanes = slice(half * 128, half * 128 + 128)
            index = listing[at, lanes]
            low, high = index & 127, lax.shift_right_logical(index, 7)
            found = [jnp.zeros((chunk, 128), f32)] * 4
            for h in range(16):
                hit = high == h
                for c in range(4):
                    r = 2 * c + h % 2
                    row = table[h // 2, r : r + 1, :]
                    found[c] = jnp.where(hit, lane_pick(row, low), found[c])
            for c in range(4):
                near[c, at, lanes] = found[c]
        return carry

    lax.fori_loop(0, chunks, step, 0)


def factor_kernel(rank, table, high, low, waves_x):
    shape = (plane_rows, 128)
    ky, kz = plane_of(rank[0], shape, 0)
    kx = (lax.broadcasted_iota(i32, (top, 128), 0) + 1).astype(f32)

    def step(z, carry):
        for half in range(2):
            at = pl.ds(pl.multiple_of(z * own + half * 128, 128), 128)
            x, y, w = (table[z, 2 * c + half : 2 * c + half + 1, :] for c in range(3))
            cosine, sine = circle(ky * y + kz * w)
            both = jnp.concatenate([cosine, sine], axis=0)
            upper, lower = split(both)
            high[:, at] = upper
            low[:, at] = lower
            cosine, sine = circle(kx * x)
            waves_x[0:top, at] = cosine
            waves_x[top : 2 * top, at] = sine
        return carry

    lax.fori_loop(0, ranks, step, 0)


def count_kernel(triples, out):
    kx, ky, kz = (triples[d : d + 1, :].astype(f32) for d in range(3))
    code = span * ky + kz
    flip = jnp.where(code < 0.0, -1.0, 1.0)
    code = code * flip
    kx = kx * flip
    count = kx.shape[1]
    row = lax.broadcasted_iota(i32, (48, count), 0).astype(f32)
    wanted = jnp.where(row < top, row + 1.0, row - (top - 1.0))
    sign = jnp.where(kx < 0.0, -1.0, 1.0)
    value = jnp.where(row < top, 1.0, sign)
    line = jnp.where(row < 2 * top, jnp.where(jnp.abs(kx) == wanted, value, 0.0), 0.0)
    line = jnp.where((row == 2 * top) & (kx == 0.0), 1.0, line).astype(bf16)
    place = lax.broadcasted_iota(i32, (128, count), 0).astype(f32)
    valid = place < plane_own
    for z in range(ranks):
        hit = jnp.where(valid & (code == place + float(z * plane_own)), 1.0, 0.0).astype(bf16)
        out[z] = dot_t(line, hit)[0:40, :]


def message_kernel(
    edges, listing, near, left, right, head, tail, place, kind, tally, counts, first, second_t,
    embed_t, blend_t, project_t, send, feature_out, disp_out, mark_out, slope_out,
    cells, pooled, active,
):
    for u in range(4):
        for c in range(4):
            cells[c * 16 + u * 4 : c * 16 + u * 4 + 1, :] = head[u * 4 + c : u * 4 + c + 1, :]
            cells[c * 16 + u * 4 + 3 : c * 16 + u * 4 + 4, :] = tail[u * 4 + c : u * 4 + c + 1, :]
    for u, ref in ((0, left), (3, right)):
        for j in range(2):
            for c in range(4):
                spot = c * 16 + u * 4 + 1 + j
                cells[spot : spot + 1, :] = ref[j * 4 + c : j * 4 + c + 1, :]
    pooled[...] = jnp.zeros_like(pooled)

    def step(j, carry):
        at = pl.ds(pl.multiple_of(j * chunk, chunk), chunk)
        halves = []
        for half in range(2):
            lanes = slice(half * 128, half * 128 + 128)
            index = listing[at, lanes]
            low, high = index & 127, lax.shift_right_logical(index, 7)
            found = [near[c, at, lanes] for c in range(4)]
            for u, v in outer:
                hit = high == 16 + u * 4 + v
                for c in range(4):
                    spot = c * 16 + u * 4 + v
                    row = cells[spot : spot + 1, :]
                    found[c] = jnp.where(hit, lane_pick(row, low), found[c])
            halves.append(found)
        found = [jnp.concatenate([halves[0][c], halves[1][c]], axis=1) for c in range(4)]
        squared = jnp.zeros((chunk, own), f32)
        for d in range(3):
            offset = found[d] - place[d : d + 1, :]
            offset = offset - jnp.floor(offset + 0.5)
            offset = offset * edges[d]
            disp_out[d, at, :] = offset
            squared = squared + offset * offset
        slot = lax.broadcasted_iota(i32, (chunk, own), 0) + j * chunk
        mark = jnp.where(slot < tally[...], found[3], -1.0)
        mark_out[at, :] = mark
        basis = jnp.concatenate(
            [jnp.exp(squared * (-1.0 / (w * w))) for w in radial_widths], axis=0
        )
        upper, lower = split(basis)
        pre = dot_n(first[...], jnp.concatenate([upper, lower, upper], axis=0))
        gate = 0.5 * jnp.tanh(0.5 * pre) + 0.5
        out = pre * gate
        active[...] = out
        slope_out[j] = gate + out * (1.0 - gate)
        for s in range(kinds):
            total = pooled[s * hidden : (s + 1) * hidden, :]
            for m in range(chunk):
                hit = jnp.broadcast_to(mark[m : m + 1, :], (hidden, own)) == float(s)
                total = total + jnp.where(hit, active[m * hidden : (m + 1) * hidden, :], 0.0)
            pooled[s * hidden : (s + 1) * hidden, :] = total
        return carry

    lax.fori_loop(0, chunks, step, 0)
    message = jnp.zeros((128, own), f32)
    features = jnp.zeros((128, own), f32)
    for s in range(kinds):
        message = message + embed_t[:, s : s + 1] * dot3(
            second_t[...], pooled[s * hidden : (s + 1) * hidden, :]
        )
        features = features + embed_t[:, s : s + 1] * jnp.where(kind[...] == s, 1.0, 0.0)
    features = features + dot3(blend_t[...], message * (1.0 / slots))
    feature_out[...] = features
    charges = dot3(project_t[...], features)
    for z in range(ranks):
        send[z, 0:8, :] = charges[:, 0:128]
        send[z, 8:16, :] = charges[:, 128:256]
        send[z, 16:56, :] = counts[z]


def structure_kernel(core, got, waves_x, high, low, mine, other, total, extra, left_high, left_low):
    total[...] = jnp.zeros_like(total)
    extra[...] = jnp.zeros_like(extra)

    def step(z, carry):
        at = pl.ds(pl.multiple_of(z * own, own), own)
        charge = jnp.concatenate([got[z, 0:8, :], got[z, 8:16, :]], axis=1)
        for f in range(0, 2 * top, 2):
            pair = jnp.concatenate(
                [charge * waves_x[f : f + 1, at], charge * waves_x[f + 1 : f + 2, at]], axis=0
            )
            upper, lower = split(pair)
            left_high[f * 8 : f * 8 + 16, :] = upper
            left_low[f * 8 : f * 8 + 16, :] = lower
        plane_high, plane_low = high[:, at], low[:, at]
        total[...] += dot_t(plane_high, left_high[...]) + (
            dot_t(plane_low, left_high[...]) + dot_t(plane_high, left_low[...])
        )
        upper, lower = split(charge)
        extra[:, 0:waves] += dot_t(upper, plane_high) + (
            dot_t(lower, plane_high) + dot_t(upper, plane_low)
        )
        return carry

    lax.fori_loop(0, ranks, step, 0)
    first = core[0] == 0
    real, imaginary = total[0:plane_rows, :], total[plane_rows:waves, :]
    begin, rest = extra[:, 0:128], extra[:, 128:256]
    for ref, one in ((mine, first), (other, jnp.logical_not(first))):
        ref[0:plane_rows, :] = jnp.where(one, real, imaginary)
        ref[plane_rows : plane_rows + 8, 0:128] = jnp.where(one, begin, rest)
        ref[plane_rows : plane_rows + 8, 128:256] = jnp.zeros((8, 128), f32)


def potential_kernel(
    rank, core, edges, mine, other, got, waves_x, high, low, potential, gradient,
    table, table_high, table_low, result,
):
    first = core[0] == 0
    real = jnp.where(first, mine[0:plane_rows, :], other[0:plane_rows, :])
    imaginary = jnp.where(first, other[0:plane_rows, :], mine[0:plane_rows, :])
    tail = slice(plane_rows, plane_rows + 8)
    begin = jnp.where(first, mine[tail, 0:128], other[tail, 0:128])
    rest = jnp.where(first, other[tail, 0:128], mine[tail, 0:128])
    counts = got[0, 16:56, :]
    for z in range(1, ranks):
        counts = counts + got[z, 16:56, :]
    lane = lax.broadcasted_iota(i32, (top, 128), 1)
    spread = jnp.where(
        lax.shift_right_logical(lane, 3) == lax.broadcasted_iota(i32, (top, 128), 0), 1.0, 0.0
    )
    lane = lax.broadcasted_iota(i32, (8, 128), 1)
    line = lax.broadcasted_iota(i32, (8, 128), 0)
    flat = jnp.where(line == 0, 1.0, 0.0)
    repeat = jnp.where((lane & 7) == line, 1.0, 0.0)
    both = dot_c(counts[0:top], spread)[0:plane_rows]
    apart = dot_c(counts[top : 2 * top], spread)[0:plane_rows]
    zero = dot_c(counts[2 * top : 2 * top + 8], flat)[0:plane_rows]
    lone = dot_c(jnp.concatenate([begin, rest], axis=1), repeat)
    shape = (plane_rows, 128)
    ky, kz = plane_of(rank[0], shape, 0)
    lanes = lax.broadcasted_iota(i32, shape, 1)
    kx = (lax.shift_right_logical(lanes, 3) + 1).astype(f32)
    qx, qy, qz = tau * kx / edges[0], tau * ky / edges[1], tau * kz / edges[2]
    flat_square = qy * qy + qz * qz
    square = qx * qx + flat_square

    def weigh(q):
        return (tau / atoms_all) * jnp.exp((-0.5 * gauss_width * gauss_width) * q) / q

    weight = weigh(square)
    both, apart = both * weight, apart * weight
    zero = zero * jnp.where(flat_square > 0.0, weigh(jnp.maximum(flat_square, 1e-6)), 0.0)
    real_c, real_s = real[:, 0:128], real[:, 128:256]
    imag_c, imag_s = imaginary[:, 0:128], imaginary[:, 128:256]
    pair_c = (both * real_c - apart * imag_s, both * imag_c + apart * real_s)
    pair_s = (both * real_s + apart * imag_c, both * imag_s - apart * real_c)
    ty, tz = tau * ky, tau * kz
    upper, lower = slice(0, plane_rows), slice(plane_rows, waves)
    for part, (re, im) in enumerate((pair_c, pair_s)):
        for form, scale in enumerate((None, ty, tz)):
            at = slice(form * 256 + part * 128, form * 256 + part * 128 + 128)
            table[upper, at] = re if scale is None else scale * im
            table[lower, at] = im if scale is None else -(scale * re)
    re, im = zero * lone[0:plane_rows], zero * lone[plane_rows:waves]
    group = lax.shift_right_logical(lanes, 3)
    turn = jnp.where(group == 1, ty, tz)
    at = slice(768, 896)
    table[upper, at] = jnp.where(group == 0, re, turn * im)
    table[lower, at] = jnp.where(group == 0, im, -(turn * re))
    for block in range(7):
        at = slice(block * 128, block * 128 + 128)
        turned = jnp.transpose(table[:, at])
        table_high[at, 0:waves], table_low[at, 0:waves] = split(turned)

    def step(z, carry):
        at = pl.ds(pl.multiple_of(z * own, own), own)
        plane_high, plane_low = high[:, at], low[:, at]
        weights = table_high[0:800, 0:waves]
        result[...] = dot_n(weights, plane_high) + (
            dot_n(table_low[0:800, 0:waves], plane_high) + dot_n(weights, plane_low)
        )
        total = [result[768:776, :], jnp.zeros((8, own), f32), result[776:784, :], result[784:792, :]]
        for f in range(2 * top):
            wave = waves_x[f : f + 1, at]
            for form, slot in enumerate((0, 2, 3)):
                lines = slice(form * 256 + f * 8, form * 256 + f * 8 + 8)
                total[slot] = total[slot] + wave * result[lines, :]
        for k in range(top):
            cosine, sine = waves_x[k : k + 1, at], waves_x[top + k : top + k + 1, at]
            turn = tau * (k + 1)
            total[1] = total[1] + (turn * cosine) * result[(top + k) * 8 : (top + k) * 8 + 8, :]
            total[1] = total[1] - (turn * sine) * result[k * 8 : k * 8 + 8, :]
        potential[z] = total[0]
        charge = jnp.concatenate([got[z, 0:8, :], got[z, 8:16, :]], axis=1)
        for d in range(3):
            line = jnp.sum(charge * total[1 + d], axis=0, keepdims=True) / edges[d]
            gradient[z, 2 * d : 2 * d + 1, :] = line[:, 0:128]
            gradient[z, 2 * d + 1 : 2 * d + 2, :] = line[:, 128:256]
        return carry

    lax.fori_loop(0, ranks, step, 0)


def pair_kernel(
    got, features, disp, marks, slope, listing, lines, first_high, first_low, second, embed_t,
    blend, energy, energy_t, energy_final, project, cells0, cells3, mid0, mid3, domain, direct,
    upstream, upper, lower, left, right, total, pulled,
):
    potential = got[0]
    for z in range(1, ranks):
        potential = potential + got[z]
    activation = dot3(energy_t[...], features[...])
    gate = 0.5 * jnp.tanh(0.5 * activation) + 0.5
    ramp = energy_final[...] * gate * (1.0 + activation * (1.0 - gate))
    change = dot3(energy[...], ramp) + dot3(project[...], potential)
    change = dot3(blend[...], change) * (1.0 / slots)
    for s in range(kinds):
        upstream[s] = dot3(second[...], embed_t[:, s : s + 1] * change)
    total[...] = jnp.zeros_like(total)
    pulled[...] = jnp.zeros_like(pulled)
    row_high = lax.broadcasted_iota(i32, (32, own), 0)
    row_low = lax.broadcasted_iota(i32, (128, own), 0)

    def step(j, carry):
        at = pl.ds(pl.multiple_of(j * chunk, chunk), chunk)
        offsets = [disp[d, at, :] for d in range(3)]
        mark = marks[at, :]
        for m in range(chunk):
            mine = jnp.broadcast_to(mark[m : m + 1, :], (hidden, own))
            chosen = jnp.zeros((hidden, own), f32)
            for s in range(kinds):
                chosen = jnp.where(mine == float(s), upstream[s], chosen)
            chosen = chosen * slope[j, m * hidden : (m + 1) * hidden, :]
            upper[m * hidden : (m + 1) * hidden, :], lower[m * hidden : (m + 1) * hidden, :] = (
                split(chosen)
            )
        back = dot_n(first_high[...], upper[...]) + (
            dot_n(first_low[...], upper[...]) + dot_n(first_high[...], lower[...])
        )
        squared = offsets[0] * offsets[0] + offsets[1] * offsets[1] + offsets[2] * offsets[2]
        radial = jnp.zeros((chunk, own), f32)
        for n, w in enumerate(radial_widths):
            lean = jnp.exp(squared * (-1.0 / (w * w))) * (-2.0 / (w * w))
            radial = radial + lean * back[n * chunk : (n + 1) * chunk, :]
        pulls = [radial * offset for offset in offsets]
        index = listing[at, :]
        low, high = index & 127, lax.shift_right_logical(index, 7)
        pieces = []
        for d in range(3):
            pulled[d] += pulls[d]
            main = pulls[d].astype(bf16).astype(f32)
            pieces.append((main, pulls[d] - main))
        for m in range(chunk):
            lanes = slice(m * own, (m + 1) * own)
            hit = jnp.broadcast_to(high[m : m + 1, :], (32, own)) == row_high
            for part in range(2):
                for d in range(3):
                    row = part * 96 + d * 32
                    left[row : row + 32, lanes] = jnp.where(
                        hit, pieces[d][part][m : m + 1, :], 0.0
                    ).astype(bf16)
            spot = jnp.broadcast_to(low[m : m + 1, :], (128, own)) == row_low
            right[:, lanes] = jnp.where(spot, 1.0, 0.0).astype(bf16)
        total[...] += dot_t(left[...], right[...])
        return carry

    lax.fori_loop(0, chunks, step, 0)
    scattered = total[0:96, :] + total[96:192, :]
    nothing = jnp.zeros((1, 128), f32)
    for u in range(4):
        for c in range(4):
            for ref, v in ((cells0, 0), (cells3, 3)):
                spot = c * 32 + 16 + u * 4 + v
                value = scattered[spot : spot + 1, :] if c < 3 else nothing
                ref[u * 4 + c : u * 4 + c + 1, :] = value
    for ref, u in ((mid0, 0), (mid3, 3)):
        for j in range(2):
            for c in range(4):
                spot = c * 32 + 16 + u * 4 + 1 + j
                value = scattered[spot : spot + 1, :] if c < 3 else nothing
                ref[j * 4 + c : j * 4 + c + 1, :] = value
    for z in range(ranks):
        for d in range(3):
            for half in range(2):
                spot, r = d * 32 + z * 2 + half, 2 * d + half
                domain[z, r : r + 1, :] = scattered[spot : spot + 1, :] + lines[z, r : r + 1, :]
        domain[z, 6:8, :] = jnp.zeros((2, 128), f32)
    for d in range(3):
        line = -jnp.sum(pulled[d], axis=0, keepdims=True)
        direct[2 * d : 2 * d + 1, :] = line[:, 0:128]
        direct[2 * d + 1 : 2 * d + 2, :] = line[:, 128:256]
    direct[6:8, :] = jnp.zeros((2, 128), f32)


def echo_kernel(above, below, mid0, mid3, send0, send3, inner0, inner1):
    for u, ref in ((0, send0), (1, inner0), (2, inner1), (3, send3)):
        both = jnp.concatenate([below[u * 4 : u * 4 + 4, :], above[u * 4 : u * 4 + 4, :]], axis=0)
        if u == 0:
            both = both + mid0[...]
        if u == 3:
            both = both + mid3[...]
        ref[...] = both


def border_back_kernel(inner0, inner1, from_left, from_right, rows, domain, out):
    cells = (inner0[...] + from_left[...], inner1[...] + from_right[...])
    row_high = lax.broadcasted_iota(i32, (16, 128), 0)
    row_low = lax.broadcasted_iota(i32, (128, 128), 0)
    total = jnp.zeros((96, 128), f32)
    for i in range(2):
        index = rows[i]
        low, high = index & 127, lax.shift_right_logical(index, 7)
        for j in range(2):
            hit = jnp.broadcast_to(high[j : j + 1, :], (16, 128)) == row_high
            spot = jnp.broadcast_to(low[j : j + 1, :], (128, 128)) == row_low
            left = []
            for part in range(2):
                for c in range(3):
                    value = cells[i][j * 4 + c : j * 4 + c + 1, :]
                    main = value.astype(bf16).astype(f32)
                    left.append(jnp.where(hit, main if part == 0 else value - main, 0.0))
            total = total + dot_t(
                jnp.concatenate(left, axis=0).astype(bf16),
                jnp.where(spot, 1.0, 0.0).astype(bf16),
            )
    total = total[0:48, :] + total[48:96, :]
    for z in range(ranks):
        lines = [total[d * 16 + z * 2 : d * 16 + z * 2 + 2, :] for d in range(3)]
        lines.append(jnp.zeros((2, 128), f32))
        out[z] = domain[z] + jnp.concatenate(lines, axis=0)


def step_kernel(edges, got, direct, place, speed, kind, kicks, force_out, place_out, speed_out):
    gradient = direct[...]
    for z in range(ranks):
        gradient = gradient + got[z]
    species = kind[...]
    mass = jnp.zeros((1, own), f32)
    for s in range(kinds):
        mass = jnp.where(species == s, masses_table[s], mass)
    retain = math.exp(-friction * time_step)
    spread = jnp.sqrt((1.0 - retain * retain) / mass)
    for d in range(3):
        row = slice(d, d + 1)
        force = -jnp.concatenate(
            [gradient[2 * d : 2 * d + 1, :], gradient[2 * d + 1 : 2 * d + 2, :]], axis=1
        )
        halfway = speed[row, :] + 0.5 * time_step * force / mass
        updated = retain * halfway + spread * kicks[row, :]
        force_out[row, :] = force
        speed_out[row, :] = updated
        place_out[row, :] = place[row, :] + 0.5 * time_step * (halfway + updated) / edges[d]


def shift(axis, by):
    count = lax.axis_size(axis)
    return [(i, (i + by) % count) for i in range(count)]


def partners():
    maps = (
        lambda x, yl, yh, c: (x, yl, yh, 1 - c),
        lambda x, yl, yh, c: (x, 1 - yl, yh, c),
        lambda x, yl, yh, c: (x, 1 - yl, 1 - yh, c),
        lambda x, yl, yh, c: (x ^ 1, yl, yh, c),
        lambda x, yl, yh, c: (3 - x, yl, yh, c),
    )
    places = [(x, a, b, c) for x in range(4) for a in range(2) for b in range(2) for c in range(2)]
    number = {p: (p[0] * 2 + p[1]) * 4 + p[2] * 2 + p[3] for p in places}
    return [[(number[p], number[m(*p)]) for p in places] for m in maps]


def body(
    fractional_placements,
    particle_speeds,
    element_kinds,
    adjacent_padded_indices,
    adjacent_valid_tally,
    border_particle_rows,
    reciprocal_integer_triples,
    cell_edge_sizes,
    friction_random_kicks,
    element_feature_vectors,
    distance_net_initial_weights,
    distance_net_final_weights,
    message_blend_matrix,
    energy_head_initial_weights,
    energy_head_final_weights,
    hidden_electric_projection,
):
    rank = lax.axis_index("ka").astype(i32).reshape(1)
    core = (lax.axis_index("gy") % 2).astype(i32).reshape(1)
    kind = element_kinds.reshape(1, own)
    tally = adjacent_valid_tally.reshape(1, own)
    listing = adjacent_padded_indices.T
    blocks = jnp.einsum(
        "nh,ml->mhnl", distance_net_initial_weights, jnp.eye(chunk, dtype=f32), precision="highest"
    ).reshape(chunk * hidden, 8 * chunk)
    blocks_high, blocks_low = split(blocks)
    first = jnp.concatenate([blocks_high, blocks_high, blocks_low], axis=1)
    embed_t = element_feature_vectors.T

    packed = call(pack_kernel, [((ranks, 8, 128), f32)], [vmem] * 2)(fractional_placements, kind)[0]
    table = lax.all_to_all(packed, "ka", 0, 0)
    cell0, cell1 = call(border_kernel, [((8, 128), f32)] * 2, [vmem] * 2)(
        table, border_particle_rows
    )
    left = lax.ppermute(cell1, "gx", shift("gx", 1))
    right = lax.ppermute(cell0, "gx", shift("gx", -1))
    head, tail = call(columns_kernel, [((16, 128), f32)] * 2, [vmem] * 4)(left, cell0, cell1, right)
    tail_in = lax.ppermute(tail, "gy", shift("gy", 1))
    head_in = lax.ppermute(head, "gy", shift("gy", -1))

    near = call(
        own_gather_kernel,
        [((4, slots, own), f32)],
        [vmem] * 2,
        cost=pl.CostEstimate(flops=20_000_000, bytes_accessed=400_000, transcendentals=0),
    )(table, listing)[0]
    high, low, waves_x = call(
        factor_kernel,
        [((waves, ranks * own), bf16), ((waves, ranks * own), bf16), ((2 * top, ranks * own), f32)],
        [smem, vmem],
        cost=pl.CostEstimate(flops=10_000_000, bytes_accessed=1_500_000, transcendentals=0),
    )(rank, table)
    counts = call(
        count_kernel,
        [((ranks, 40, 128), f32)],
        [vmem],
        cost=pl.CostEstimate(flops=10_000_000, bytes_accessed=200_000, transcendentals=0),
    )(reciprocal_integer_triples)[0]

    send, features, disp, marks, slope = call(
        message_kernel,
        [
            ((ranks, 56, 128), f32),
            ((128, own), f32),
            ((3, slots, own), f32),
            ((slots, own), f32),
            ((chunks, chunk * hidden, own), f32),
        ],
        [smem] + [vmem] * 15,
        [
            pltpu.VMEM((64, 128), f32),
            pltpu.VMEM((kinds * hidden, own), f32),
            pltpu.VMEM((chunk * hidden, own), f32),
        ],
    )(
        cell_edge_sizes, listing, near, left, right, tail_in, head_in, fractional_placements, kind,
        tally, counts, first, distance_net_final_weights.T, embed_t, message_blend_matrix.T,
        hidden_electric_projection.T,
    )
    got = lax.all_to_all(send, "ka", 0, 0)

    mine, other = call(
        structure_kernel,
        [((plane_rows + 8, own), f32)] * 2,
        [smem] + [vmem] * 4,
        [
            pltpu.VMEM((waves, own), f32),
            pltpu.VMEM((8, own), f32),
            pltpu.VMEM((own, own), bf16),
            pltpu.VMEM((own, own), bf16),
        ],
    )(core, got, waves_x, high, low)
    swaps = partners()
    both = ("gx", "gy")
    summed = mine + lax.ppermute(other, both, swaps[0])
    for swap in swaps[1:]:
        summed = summed + lax.ppermute(summed, both, swap)
    opposite = lax.ppermute(summed, both, swaps[0])

    potential, lines = call(
        potential_kernel,
        [((ranks, 8, own), f32), ((ranks, 8, 128), f32)],
        [smem] * 3 + [vmem] * 6,
        [
            pltpu.VMEM((waves, 896), f32),
            pltpu.VMEM((896, own), bf16),
            pltpu.VMEM((896, own), bf16),
            pltpu.VMEM((800, own), f32),
        ],
    )(rank, core, cell_edge_sizes, summed, opposite, got, waves_x, high, low)
    shares = lax.all_to_all(potential, "ka", 0, 0)

    cells0, cells3, mid0, mid3, domain, direct = call(
        pair_kernel,
        [
            ((16, 128), f32),
            ((16, 128), f32),
            ((8, 128), f32),
            ((8, 128), f32),
            ((ranks, 8, 128), f32),
            ((8, 128), f32),
        ],
        [vmem] * 16,
        [
            pltpu.VMEM((kinds, hidden, own), f32),
            pltpu.VMEM((chunk * hidden, own), bf16),
            pltpu.VMEM((chunk * hidden, own), bf16),
            pltpu.VMEM((192, chunk * own), bf16),
            pltpu.VMEM((128, chunk * own), bf16),
            pltpu.VMEM((192, 128), f32),
            pltpu.VMEM((3, chunk, own), f32),
        ],
    )(
        shares, features, disp, marks, slope, listing, lines, blocks_high.T, blocks_low.T,
        distance_net_final_weights, embed_t, message_blend_matrix, energy_head_initial_weights,
        energy_head_initial_weights.T, energy_head_final_weights.reshape(-1, 1),
        hidden_electric_projection,
    )
    above = lax.ppermute(cells0, "gy", shift("gy", -1))
    below = lax.ppermute(cells3, "gy", shift("gy", 1))
    send0, send3, inner0, inner1 = call(echo_kernel, [((8, 128), f32)] * 4, [vmem] * 4)(
        above, below, mid0, mid3
    )
    from_right = lax.ppermute(send0, "gx", shift("gx", -1))
    from_left = lax.ppermute(send3, "gx", shift("gx", 1))
    reaction = call(border_back_kernel, [((ranks, 8, 128), f32)], [vmem] * 6)(
        inner0, inner1, from_left, from_right, border_particle_rows, domain
    )[0]
    returned = lax.all_to_all(reaction, "ka", 0, 0)
    forces, places, speeds = call(
        step_kernel, [((3, own), f32)] * 3, [smem] + [vmem] * 6
    )(
        cell_edge_sizes, returned, direct, fractional_placements, particle_speeds, kind,
        friction_random_kicks,
    )
    return (forces, places, speeds)


def solution(mesh):
    atoms = ("gx", "gy", "ka")
    return jax.shard_map(
        body,
        mesh=mesh,
        in_specs=(
            P(None, atoms),
            P(None, atoms),
            P(atoms),
            P(atoms, None),
            P(atoms),
            P("gx", "gy", None),
            P(None, "ka"),
            P(),
            P(None, atoms),
            P(),
            P(),
            P(),
            P(),
            P(),
            P(),
            P(),
        ),
        out_specs=(P(None, atoms), P(None, atoms), P(None, atoms)),
        check_vma=False,
    )
```

```python
import math

import jax
import jax.numpy as jnp
from jax import lax
from jax.experimental import pallas as pl
from jax.experimental.pallas import tpu as pltpu
from jax.sharding import PartitionSpec as P

f32 = jnp.float32
bf16 = jnp.bfloat16
i32 = jnp.int32
masses_table = (1.008, 12.011, 15.999, 6.94, 30.974, 18.998)
radial_widths = (2.0, 4.0, 6.0, 8.0, 10.0, 12.0, 14.0, 16.0)
time_step = 0.5
friction = 0.2
gauss_width = 0.3
kinds = 6
slots = 64
hidden = 64
chunk = 8
chunks = slots // chunk
own = 256
ranks = 8
atoms_all = 65536
top = 16
span = 2 * top + 1
plane_own = 69
plane_rows = 72
waves = 2 * plane_rows
tau = 2.0 * math.pi
outer = [(u, v) for u in range(4) for v in range(4) if not (u in (1, 2) and v in (1, 2))]
vmem = pl.BlockSpec(memory_space=pltpu.VMEM)
smem = pl.BlockSpec(memory_space=pltpu.SMEM)
far = pl.BlockSpec(memory_space=pltpu.HBM)
anywhere = pl.BlockSpec(memory_space=pl.ANY)
params = pltpu.CompilerParams(vmem_limit_bytes=24 * 1024 * 1024)


def work(micros):
    return pl.CostEstimate(
        flops=int(micros * 5e8), bytes_accessed=int(micros * 2e6), transcendentals=0
    )


def call(kernel, outs, specs, scratch=(), cost=None):
    shapes = [jax.ShapeDtypeStruct(s, d) for s, d in outs]
    return pl.pallas_call(
        kernel,
        out_shape=shapes,
        in_specs=specs,
        out_specs=[vmem] * len(shapes),
        scratch_shapes=list(scratch),
        compiler_params=params,
        cost_estimate=cost,
    )


def dot_n(a, b):
    return lax.dot_general(a, b, (((1,), (0,)), ((), ())), preferred_element_type=f32)


def dot_t(a, b):
    return lax.dot_general(a, b, (((1,), (1,)), ((), ())), preferred_element_type=f32)


def dot_c(a, b):
    return lax.dot_general(
        a, b, (((0,), (0,)), ((), ())), precision=lax.Precision.HIGHEST, preferred_element_type=f32
    )


def dot_h(a, b):
    return lax.dot_general(
        a, b, (((1,), (1,)), ((), ())), precision=lax.Precision.HIGHEST, preferred_element_type=f32
    )


def split(x):
    high = x.astype(bf16)
    return high, (x - high.astype(f32)).astype(bf16)


def dot3(a, b):
    ah, al = split(a)
    bh, bl = split(b)
    return dot_n(ah, bh) + (dot_n(al, bh) + dot_n(ah, bl))


def lane_pick(row, where):
    return jnp.take_along_axis(
        jnp.broadcast_to(row, where.shape), where, axis=1, mode="promise_in_bounds"
    )


def sine_turns(w):
    square = w * w
    total = jnp.full_like(w, -(tau**11) / math.factorial(11))
    for power in (9, 7, 5, 3, 1):
        sign = -1.0 if power % 4 == 3 else 1.0
        total = total * square + sign * tau**power / math.factorial(power)
    return total * w


def circle(turns):
    t = turns - jnp.floor(turns + 0.5)
    cosine = sine_turns(0.25 - jnp.abs(t))
    folded = jnp.where(t > 0.25, 0.5 - t, jnp.where(t < -0.25, -0.5 - t, t))
    return cosine, sine_turns(folded)


def plane_of(rank, shape, axis):
    index = (lax.broadcasted_iota(i32, shape, axis) + rank * plane_own).astype(f32)
    first = jnp.floor((index + (top + 0.5)) * (1.0 / span))
    return first, index - span * first


def pack_kernel(place_far, kind_far, out, place, kind, done):
    copies = [
        pltpu.make_async_copy(place_far, place, done.at[0]),
        pltpu.make_async_copy(kind_far, kind, done.at[1]),
    ]
    for copy in copies:
        copy.start()
    for copy in copies:
        copy.wait()
    rows = []
    for c in range(3):
        rows += [place[c : c + 1, 0:128], place[c : c + 1, 128:256]]
    species = kind[...].astype(f32)
    rows += [species[:, 0:128], species[:, 128:256]]
    tile = jnp.concatenate(rows, axis=0)
    for z in range(ranks):
        out[z] = tile


def count_triples(triples, out):
    kx, ky, kz = (triples[d : d + 1, :].astype(f32) for d in range(3))
    code = span * ky + kz
    flip = jnp.where(code < 0.0, -1.0, 1.0)
    code = code * flip
    kx = kx * flip
    count = kx.shape[1]
    row = lax.broadcasted_iota(i32, (48, count), 0).astype(f32)
    wanted = jnp.where(row < top, row + 1.0, row - (top - 1.0))
    sign = jnp.where(kx < 0.0, -1.0, 1.0)
    value = jnp.where(row < top, 1.0, sign)
    line = jnp.where(row < 2 * top, jnp.where(jnp.abs(kx) == wanted, value, 0.0), 0.0)
    line = jnp.where((row == 2 * top) & (kx == 0.0), 1.0, line).astype(bf16)
    place = lax.broadcasted_iota(i32, (128, count), 0).astype(f32)
    valid = place < plane_own
    for z in range(ranks):
        hit = jnp.where(valid & (code == place + float(z * plane_own)), 1.0, 0.0).astype(bf16)
        out[z] = dot_t(line, hit)[0:40, :]


def prepare_kernel(
    edges_far, listing_far, tally_far, rows_far, triples_far, initial_far, second_far, embed_far,
    blend_far, energy_far, project_far, final_far,
    edges_out, listing, tally, rows, counts, first, mixed_high, mixed_low, ball, base, final_out,
    triples, initial, second, embed, blend, heads, final, edges, wide, done,
):
    embed[...] = jnp.zeros_like(embed)
    far = (
        (edges_far, edges), (listing_far, listing), (tally_far, tally), (rows_far, rows),
        (triples_far, triples), (initial_far, initial), (second_far, second),
        (embed_far, embed.at[0:kinds]), (blend_far, blend), (energy_far, heads.at[8:24]),
        (project_far, heads.at[0:8]), (final_far, final),
    )
    copies = [pltpu.make_async_copy(a, b, done.at[n]) for n, (a, b) in enumerate(far)]
    for copy in copies:
        copy.start()
    for copy in copies:
        copy.wait()
    for d in range(3):
        edges_out[d : d + 1, :] = jnp.full((1, own), 1.0, f32) * edges[d]
    edges_out[3:8, :] = jnp.zeros((5, own), f32)
    lane = lax.broadcasted_iota(i32, (8, 64), 1)
    pick = jnp.where(lax.shift_right_logical(lane, 3) == lax.broadcasted_iota(i32, (8, 64), 0), 1.0, 0.0)
    repeated = dot_c(initial[...], pick)
    lane = lax.broadcasted_iota(i32, (hidden, 64), 1) & 7
    blocks = jnp.concatenate(
        [jnp.where(lane == m, repeated, 0.0) for m in range(chunk)], axis=0
    )
    high, low = split(blocks)
    first[:, 0:64], first[:, 64:128], first[:, 128:192] = high, high, low
    through = dot_h(heads[...], blend[...])
    base[...] = dot_h(heads[...], embed[...])
    doubled = jnp.concatenate([second[...], second[...]], axis=0)
    left = lax.broadcasted_iota(i32, (24, 128), 1) < hidden
    slot = lax.broadcasted_iota(i32, (8, 128), 0)
    group = lax.shift_right_logical(lax.broadcasted_iota(i32, (8, 128), 1), 6)
    responses = []
    for s in range(kinds):
        response = dot_h(through * embed[s : s + 1, :], doubled) * (1.0 / slots)
        responses.append(response)
        for l in range(8):
            line = jnp.broadcast_to(response[l : l + 1, :], (8, 128))
            for t in range(4):
                at = (l * kinds + s) * 8
                wide[at : at + 8, t * 128 : (t + 1) * 128] = jnp.where(
                    group + 2 * t == slot, line, 0.0
                )
    for t in range(kinds // 2):
        ball[:, t * 128 : (t + 1) * 128] = jnp.where(left, responses[2 * t], responses[2 * t + 1])
    mixed_high[...], mixed_low[...] = split(wide[...])
    square = (16, 16)
    same = lax.broadcasted_iota(i32, square, 0) == lax.broadcasted_iota(i32, square, 1)
    final_out[...] = jnp.sum(
        jnp.where(same, jnp.broadcast_to(final[...], square), 0.0), axis=1, keepdims=True
    )
    count_triples(triples, counts)


def border_kernel(table, rows, cell0, cell1):
    index = jnp.concatenate([rows[0], rows[1], rows[0], rows[1]], axis=0)
    low, high = index & 127, lax.shift_right_logical(index, 7)
    for c in range(4):
        found = jnp.zeros((8, 128), f32)
        for h in range(16):
            row = table[h // 2, 2 * c + h % 2 : 2 * c + h % 2 + 1, :]
            found = jnp.where(high == h, lane_pick(row, low), found)
        for j in range(2):
            cell0[j * 4 + c : j * 4 + c + 1, :] = found[j : j + 1]
            cell1[j * 4 + c : j * 4 + c + 1, :] = found[2 + j : 3 + j]


def columns_kernel(left, cell0, cell1, right, after, head, tail):
    for u, ref in enumerate((left, cell0, cell1, right)):
        head[u * 4 : u * 4 + 4, :] = ref[0:4, :]
        tail[u * 4 : u * 4 + 4, :] = ref[4:8, :]


def own_gather_kernel(table, listing, near):
    def step(j, carry):
        at = pl.ds(pl.multiple_of(j * chunk, chunk), chunk)
        for half in range(2):
            lanes = slice(half * 128, half * 128 + 128)
            index = listing[at, lanes]
            low, high = index & 127, lax.shift_right_logical(index, 7)
            found = [jnp.zeros((chunk, 128), f32)] * 4
            for h in range(16):
                hit = high == h
                for c in range(4):
                    r = 2 * c + h % 2
                    row = table[h // 2, r : r + 1, :]
                    found[c] = jnp.where(hit, lane_pick(row, low), found[c])
            for c in range(4):
                near[c, at, lanes] = found[c]
        return carry

    lax.fori_loop(0, chunks, step, 0)


def factor_kernel(rank, table, high, low, waves_x):
    shape = (plane_rows, 128)
    ky, kz = plane_of(rank[0], shape, 0)
    kx = (lax.broadcasted_iota(i32, (top, 128), 0) + 1).astype(f32)

    def step(z, carry):
        for half in range(2):
            at = pl.ds(pl.multiple_of(z * own + half * 128, 128), 128)
            x, y, w = (table[z, 2 * c + half : 2 * c + half + 1, :] for c in range(3))
            cosine, sine = circle(ky * y + kz * w)
            both = jnp.concatenate([cosine, sine], axis=0)
            upper, lower = split(both)
            high[:, at] = upper
            low[:, at] = lower
            cosine, sine = circle(kx * x)
            waves_x[0:top, at] = cosine
            waves_x[top : 2 * top, at] = sine
        return carry

    lax.fori_loop(0, ranks, step, 0)


def message_kernel(
    edges, listing, near, left, right, head, tail, place, kind, tally, counts, first, ball, base,
    after, send, activation, disp_out, mark_out,
    cells, pooled, active,
):
    for u in range(4):
        for c in range(4):
            cells[c * 16 + u * 4 : c * 16 + u * 4 + 1, :] = head[u * 4 + c : u * 4 + c + 1, :]
            cells[c * 16 + u * 4 + 3 : c * 16 + u * 4 + 4, :] = tail[u * 4 + c : u * 4 + c + 1, :]
    for u, ref in ((0, left), (3, right)):
        for j in range(2):
            for c in range(4):
                spot = c * 16 + u * 4 + 1 + j
                cells[spot : spot + 1, :] = ref[j * 4 + c : j * 4 + c + 1, :]
    pooled[...] = jnp.zeros_like(pooled)

    def step(j, carry):
        at = pl.ds(pl.multiple_of(j * chunk, chunk), chunk)
        halves = []
        for half in range(2):
            lanes = slice(half * 128, half * 128 + 128)
            index = listing[at, lanes]
            low, high = index & 127, lax.shift_right_logical(index, 7)
            found = [near[c, at, lanes] for c in range(4)]
            for u, v in outer:
                hit = high == 16 + u * 4 + v
                for c in range(4):
                    spot = c * 16 + u * 4 + v
                    row = cells[spot : spot + 1, :]
                    found[c] = jnp.where(hit, lane_pick(row, low), found[c])
            halves.append(found)
        found = [jnp.concatenate([halves[0][c], halves[1][c]], axis=1) for c in range(4)]
        squared = jnp.zeros((chunk, own), f32)
        for d in range(3):
            offset = found[d] - place[d : d + 1, :]
            offset = offset - jnp.floor(offset + 0.5)
            offset = offset * edges[d : d + 1, :]
            disp_out[d, at, :] = offset
            squared = squared + offset * offset
        slot = lax.broadcasted_iota(i32, (chunk, own), 0) + j * chunk
        mark = jnp.where(slot < tally[...], found[3], -1.0)
        mark_out[at, :] = mark
        basis = jnp.concatenate(
            [jnp.exp(squared * (-1.0 / (w * w))) for w in radial_widths], axis=0
        )
        upper, lower = split(basis)
        pre = dot_n(first[...], jnp.concatenate([upper, lower, upper], axis=0))
        gate = 0.5 * jnp.tanh(0.5 * pre) + 0.5
        active[...] = pre * gate
        for s in range(kinds):
            total = pooled[s * hidden : (s + 1) * hidden, :]
            for m in range(chunk):
                hit = jnp.broadcast_to(mark[m : m + 1, :], (hidden, own)) == float(s)
                total = total + jnp.where(hit, active[m * hidden : (m + 1) * hidden, :], 0.0)
            pooled[s * hidden : (s + 1) * hidden, :] = total
        return carry

    lax.fori_loop(0, chunks, step, 0)
    answers = dot3(ball[...], pooled[...])
    for s in range(kinds):
        answers = answers + base[:, s : s + 1] * jnp.where(kind[...] == s, 1.0, 0.0)
    activation[...] = answers[8:24]
    charges = answers[0:8]
    for z in range(ranks):
        send[z, 0:8, :] = charges[:, 0:128]
        send[z, 8:16, :] = charges[:, 128:256]
        send[z, 16:56, :] = counts[z]


def response_kernel(
    activation, final, disp, marks, first, mixed_high, mixed_low, ball, out, upstream, bend, upper,
    lower,
):
    value = activation[...]
    gate = 0.5 * jnp.tanh(0.5 * value) + 0.5
    ramp = final[...] * gate * (1.0 + value * (1.0 - gate))
    upstream[...] = dot_c(ball[8:24, :], ramp)

    def step(j, carry):
        at = pl.ds(pl.multiple_of(j * chunk, chunk), chunk)
        mark = marks[at, :]
        squared = disp[0, at, :] * disp[0, at, :]
        squared = squared + disp[1, at, :] * disp[1, at, :] + disp[2, at, :] * disp[2, at, :]
        basis = [jnp.exp(squared * (-1.0 / (w * w))) for w in radial_widths]
        lean = [b * (-2.0 / (w * w)) for b, w in zip(basis, radial_widths)]
        ah, al = split(jnp.concatenate(basis, axis=0))
        bh, bl = split(jnp.concatenate(lean, axis=0))
        pre = dot_n(first[...], jnp.concatenate([ah, al, ah], axis=0))
        gate = 0.5 * jnp.tanh(0.5 * pre) + 0.5
        bend[...] = (gate + pre * gate * (1.0 - gate)) * dot_n(
            first[...], jnp.concatenate([bh, bl, bh], axis=0)
        )
        upper[...], lower[...] = split(bend[...])
        mixed = dot_n(mixed_high[...], upper[...]) + (
            dot_n(mixed_low[...], upper[...]) + dot_n(mixed_high[...], lower[...])
        )
        for l in range(8):
            total = jnp.zeros((chunk, own), f32)
            for s in range(kinds):
                row = (l * kinds + s) * 8
                total = jnp.where(mark == float(s), mixed[row : row + 8, :], total)
            out[l, at, :] = total
        for m in range(chunk):
            mine = jnp.broadcast_to(mark[m : m + 1, :], (hidden, own))
            chosen = jnp.zeros((hidden, own), f32)
            for s in range(kinds):
                chosen = jnp.where(
                    mine == float(s), upstream[s * hidden : (s + 1) * hidden, :], chosen
                )
            line = jnp.sum(chosen * bend[m * hidden : (m + 1) * hidden, :], axis=0, keepdims=True)
            out[8, pl.ds(j * chunk + m, 1), :] = line
        return carry

    lax.fori_loop(0, chunks, step, 0)


def structure_kernel(
    core, got, waves_x, high, low, after, mine, other, total, extra, left_high, left_low
):
    total[...] = jnp.zeros_like(total)
    extra[...] = jnp.zeros_like(extra)

    def step(z, carry):
        at = pl.ds(pl.multiple_of(z * own, own), own)
        charge = jnp.concatenate([got[z, 0:8, :], got[z, 8:16, :]], axis=1)
        for f in range(0, 2 * top, 2):
            pair = jnp.concatenate(
                [charge * waves_x[f : f + 1, at], charge * waves_x[f + 1 : f + 2, at]], axis=0
            )
            upper, lower = split(pair)
            left_high[f * 8 : f * 8 + 16, :] = upper
            left_low[f * 8 : f * 8 + 16, :] = lower
        plane_high, plane_low = high[:, at], low[:, at]
        total[...] += dot_t(plane_high, left_high[...]) + (
            dot_t(plane_low, left_high[...]) + dot_t(plane_high, left_low[...])
        )
        upper, lower = split(charge)
        extra[:, 0:waves] += dot_t(upper, plane_high) + (
            dot_t(lower, plane_high) + dot_t(upper, plane_low)
        )
        return carry

    lax.fori_loop(0, ranks, step, 0)
    first = core[0] == 0
    real, imaginary = total[0:plane_rows, :], total[plane_rows:waves, :]
    begin, rest = extra[:, 0:128], extra[:, 128:256]
    for ref, one in ((mine, first), (other, jnp.logical_not(first))):
        ref[0:plane_rows, :] = jnp.where(one, real, imaginary)
        ref[plane_rows : plane_rows + 8, 0:128] = jnp.where(one, begin, rest)
        ref[plane_rows : plane_rows + 8, 128:256] = jnp.zeros((8, 128), f32)


def weight_kernel(rank, edges, got, out):
    counts = got[0, 16:56, :]
    for z in range(1, ranks):
        counts = counts + got[z, 16:56, :]
    lane = lax.broadcasted_iota(i32, (top, 128), 1)
    spread = jnp.where(
        lax.shift_right_logical(lane, 3) == lax.broadcasted_iota(i32, (top, 128), 0), 1.0, 0.0
    )
    flat = jnp.where(lax.broadcasted_iota(i32, (8, 128), 0) == 0, 1.0, 0.0)
    both = dot_c(counts[0:top], spread)[0:plane_rows]
    apart = dot_c(counts[top : 2 * top], spread)[0:plane_rows]
    zero = dot_c(counts[2 * top : 2 * top + 8], flat)[0:plane_rows]
    shape = (plane_rows, 128)
    ky, kz = plane_of(rank[0], shape, 0)
    kx = (lax.shift_right_logical(lax.broadcasted_iota(i32, shape, 1), 3) + 1).astype(f32)
    qx, qy, qz = (tau * k / edges[d : d + 1, 0:128] for d, k in enumerate((kx, ky, kz)))
    flat_square = qy * qy + qz * qz
    square = qx * qx + flat_square

    def weigh(q):
        return (tau / atoms_all) * jnp.exp((-0.5 * gauss_width * gauss_width) * q) / q

    weight = weigh(square)
    out[0] = both * weight
    out[1] = apart * weight
    out[2] = zero * jnp.where(flat_square > 0.0, weigh(jnp.maximum(flat_square, 1e-6)), 0.0)


def turn_table(table, blocks, table_high, table_low):
    for block in range(blocks):
        at = slice(block * 128, block * 128 + 128)
        table_high[at, 0:waves], table_low[at, 0:waves] = split(jnp.transpose(table[:, at]))


def potential_kernel(
    core, mine, other, weights, waves_x, high, low, potential, table, table_high, table_low, result
):
    first = core[0] == 0
    real = jnp.where(first, mine[0:plane_rows, :], other[0:plane_rows, :])
    imaginary = jnp.where(first, other[0:plane_rows, :], mine[0:plane_rows, :])
    tail = slice(plane_rows, plane_rows + 8)
    begin = jnp.where(first, mine[tail, 0:128], other[tail, 0:128])
    rest = jnp.where(first, other[tail, 0:128], mine[tail, 0:128])
    lane = lax.broadcasted_iota(i32, (8, 128), 1)
    repeat = jnp.where((lane & 7) == lax.broadcasted_iota(i32, (8, 128), 0), 1.0, 0.0)
    lone = dot_c(jnp.concatenate([begin, rest], axis=1), repeat)
    both, apart, zero = weights[0], weights[1], weights[2]
    real_c, real_s = real[:, 0:128], real[:, 128:256]
    imag_c, imag_s = imaginary[:, 0:128], imaginary[:, 128:256]
    upper, lower = slice(0, plane_rows), slice(plane_rows, waves)
    table[upper, 0:128] = both * real_c - apart * imag_s
    table[lower, 0:128] = both * imag_c + apart * real_s
    table[upper, 128:256] = both * real_s + apart * imag_c
    table[lower, 128:256] = both * imag_s - apart * real_c
    table[upper, 256:384] = zero * lone[0:plane_rows]
    table[lower, 256:384] = zero * lone[plane_rows:waves]
    turn_table(table, 3, table_high, table_low)

    def step(z, carry):
        at = pl.ds(pl.multiple_of(z * own, own), own)
        plane_high, plane_low = high[:, at], low[:, at]
        lines = table_high[0:272, 0:waves]
        result[...] = dot_n(lines, plane_high) + (
            dot_n(table_low[0:272, 0:waves], plane_high) + dot_n(lines, plane_low)
        )
        total = result[256:264, :]
        for f in range(2 * top):
            total = total + waves_x[f : f + 1, at] * result[f * 8 : f * 8 + 8, :]
        potential[z] = total
        return carry

    lax.fori_loop(0, ranks, step, 0)


def gradient_kernel(
    rank, edges, table, got, waves_x, high, low, gradient, wide, table_high, table_low, result
):
    shape = (plane_rows, 128)
    ky, kz = plane_of(rank[0], shape, 0)
    ty, tz = tau * ky, tau * kz
    upper, lower = slice(0, plane_rows), slice(plane_rows, waves)
    for part in range(2):
        at = slice(part * 128, part * 128 + 128)
        re, im = table[upper, at], table[lower, at]
        wide[upper, at], wide[lower, at] = re, im
        for form, scale in ((1, ty), (2, tz)):
            at = slice(form * 256 + part * 128, form * 256 + part * 128 + 128)
            wide[upper, at] = scale * im
            wide[lower, at] = -(scale * re)
    re, im = table[upper, 256:384], table[lower, 256:384]
    group = lax.shift_right_logical(lax.broadcasted_iota(i32, shape, 1), 3)
    turn = jnp.where(group == 0, ty, tz)
    wide[upper, 768:896] = turn * im
    wide[lower, 768:896] = -(turn * re)
    turn_table(wide, 7, table_high, table_low)

    def step(z, carry):
        at = pl.ds(pl.multiple_of(z * own, own), own)
        plane_high, plane_low = high[:, at], low[:, at]
        lines = table_high[0:784, 0:waves]
        result[...] = dot_n(lines, plane_high) + (
            dot_n(table_low[0:784, 0:waves], plane_high) + dot_n(lines, plane_low)
        )
        total = [jnp.zeros((8, own), f32), result[768:776, :], result[776:784, :]]
        for f in range(2 * top):
            wave = waves_x[f : f + 1, at]
            for form in (1, 2):
                row = form * 256 + f * 8
                total[form] = total[form] + wave * result[row : row + 8, :]
        for k in range(top):
            cosine, sine = waves_x[k : k + 1, at], waves_x[top + k : top + k + 1, at]
            turn = tau * (k + 1)
            total[0] = total[0] + (turn * cosine) * result[(top + k) * 8 : (top + k) * 8 + 8, :]
            total[0] = total[0] - (turn * sine) * result[k * 8 : k * 8 + 8, :]
        charge = jnp.concatenate([got[z, 0:8, :], got[z, 8:16, :]], axis=1)
        for d in range(3):
            line = jnp.sum(charge * total[d], axis=0, keepdims=True) / edges[d : d + 1, :]
            gradient[z, 2 * d : 2 * d + 1, :] = line[:, 0:128]
            gradient[z, 2 * d + 1 : 2 * d + 2, :] = line[:, 128:256]
        return carry

    lax.fori_loop(0, ranks, step, 0)


def pair_kernel(
    got, response, disp, listing, lines, cells0, cells3, mid0, mid3, domain, direct, left, right,
    total, pulled,
):
    potential = got[0]
    for z in range(1, ranks):
        potential = potential + got[z]
    total[...] = jnp.zeros_like(total)
    pulled[...] = jnp.zeros_like(pulled)
    row_high = lax.broadcasted_iota(i32, (32, own), 0)
    row_low = lax.broadcasted_iota(i32, (128, own), 0)

    def step(j, carry):
        at = pl.ds(pl.multiple_of(j * chunk, chunk), chunk)
        offsets = [disp[d, at, :] for d in range(3)]
        radial = response[8, at, :]
        for l in range(8):
            radial = radial + potential[l : l + 1, :] * response[l, at, :]
        pulls = [radial * offset for offset in offsets]
        index = listing[at, :]
        low, high = index & 127, lax.shift_right_logical(index, 7)
        pieces = []
        for d in range(3):
            pulled[d] += pulls[d]
            main = pulls[d].astype(bf16).astype(f32)
            pieces.append((main, pulls[d] - main))
        for m in range(chunk):
            lanes = slice(m * own, (m + 1) * own)
            hit = jnp.broadcast_to(high[m : m + 1, :], (32, own)) == row_high
            for part in range(2):
                for d in range(3):
                    row = part * 96 + d * 32
                    left[row : row + 32, lanes] = jnp.where(
                        hit, pieces[d][part][m : m + 1, :], 0.0
                    ).astype(bf16)
            spot = jnp.broadcast_to(low[m : m + 1, :], (128, own)) == row_low
            right[:, lanes] = jnp.where(spot, 1.0, 0.0).astype(bf16)
        total[...] += dot_t(left[...], right[...])
        return carry

    lax.fori_loop(0, chunks, step, 0)
    scattered = total[0:96, :] + total[96:192, :]
    nothing = jnp.zeros((1, 128), f32)
    for u in range(4):
        for c in range(4):
            for ref, v in ((cells0, 0), (cells3, 3)):
                spot = c * 32 + 16 + u * 4 + v
                value = scattered[spot : spot + 1, :] if c < 3 else nothing
                ref[u * 4 + c : u * 4 + c + 1, :] = value
    for ref, u in ((mid0, 0), (mid3, 3)):
        for j in range(2):
            for c in range(4):
                spot = c * 32 + 16 + u * 4 + 1 + j
                value = scattered[spot : spot + 1, :] if c < 3 else nothing
                ref[j * 4 + c : j * 4 + c + 1, :] = value
    for z in range(ranks):
        for d in range(3):
            for half in range(2):
                spot, r = d * 32 + z * 2 + half, 2 * d + half
                domain[z, r : r + 1, :] = scattered[spot : spot + 1, :] + lines[z, r : r + 1, :]
        domain[z, 6:8, :] = jnp.zeros((2, 128), f32)
    for d in range(3):
        line = -jnp.sum(pulled[d], axis=0, keepdims=True)
        direct[2 * d : 2 * d + 1, :] = line[:, 0:128]
        direct[2 * d + 1 : 2 * d + 2, :] = line[:, 128:256]
    direct[6:8, :] = jnp.zeros((2, 128), f32)


def echo_kernel(above, below, mid0, mid3, send0, send3, inner0, inner1):
    for u, ref in ((0, send0), (1, inner0), (2, inner1), (3, send3)):
        both = jnp.concatenate([below[u * 4 : u * 4 + 4, :], above[u * 4 : u * 4 + 4, :]], axis=0)
        if u == 0:
            both = both + mid0[...]
        if u == 3:
            both = both + mid3[...]
        ref[...] = both


def border_back_kernel(inner0, inner1, from_left, from_right, rows, domain, out):
    cells = (inner0[...] + from_left[...], inner1[...] + from_right[...])
    row_high = lax.broadcasted_iota(i32, (16, 128), 0)
    row_low = lax.broadcasted_iota(i32, (128, 128), 0)
    total = jnp.zeros((96, 128), f32)
    for i in range(2):
        index = rows[i]
        low, high = index & 127, lax.shift_right_logical(index, 7)
        for j in range(2):
            hit = jnp.broadcast_to(high[j : j + 1, :], (16, 128)) == row_high
            spot = jnp.broadcast_to(low[j : j + 1, :], (128, 128)) == row_low
            left = []
            for part in range(2):
                for c in range(3):
                    value = cells[i][j * 4 + c : j * 4 + c + 1, :]
                    main = value.astype(bf16).astype(f32)
                    left.append(jnp.where(hit, main if part == 0 else value - main, 0.0))
            total = total + dot_t(
                jnp.concatenate(left, axis=0).astype(bf16),
                jnp.where(spot, 1.0, 0.0).astype(bf16),
            )
    total = total[0:48, :] + total[48:96, :]
    for z in range(ranks):
        lines = [total[d * 16 + z * 2 : d * 16 + z * 2 + 2, :] for d in range(3)]
        lines.append(jnp.zeros((2, 128), f32))
        out[z] = domain[z] + jnp.concatenate(lines, axis=0)


def step_kernel(edges, got, direct, place, speed, kind, kicks, force_out, place_out, speed_out):
    gradient = direct[...]
    for z in range(ranks):
        gradient = gradient + got[z]
    species = kind[...]
    mass = jnp.zeros((1, own), f32)
    for s in range(kinds):
        mass = jnp.where(species == s, masses_table[s], mass)
    retain = math.exp(-friction * time_step)
    spread = jnp.sqrt((1.0 - retain * retain) / mass)
    for d in range(3):
        row = slice(d, d + 1)
        force = -jnp.concatenate(
            [gradient[2 * d : 2 * d + 1, :], gradient[2 * d + 1 : 2 * d + 2, :]], axis=1
        )
        halfway = speed[row, :] + 0.5 * time_step * force / mass
        updated = retain * halfway + spread * kicks[row, :]
        force_out[row, :] = force
        speed_out[row, :] = updated
        place_out[row, :] = place[row, :] + 0.5 * time_step * (halfway + updated) / edges[row, :]


def shift(axis, by):
    count = lax.axis_size(axis)
    return [(i, (i + by) % count) for i in range(count)]


def partners():
    maps = (
        lambda x, yl, yh, c: (x, yl, yh, 1 - c),
        lambda x, yl, yh, c: (x, 1 - yl, yh, c),
        lambda x, yl, yh, c: (x, 1 - yl, 1 - yh, c),
        lambda x, yl, yh, c: (x ^ 1, yl, yh, c),
        lambda x, yl, yh, c: (3 - x, yl, yh, c),
    )
    places = [(x, a, b, c) for x in range(4) for a in range(2) for b in range(2) for c in range(2)]
    number = {p: (p[0] * 2 + p[1]) * 4 + p[2] * 2 + p[3] for p in places}
    return [[(number[p], number[m(*p)]) for p in places] for m in maps]


def body(
    fractional_placements,
    particle_speeds,
    element_kinds,
    adjacent_padded_indices,
    adjacent_valid_tally,
    border_particle_rows,
    reciprocal_integer_triples,
    cell_edge_sizes,
    friction_random_kicks,
    element_feature_vectors,
    distance_net_initial_weights,
    distance_net_final_weights,
    message_blend_matrix,
    energy_head_initial_weights,
    energy_head_final_weights,
    hidden_electric_projection,
):
    rank = lax.axis_index("ka").astype(i32).reshape(1)
    core = (lax.axis_index("gy") % 2).astype(i32).reshape(1)
    packed, place, kind = call(
        pack_kernel,
        [((ranks, 8, 128), f32), ((3, own), f32), ((1, own), i32)],
        [far] * 2,
        [pltpu.SemaphoreType.DMA((2,))],
    )(fractional_placements, element_kinds.reshape(1, own))
    table = lax.all_to_all(packed, "ka", 0, 0)
    edges, listing, tally, rows, counts, first, mixed_high, mixed_low, ball, base, final = call(
        prepare_kernel,
        [
            ((8, own), f32),
            ((slots, own), i32),
            ((1, own), i32),
            ((2, 2, 128), i32),
            ((ranks, 40, 128), f32),
            ((chunk * hidden, 192), bf16),
            ((8 * 8 * kinds, chunk * hidden), bf16),
            ((8 * 8 * kinds, chunk * hidden), bf16),
            ((24, kinds * hidden), f32),
            ((24, 8), f32),
            ((16, 1), f32),
        ],
        [far] * 12,
        [
            pltpu.VMEM((3, reciprocal_integer_triples.shape[1]), i32),
            pltpu.VMEM((8, hidden), f32),
            pltpu.VMEM((hidden, 128), f32),
            pltpu.VMEM((8, 128), f32),
            pltpu.VMEM((128, 128), f32),
            pltpu.VMEM((24, 128), f32),
            pltpu.VMEM((1, 16), f32),
            pltpu.SMEM((3,), f32),
            pltpu.VMEM((8 * 8 * kinds, chunk * hidden), f32),
            pltpu.SemaphoreType.DMA((12,)),
        ],
        cost=work(8),
    )(
        cell_edge_sizes, adjacent_padded_indices.T, adjacent_valid_tally.reshape(1, own),
        border_particle_rows, reciprocal_integer_triples, distance_net_initial_weights,
        distance_net_final_weights, element_feature_vectors, message_blend_matrix,
        energy_head_initial_weights.T, hidden_electric_projection.T,
        energy_head_final_weights.reshape(1, 16),
    )
    cell0, cell1 = call(border_kernel, [((8, 128), f32)] * 2, [vmem] * 2)(table, rows)
    left = lax.ppermute(cell1, "gx", shift("gx", 1))
    right = lax.ppermute(cell0, "gx", shift("gx", -1))
    near = call(own_gather_kernel, [((4, slots, own), f32)], [vmem] * 2, cost=work(2))(
        table, listing
    )[0]
    head, tail = call(columns_kernel, [((16, 128), f32)] * 2, [vmem] * 4 + [anywhere])(
        left, cell0, cell1, right, near
    )
    tail_in = lax.ppermute(tail, "gy", shift("gy", 1))
    head_in = lax.ppermute(head, "gy", shift("gy", -1))
    high, low, waves_x = call(
        factor_kernel,
        [((waves, ranks * own), bf16), ((waves, ranks * own), bf16), ((2 * top, ranks * own), f32)],
        [smem, vmem],
        cost=work(2),
    )(rank, table)

    send, activation, disp, marks = call(
        message_kernel,
        [
            ((ranks, 56, 128), f32),
            ((16, own), f32),
            ((3, slots, own), f32),
            ((slots, own), f32),
        ],
        [vmem] * 14 + [anywhere],
        [
            pltpu.VMEM((64, 128), f32),
            pltpu.VMEM((kinds * hidden, own), f32),
            pltpu.VMEM((chunk * hidden, own), f32),
        ],
        cost=work(8),
    )(
        edges, listing, near, left, right, tail_in, head_in, place, kind, tally, counts, first,
        ball, base, waves_x,
    )
    got = lax.all_to_all(send, "ka", 0, 0)
    response = call(
        response_kernel,
        [((9, slots, own), f32)],
        [vmem] * 8,
        [
            pltpu.VMEM((kinds * hidden, own), f32),
            pltpu.VMEM((chunk * hidden, own), f32),
            pltpu.VMEM((chunk * hidden, own), bf16),
            pltpu.VMEM((chunk * hidden, own), bf16),
        ],
        cost=work(8),
    )(activation, final, disp, marks, first, mixed_high, mixed_low, ball)[0]

    mine, other = call(
        structure_kernel,
        [((plane_rows + 8, own), f32)] * 2,
        [smem] + [vmem] * 4 + [anywhere],
        [
            pltpu.VMEM((waves, own), f32),
            pltpu.VMEM((8, own), f32),
            pltpu.VMEM((own, own), bf16),
            pltpu.VMEM((own, own), bf16),
        ],
        cost=work(3),
    )(core, got, waves_x, high, low, response)
    swaps = partners()
    both = ("gx", "gy")
    summed = mine + lax.ppermute(other, both, swaps[0])
    for swap in swaps[1:]:
        summed = summed + lax.ppermute(summed, both, swap)
    opposite = lax.ppermute(summed, both, swaps[0])

    weights = call(
        weight_kernel, [((3, plane_rows, 128), f32)], [smem] + [vmem] * 2, cost=work(0.5)
    )(rank, edges, got)[0]
    potential, spectrum = call(
        potential_kernel,
        [((ranks, 8, own), f32), ((waves, 384), f32)],
        [smem] + [vmem] * 6,
        [
            pltpu.VMEM((384, own), bf16),
            pltpu.VMEM((384, own), bf16),
            pltpu.VMEM((272, own), f32),
        ],
        cost=work(2),
    )(core, summed, opposite, weights, waves_x, high, low)
    shares = lax.all_to_all(potential, "ka", 0, 0)
    lines = call(
        gradient_kernel,
        [((ranks, 8, 128), f32)],
        [smem] + [vmem] * 6,
        [
            pltpu.VMEM((waves, 896), f32),
            pltpu.VMEM((896, own), bf16),
            pltpu.VMEM((896, own), bf16),
            pltpu.VMEM((784, own), f32),
        ],
        cost=work(5),
    )(rank, edges, spectrum, got, waves_x, high, low)[0]
    cells0, cells3, mid0, mid3, domain, direct = call(
        pair_kernel,
        [
            ((16, 128), f32),
            ((16, 128), f32),
            ((8, 128), f32),
            ((8, 128), f32),
            ((ranks, 8, 128), f32),
            ((8, 128), f32),
        ],
        [vmem] * 5,
        [
            pltpu.VMEM((192, chunk * own), bf16),
            pltpu.VMEM((128, chunk * own), bf16),
            pltpu.VMEM((192, 128), f32),
            pltpu.VMEM((3, chunk, own), f32),
        ],
        cost=work(4),
    )(shares, response, disp, listing, lines)
    above = lax.ppermute(cells0, "gy", shift("gy", -1))
    below = lax.ppermute(cells3, "gy", shift("gy", 1))
    send0, send3, inner0, inner1 = call(echo_kernel, [((8, 128), f32)] * 4, [vmem] * 4)(
        above, below, mid0, mid3
    )
    from_right = lax.ppermute(send0, "gx", shift("gx", -1))
    from_left = lax.ppermute(send3, "gx", shift("gx", 1))
    reaction = call(border_back_kernel, [((ranks, 8, 128), f32)], [vmem] * 6)(
        inner0, inner1, from_left, from_right, rows, domain
    )[0]
    returned = lax.all_to_all(reaction, "ka", 0, 0)
    forces, places, speeds = call(
        step_kernel, [((3, own), f32)] * 3, [vmem] * 7
    )(
        edges, returned, direct, place, particle_speeds, kind, friction_random_kicks,
    )
    return (forces, places, speeds)


def solution(mesh):
    atoms = ("gx", "gy", "ka")
    return jax.shard_map(
        body,
        mesh=mesh,
        in_specs=(
            P(None, atoms),
            P(None, atoms),
            P(atoms),
            P(atoms, None),
            P(atoms),
            P("gx", "gy", None),
            P(None, "ka"),
            P(),
            P(None, atoms),
            P(),
            P(),
            P(),
            P(),
            P(),
            P(),
            P(),
        ),
        out_specs=(P(None, atoms), P(None, atoms), P(None, atoms)),
        check_vma=False,
    )
```

```python
import functools
import math

import jax
import jax.numpy as jnp
from jax import lax
from jax.experimental import pallas as pl
from jax.experimental.pallas import tpu as pltpu
from jax.sharding import PartitionSpec as P

f32 = jnp.float32
bf16 = jnp.bfloat16
i32 = jnp.int32
masses_table = (1.008, 12.011, 15.999, 6.94, 30.974, 18.998)
radial_widths = (2.0, 4.0, 6.0, 8.0, 10.0, 12.0, 14.0, 16.0)
time_step = 0.5
friction = 0.2
gauss_width = 0.3
kinds = 6
slots = 64
hidden = 64
chunk = 8
chunks = slots // chunk
own = 256
ranks = 8
atoms_all = 65536
top = 16
span = 2 * top + 1
plane_own = 69
plane_rows = 72
waves = 2 * plane_rows
tau = 2.0 * math.pi
outer = [(u, v) for u in range(4) for v in range(4) if not (u in (1, 2) and v in (1, 2))]
vmem = pl.BlockSpec(memory_space=pltpu.VMEM)
smem = pl.BlockSpec(memory_space=pltpu.SMEM)
far = pl.BlockSpec(memory_space=pltpu.HBM)
anywhere = pl.BlockSpec(memory_space=pl.ANY)
params = pltpu.CompilerParams(vmem_limit_bytes=24 * 1024 * 1024)


def work(micros):
    return pl.CostEstimate(
        flops=int(micros * 5e8), bytes_accessed=int(micros * 2e6), transcendentals=0
    )


def call(kernel, outs, specs, scratch=(), cost=None):
    shapes = [jax.ShapeDtypeStruct(s, d) for s, d in outs]
    return pl.pallas_call(
        kernel,
        out_shape=shapes,
        in_specs=specs,
        out_specs=[vmem] * len(shapes),
        scratch_shapes=list(scratch),
        compiler_params=params,
        cost_estimate=cost,
    )


def dot_n(a, b):
    return lax.dot_general(a, b, (((1,), (0,)), ((), ())), preferred_element_type=f32)


def dot_t(a, b):
    return lax.dot_general(a, b, (((1,), (1,)), ((), ())), preferred_element_type=f32)


def dot_c(a, b):
    return lax.dot_general(
        a, b, (((0,), (0,)), ((), ())), precision=lax.Precision.HIGHEST, preferred_element_type=f32
    )


def dot_h(a, b):
    return lax.dot_general(
        a, b, (((1,), (1,)), ((), ())), precision=lax.Precision.HIGHEST, preferred_element_type=f32
    )


def split(x):
    high = x.astype(bf16)
    return high, (x - high.astype(f32)).astype(bf16)


def dot3(a, b):
    ah, al = split(a)
    bh, bl = split(b)
    return dot_n(ah, bh) + (dot_n(al, bh) + dot_n(ah, bl))


def lane_pick(row, where):
    return jnp.take_along_axis(
        jnp.broadcast_to(row, where.shape), where, axis=1, mode="promise_in_bounds"
    )


def sine_turns(w):
    square = w * w
    total = jnp.full_like(w, -(tau**11) / math.factorial(11))
    for power in (9, 7, 5, 3, 1):
        sign = -1.0 if power % 4 == 3 else 1.0
        total = total * square + sign * tau**power / math.factorial(power)
    return total * w


def circle(turns):
    t = turns - jnp.floor(turns + 0.5)
    cosine = sine_turns(0.25 - jnp.abs(t))
    folded = jnp.where(t > 0.25, 0.5 - t, jnp.where(t < -0.25, -0.5 - t, t))
    return cosine, sine_turns(folded)


def plane_of(rank, shape, axis):
    index = (lax.broadcasted_iota(i32, shape, axis) + rank * plane_own).astype(f32)
    first = jnp.floor((index + (top + 0.5)) * (1.0 / span))
    return first, index - span * first


def pack_kernel(place_far, kind_far, out, place, kind, done):
    copies = [
        pltpu.make_async_copy(place_far, place, done.at[0]),
        pltpu.make_async_copy(kind_far, kind, done.at[1]),
    ]
    for copy in copies:
        copy.start()
    for copy in copies:
        copy.wait()
    rows = []
    for c in range(3):
        rows += [place[c : c + 1, 0:128], place[c : c + 1, 128:256]]
    species = kind[...].astype(f32)
    rows += [species[:, 0:128], species[:, 128:256]]
    tile = jnp.concatenate(rows, axis=0)
    for z in range(ranks):
        out[z] = tile


def count_triples(triples, out):
    kx, ky, kz = (triples[d : d + 1, :].astype(f32) for d in range(3))
    code = span * ky + kz
    flip = jnp.where(code < 0.0, -1.0, 1.0)
    code = code * flip
    kx = kx * flip
    count = kx.shape[1]
    row = lax.broadcasted_iota(i32, (48, count), 0).astype(f32)
    wanted = jnp.where(row < top, row + 1.0, row - (top - 1.0))
    sign = jnp.where(kx < 0.0, -1.0, 1.0)
    value = jnp.where(row < top, 1.0, sign)
    line = jnp.where(row < 2 * top, jnp.where(jnp.abs(kx) == wanted, value, 0.0), 0.0)
    line = jnp.where((row == 2 * top) & (kx == 0.0), 1.0, line).astype(bf16)
    place = lax.broadcasted_iota(i32, (128, count), 0).astype(f32)
    valid = place < plane_own
    for z in range(ranks):
        hit = jnp.where(valid & (code == place + float(z * plane_own)), 1.0, 0.0).astype(bf16)
        out[z] = dot_t(line, hit)[0:40, :]


def prepare_kernel(
    edges_far, listing_far, tally_far, rows_far, triples_far, initial_far, second_far, embed_far,
    blend_far, energy_far, project_far, final_far,
    edges_out, listing, tally, rows, counts, first, mixed_high, mixed_low, ball, base, final_out,
    triples, initial, second, embed, blend, heads, final, edges, wide, done,
):
    embed[...] = jnp.zeros_like(embed)
    far = (
        (edges_far, edges), (listing_far, listing), (tally_far, tally), (rows_far, rows),
        (triples_far, triples), (initial_far, initial), (second_far, second),
        (embed_far, embed.at[0:kinds]), (blend_far, blend), (energy_far, heads.at[8:24]),
        (project_far, heads.at[0:8]), (final_far, final),
    )
    copies = [pltpu.make_async_copy(a, b, done.at[n]) for n, (a, b) in enumerate(far)]
    for copy in copies:
        copy.start()
    for copy in copies:
        copy.wait()
    for d in range(3):
        edges_out[d : d + 1, :] = jnp.full((1, own), 1.0, f32) * edges[d]
    edges_out[3:8, :] = jnp.zeros((5, own), f32)
    lane = lax.broadcasted_iota(i32, (8, 64), 1)
    pick = jnp.where(lax.shift_right_logical(lane, 3) == lax.broadcasted_iota(i32, (8, 64), 0), 1.0, 0.0)
    repeated = dot_c(initial[...], pick)
    lane = lax.broadcasted_iota(i32, (hidden, 64), 1) & 7
    blocks = jnp.concatenate(
        [jnp.where(lane == m, repeated, 0.0) for m in range(chunk)], axis=0
    )
    high, low = split(blocks)
    first[:, 0:64], first[:, 64:128], first[:, 128:192] = high, high, low
    through = dot_h(heads[...], blend[...])
    base[...] = dot_h(heads[...], embed[...])
    doubled = jnp.concatenate([second[...], second[...]], axis=0)
    left = lax.broadcasted_iota(i32, (24, 128), 1) < hidden
    slot = lax.broadcasted_iota(i32, (8, 128), 0)
    group = lax.shift_right_logical(lax.broadcasted_iota(i32, (8, 128), 1), 6)
    responses = []
    for s in range(kinds):
        response = dot_h(through * embed[s : s + 1, :], doubled) * (1.0 / slots)
        responses.append(response)
        for l in range(8):
            line = jnp.broadcast_to(response[l : l + 1, :], (8, 128))
            for t in range(4):
                at = (l * kinds + s) * 8
                wide[at : at + 8, t * 128 : (t + 1) * 128] = jnp.where(
                    group + 2 * t == slot, line, 0.0
                )
    for t in range(kinds // 2):
        ball[:, t * 128 : (t + 1) * 128] = jnp.where(left, responses[2 * t], responses[2 * t + 1])
    mixed_high[...], mixed_low[...] = split(wide[...])
    square = (16, 16)
    same = lax.broadcasted_iota(i32, square, 0) == lax.broadcasted_iota(i32, square, 1)
    final_out[...] = jnp.sum(
        jnp.where(same, jnp.broadcast_to(final[...], square), 0.0), axis=1, keepdims=True
    )
    count_triples(triples, counts)


def border_kernel(table, rows, cell0, cell1):
    index = jnp.concatenate([rows[0], rows[1], rows[0], rows[1]], axis=0)
    low, high = index & 127, lax.shift_right_logical(index, 7)
    for c in range(4):
        found = jnp.zeros((8, 128), f32)
        for h in range(16):
            row = table[h // 2, 2 * c + h % 2 : 2 * c + h % 2 + 1, :]
            found = jnp.where(high == h, lane_pick(row, low), found)
        for j in range(2):
            cell0[j * 4 + c : j * 4 + c + 1, :] = found[j : j + 1]
            cell1[j * 4 + c : j * 4 + c + 1, :] = found[2 + j : 3 + j]


def columns_kernel(left, cell0, cell1, right, after, head, tail):
    for u, ref in enumerate((left, cell0, cell1, right)):
        head[u * 4 : u * 4 + 4, :] = ref[0:4, :]
        tail[u * 4 : u * 4 + 4, :] = ref[4:8, :]


def own_gather_kernel(table, listing, near):
    def step(j, carry):
        at = pl.ds(pl.multiple_of(j * chunk, chunk), chunk)
        for half in range(2):
            lanes = slice(half * 128, half * 128 + 128)
            index = listing[at, lanes]
            low, high = index & 127, lax.shift_right_logical(index, 7)
            found = [jnp.zeros((chunk, 128), f32)] * 4
            for h in range(16):
                hit = high == h
                for c in range(4):
                    r = 2 * c + h % 2
                    row = table[h // 2, r : r + 1, :]
                    found[c] = jnp.where(hit, lane_pick(row, low), found[c])
            for c in range(4):
                near[c, at, lanes] = found[c]
        return carry

    lax.fori_loop(0, chunks, step, 0)


def factor_kernel(rank, table, high, low, waves_x):
    shape = (plane_rows, 128)
    ky, kz = plane_of(rank[0], shape, 0)
    kx = (lax.broadcasted_iota(i32, (top, 128), 0) + 1).astype(f32)

    def step(z, carry):
        for half in range(2):
            at = pl.ds(pl.multiple_of(z * own + half * 128, 128), 128)
            x, y, w = (table[z, 2 * c + half : 2 * c + half + 1, :] for c in range(3))
            cosine, sine = circle(ky * y + kz * w)
            both = jnp.concatenate([cosine, sine], axis=0)
            upper, lower = split(both)
            high[:, at] = upper
            low[:, at] = lower
            cosine, sine = circle(kx * x)
            waves_x[0:top, at] = cosine
            waves_x[top : 2 * top, at] = sine
        return carry

    lax.fori_loop(0, ranks, step, 0)


def message_kernel(
    edges, listing, near, left, right, head, tail, place, kind, tally, counts, first, ball, base,
    after, send, activation, disp_out, mark_out,
    cells, pooled, actives,
):
    for u in range(4):
        for c in range(4):
            cells[c * 16 + u * 4 : c * 16 + u * 4 + 1, :] = head[u * 4 + c : u * 4 + c + 1, :]
            cells[c * 16 + u * 4 + 3 : c * 16 + u * 4 + 4, :] = tail[u * 4 + c : u * 4 + c + 1, :]
    for u, ref in ((0, left), (3, right)):
        for j in range(2):
            for c in range(4):
                spot = c * 16 + u * 4 + 1 + j
                cells[spot : spot + 1, :] = ref[j * 4 + c : j * 4 + c + 1, :]
    pooled[...] = jnp.zeros_like(pooled)

    def part(j, active):
        at = pl.ds(pl.multiple_of(j * chunk, chunk), chunk)
        halves = []
        for half in range(2):
            lanes = slice(half * 128, half * 128 + 128)
            index = listing[at, lanes]
            low, high = index & 127, lax.shift_right_logical(index, 7)
            found = [near[c, at, lanes] for c in range(4)]
            for u, v in outer:
                hit = high == 16 + u * 4 + v
                for c in range(4):
                    spot = c * 16 + u * 4 + v
                    row = cells[spot : spot + 1, :]
                    found[c] = jnp.where(hit, lane_pick(row, low), found[c])
            halves.append(found)
        found = [jnp.concatenate([halves[0][c], halves[1][c]], axis=1) for c in range(4)]
        squared = jnp.zeros((chunk, own), f32)
        for d in range(3):
            offset = found[d] - place[d : d + 1, :]
            offset = offset - jnp.floor(offset + 0.5)
            offset = offset * edges[d : d + 1, :]
            disp_out[d, at, :] = offset
            squared = squared + offset * offset
        slot = lax.broadcasted_iota(i32, (chunk, own), 0) + j * chunk
        mark = jnp.where(slot < tally[...], found[3], -1.0)
        mark_out[at, :] = mark
        basis = jnp.concatenate(
            [jnp.exp(squared * (-1.0 / (w * w))) for w in radial_widths], axis=0
        )
        upper, lower = split(basis)
        pre = dot_n(first[...], jnp.concatenate([upper, lower, upper], axis=0))
        gate = 0.5 * jnp.tanh(0.5 * pre) + 0.5
        active[...] = pre * gate
        for s in range(kinds):
            total = pooled[s * hidden : (s + 1) * hidden, :]
            for m in range(chunk):
                hit = jnp.broadcast_to(mark[m : m + 1, :], (hidden, own)) == float(s)
                total = total + jnp.where(hit, active[m * hidden : (m + 1) * hidden, :], 0.0)
            pooled[s * hidden : (s + 1) * hidden, :] = total

    paired(chunks, part, (actives,))
    answers = dot3(ball[...], pooled[...])
    for s in range(kinds):
        answers = answers + base[:, s : s + 1] * jnp.where(kind[...] == s, 1.0, 0.0)
    activation[...] = answers[8:24]
    charges = answers[0:8]
    for z in range(ranks):
        send[z, 0:8, :] = charges[:, 0:128]
        send[z, 8:16, :] = charges[:, 128:256]
        send[z, 16:56, :] = counts[z]


def response_start(activation, final, ball, upstream):
    value = activation[...]
    gate = 0.5 * jnp.tanh(0.5 * value) + 0.5
    ramp = final[...] * gate * (1.0 + value * (1.0 - gate))
    upstream[...] = dot_c(ball[8:24, :], ramp)


def paired(count, part, scratch):
    def step(pair, carry):
        for p in range(2):
            part(pair * 2 + p, *[ref.at[p] for ref in scratch])
        return carry

    lax.fori_loop(0, count // 2, step, 0)


def response_kernel(begin, count, first_part, *refs):
    if first_part:
        activation, final, ball, disp, marks, first, mixed_high, mixed_low = refs[:8]
        out, upstream = refs[8:10]
        response_start(activation, final, ball, upstream)
    else:
        upstream, disp, marks, first, mixed_high, mixed_low, out = refs[:7]
    bends, uppers, lowers = refs[-3:]

    def part(j, bend, upper, lower):
        at = pl.ds(pl.multiple_of((j + begin) * chunk, chunk), chunk)
        to = pl.ds(pl.multiple_of(j * chunk, chunk), chunk)
        mark = marks[at, :]
        squared = disp[0, at, :] * disp[0, at, :]
        squared = squared + disp[1, at, :] * disp[1, at, :] + disp[2, at, :] * disp[2, at, :]
        basis = [jnp.exp(squared * (-1.0 / (w * w))) for w in radial_widths]
        lean = [b * (-2.0 / (w * w)) for b, w in zip(basis, radial_widths)]
        ah, al = split(jnp.concatenate(basis, axis=0))
        bh, bl = split(jnp.concatenate(lean, axis=0))
        pre = dot_n(first[...], jnp.concatenate([ah, al, ah], axis=0))
        gate = 0.5 * jnp.tanh(0.5 * pre) + 0.5
        bend[...] = (gate + pre * gate * (1.0 - gate)) * dot_n(
            first[...], jnp.concatenate([bh, bl, bh], axis=0)
        )
        upper[...], lower[...] = split(bend[...])
        mixed = dot_n(mixed_high[...], upper[...]) + (
            dot_n(mixed_low[...], upper[...]) + dot_n(mixed_high[...], lower[...])
        )
        for l in range(8):
            total = jnp.zeros((chunk, own), f32)
            for s in range(kinds):
                row = (l * kinds + s) * 8
                total = jnp.where(mark == float(s), mixed[row : row + 8, :], total)
            out[l, to, :] = total
        for m in range(chunk):
            mine = jnp.broadcast_to(mark[m : m + 1, :], (hidden, own))
            chosen = jnp.zeros((hidden, own), f32)
            for s in range(kinds):
                chosen = jnp.where(
                    mine == float(s), upstream[s * hidden : (s + 1) * hidden, :], chosen
                )
            line = jnp.sum(chosen * bend[m * hidden : (m + 1) * hidden, :], axis=0, keepdims=True)
            out[8, pl.ds(j * chunk + m, 1), :] = line

    paired(count, part, (bends, uppers, lowers))


def structure_kernel(
    core, got, waves_x, high, low, after, mine, other, total, extra, lefts_high, lefts_low
):
    total[...] = jnp.zeros_like(total)
    extra[...] = jnp.zeros_like(extra)

    def part(z, left_high, left_low):
        at = pl.ds(pl.multiple_of(z * own, own), own)
        charge = jnp.concatenate([got[z, 0:8, :], got[z, 8:16, :]], axis=1)
        for f in range(0, 2 * top, 2):
            pair = jnp.concatenate(
                [charge * waves_x[f : f + 1, at], charge * waves_x[f + 1 : f + 2, at]], axis=0
            )
            upper, lower = split(pair)
            left_high[f * 8 : f * 8 + 16, :] = upper
            left_low[f * 8 : f * 8 + 16, :] = lower
        plane_high, plane_low = high[:, at], low[:, at]
        total[...] += dot_t(plane_high, left_high[...]) + (
            dot_t(plane_low, left_high[...]) + dot_t(plane_high, left_low[...])
        )
        upper, lower = split(charge)
        extra[:, 0:waves] += dot_t(upper, plane_high) + (
            dot_t(lower, plane_high) + dot_t(upper, plane_low)
        )

    paired(ranks, part, (lefts_high, lefts_low))
    first = core[0] == 0
    real, imaginary = total[0:plane_rows, :], total[plane_rows:waves, :]
    begin, rest = extra[:, 0:128], extra[:, 128:256]
    for ref, one in ((mine, first), (other, jnp.logical_not(first))):
        ref[0:plane_rows, :] = jnp.where(one, real, imaginary)
        ref[plane_rows : plane_rows + 8, 0:128] = jnp.where(one, begin, rest)
        ref[plane_rows : plane_rows + 8, 128:256] = jnp.zeros((8, 128), f32)


def weight_kernel(rank, edges, got, out):
    counts = got[0, 16:56, :]
    for z in range(1, ranks):
        counts = counts + got[z, 16:56, :]
    lane = lax.broadcasted_iota(i32, (top, 128), 1)
    spread = jnp.where(
        lax.shift_right_logical(lane, 3) == lax.broadcasted_iota(i32, (top, 128), 0), 1.0, 0.0
    )
    flat = jnp.where(lax.broadcasted_iota(i32, (8, 128), 0) == 0, 1.0, 0.0)
    both = dot_c(counts[0:top], spread)[0:plane_rows]
    apart = dot_c(counts[top : 2 * top], spread)[0:plane_rows]
    zero = dot_c(counts[2 * top : 2 * top + 8], flat)[0:plane_rows]
    shape = (plane_rows, 128)
    ky, kz = plane_of(rank[0], shape, 0)
    kx = (lax.shift_right_logical(lax.broadcasted_iota(i32, shape, 1), 3) + 1).astype(f32)
    qx, qy, qz = (tau * k / edges[d : d + 1, 0:128] for d, k in enumerate((kx, ky, kz)))
    flat_square = qy * qy + qz * qz
    square = qx * qx + flat_square

    def weigh(q):
        return (tau / atoms_all) * jnp.exp((-0.5 * gauss_width * gauss_width) * q) / q

    weight = weigh(square)
    out[0] = both * weight
    out[1] = apart * weight
    out[2] = zero * jnp.where(flat_square > 0.0, weigh(jnp.maximum(flat_square, 1e-6)), 0.0)


def turn_table(table, blocks, table_high, table_low):
    for block in range(blocks):
        at = slice(block * 128, block * 128 + 128)
        table_high[at, 0:waves], table_low[at, 0:waves] = split(jnp.transpose(table[:, at]))


def potential_kernel(
    core, mine, other, weights, waves_x, high, low, potential, table, table_high, table_low, results
):
    first = core[0] == 0
    real = jnp.where(first, mine[0:plane_rows, :], other[0:plane_rows, :])
    imaginary = jnp.where(first, other[0:plane_rows, :], mine[0:plane_rows, :])
    tail = slice(plane_rows, plane_rows + 8)
    begin = jnp.where(first, mine[tail, 0:128], other[tail, 0:128])
    rest = jnp.where(first, other[tail, 0:128], mine[tail, 0:128])
    lane = lax.broadcasted_iota(i32, (8, 128), 1)
    repeat = jnp.where((lane & 7) == lax.broadcasted_iota(i32, (8, 128), 0), 1.0, 0.0)
    lone = dot_c(jnp.concatenate([begin, rest], axis=1), repeat)
    both, apart, zero = weights[0], weights[1], weights[2]
    real_c, real_s = real[:, 0:128], real[:, 128:256]
    imag_c, imag_s = imaginary[:, 0:128], imaginary[:, 128:256]
    upper, lower = slice(0, plane_rows), slice(plane_rows, waves)
    table[upper, 0:128] = both * real_c - apart * imag_s
    table[lower, 0:128] = both * imag_c + apart * real_s
    table[upper, 128:256] = both * real_s + apart * imag_c
    table[lower, 128:256] = both * imag_s - apart * real_c
    table[upper, 256:384] = zero * lone[0:plane_rows]
    table[lower, 256:384] = zero * lone[plane_rows:waves]
    turn_table(table, 3, table_high, table_low)

    def part(z, result):
        at = pl.ds(pl.multiple_of(z * own, own), own)
        plane_high, plane_low = high[:, at], low[:, at]
        lines = table_high[0:272, 0:waves]
        result[...] = dot_n(lines, plane_high) + (
            dot_n(table_low[0:272, 0:waves], plane_high) + dot_n(lines, plane_low)
        )
        total = result[256:264, :]
        for f in range(2 * top):
            total = total + waves_x[f : f + 1, at] * result[f * 8 : f * 8 + 8, :]
        potential[z] = total

    paired(ranks, part, (results,))


def gradient_kernel(
    rank, edges, table, got, waves_x, high, low, gradient, wide, table_high, table_low, results
):
    shape = (plane_rows, 128)
    ky, kz = plane_of(rank[0], shape, 0)
    ty, tz = tau * ky, tau * kz
    upper, lower = slice(0, plane_rows), slice(plane_rows, waves)
    for part in range(2):
        at = slice(part * 128, part * 128 + 128)
        re, im = table[upper, at], table[lower, at]
        wide[upper, at], wide[lower, at] = re, im
        for form, scale in ((1, ty), (2, tz)):
            at = slice(form * 256 + part * 128, form * 256 + part * 128 + 128)
            wide[upper, at] = scale * im
            wide[lower, at] = -(scale * re)
    re, im = table[upper, 256:384], table[lower, 256:384]
    group = lax.shift_right_logical(lax.broadcasted_iota(i32, shape, 1), 3)
    turn = jnp.where(group == 0, ty, tz)
    wide[upper, 768:896] = turn * im
    wide[lower, 768:896] = -(turn * re)
    turn_table(wide, 7, table_high, table_low)

    def part(z, result):
        at = pl.ds(pl.multiple_of(z * own, own), own)
        plane_high, plane_low = high[:, at], low[:, at]
        lines = table_high[0:784, 0:waves]
        result[...] = dot_n(lines, plane_high) + (
            dot_n(table_low[0:784, 0:waves], plane_high) + dot_n(lines, plane_low)
        )
        total = [jnp.zeros((8, own), f32), result[768:776, :], result[776:784, :]]
        for f in range(2 * top):
            wave = waves_x[f : f + 1, at]
            for form in (1, 2):
                row = form * 256 + f * 8
                total[form] = total[form] + wave * result[row : row + 8, :]
        for k in range(top):
            cosine, sine = waves_x[k : k + 1, at], waves_x[top + k : top + k + 1, at]
            turn = tau * (k + 1)
            total[0] = total[0] + (turn * cosine) * result[(top + k) * 8 : (top + k) * 8 + 8, :]
            total[0] = total[0] - (turn * sine) * result[k * 8 : k * 8 + 8, :]
        charge = jnp.concatenate([got[z, 0:8, :], got[z, 8:16, :]], axis=1)
        for d in range(3):
            line = jnp.sum(charge * total[d], axis=0, keepdims=True) / edges[d : d + 1, :]
            gradient[z, 2 * d : 2 * d + 1, :] = line[:, 0:128]
            gradient[z, 2 * d + 1 : 2 * d + 2, :] = line[:, 128:256]

    paired(ranks, part, (results,))


def pair_kernel(
    got, response0, response1, response2, disp, listing, lines, cells0, cells3, mid0, mid3, domain,
    direct, lefts, rights, total, pulled,
):
    potential = got[0]
    for z in range(1, ranks):
        potential = potential + got[z]
    total[...] = jnp.zeros_like(total)
    pulled[...] = jnp.zeros_like(pulled)
    row_high = lax.broadcasted_iota(i32, (32, own), 0)
    row_low = lax.broadcasted_iota(i32, (128, own), 0)

    def part(response, begin, j, left, right):
        to = pl.ds(pl.multiple_of(j * chunk, chunk), chunk)
        at = pl.ds(pl.multiple_of((j + begin) * chunk, chunk), chunk)
        offsets = [disp[d, at, :] for d in range(3)]
        radial = response[8, to, :]
        for l in range(8):
            radial = radial + potential[l : l + 1, :] * response[l, to, :]
        pulls = [radial * offset for offset in offsets]
        index = listing[at, :]
        low, high = index & 127, lax.shift_right_logical(index, 7)
        pieces = []
        for d in range(3):
            pulled[d] += pulls[d]
            main = pulls[d].astype(bf16).astype(f32)
            pieces.append((main, pulls[d] - main))
        for m in range(chunk):
            lanes = slice(m * own, (m + 1) * own)
            hit = jnp.broadcast_to(high[m : m + 1, :], (32, own)) == row_high
            for part in range(2):
                for d in range(3):
                    row = part * 96 + d * 32
                    left[row : row + 32, lanes] = jnp.where(
                        hit, pieces[d][part][m : m + 1, :], 0.0
                    ).astype(bf16)
            spot = jnp.broadcast_to(low[m : m + 1, :], (128, own)) == row_low
            right[:, lanes] = jnp.where(spot, 1.0, 0.0).astype(bf16)
        total[...] += dot_t(left[...], right[...])

    begin = 0
    for response in (response0, response1, response2):
        count = response.shape[1] // chunk
        paired(count, functools.partial(part, response, begin), (lefts, rights))
        begin += count
    scattered = total[0:96, :] + total[96:192, :]
    nothing = jnp.zeros((1, 128), f32)
    for u in range(4):
        for c in range(4):
            for ref, v in ((cells0, 0), (cells3, 3)):
                spot = c * 32 + 16 + u * 4 + v
                value = scattered[spot : spot + 1, :] if c < 3 else nothing
                ref[u * 4 + c : u * 4 + c + 1, :] = value
    for ref, u in ((mid0, 0), (mid3, 3)):
        for j in range(2):
            for c in range(4):
                spot = c * 32 + 16 + u * 4 + 1 + j
                value = scattered[spot : spot + 1, :] if c < 3 else nothing
                ref[j * 4 + c : j * 4 + c + 1, :] = value
    for z in range(ranks):
        for d in range(3):
            for half in range(2):
                spot, r = d * 32 + z * 2 + half, 2 * d + half
                domain[z, r : r + 1, :] = scattered[spot : spot + 1, :] + lines[z, r : r + 1, :]
        domain[z, 6:8, :] = jnp.zeros((2, 128), f32)
    for d in range(3):
        line = -jnp.sum(pulled[d], axis=0, keepdims=True)
        direct[2 * d : 2 * d + 1, :] = line[:, 0:128]
        direct[2 * d + 1 : 2 * d + 2, :] = line[:, 128:256]
    direct[6:8, :] = jnp.zeros((2, 128), f32)


def echo_kernel(above, below, mid0, mid3, send0, send3, inner0, inner1):
    for u, ref in ((0, send0), (1, inner0), (2, inner1), (3, send3)):
        both = jnp.concatenate([below[u * 4 : u * 4 + 4, :], above[u * 4 : u * 4 + 4, :]], axis=0)
        if u == 0:
            both = both + mid0[...]
        if u == 3:
            both = both + mid3[...]
        ref[...] = both


def border_back_kernel(inner0, inner1, from_left, from_right, rows, domain, out):
    cells = (inner0[...] + from_left[...], inner1[...] + from_right[...])
    row_high = lax.broadcasted_iota(i32, (16, 128), 0)
    row_low = lax.broadcasted_iota(i32, (128, 128), 0)
    total = jnp.zeros((96, 128), f32)
    for i in range(2):
        index = rows[i]
        low, high = index & 127, lax.shift_right_logical(index, 7)
        for j in range(2):
            hit = jnp.broadcast_to(high[j : j + 1, :], (16, 128)) == row_high
            spot = jnp.broadcast_to(low[j : j + 1, :], (128, 128)) == row_low
            left = []
            for part in range(2):
                for c in range(3):
                    value = cells[i][j * 4 + c : j * 4 + c + 1, :]
                    main = value.astype(bf16).astype(f32)
                    left.append(jnp.where(hit, main if part == 0 else value - main, 0.0))
            total = total + dot_t(
                jnp.concatenate(left, axis=0).astype(bf16),
                jnp.where(spot, 1.0, 0.0).astype(bf16),
            )
    total = total[0:48, :] + total[48:96, :]
    for z in range(ranks):
        lines = [total[d * 16 + z * 2 : d * 16 + z * 2 + 2, :] for d in range(3)]
        lines.append(jnp.zeros((2, 128), f32))
        out[z] = domain[z] + jnp.concatenate(lines, axis=0)


def step_kernel(edges, got, direct, place, speed, kind, kicks, force_out, place_out, speed_out):
    gradient = direct[...]
    for z in range(ranks):
        gradient = gradient + got[z]
    species = kind[...]
    mass = jnp.zeros((1, own), f32)
    for s in range(kinds):
        mass = jnp.where(species == s, masses_table[s], mass)
    retain = math.exp(-friction * time_step)
    spread = jnp.sqrt((1.0 - retain * retain) / mass)
    for d in range(3):
        row = slice(d, d + 1)
        force = -jnp.concatenate(
            [gradient[2 * d : 2 * d + 1, :], gradient[2 * d + 1 : 2 * d + 2, :]], axis=1
        )
        halfway = speed[row, :] + 0.5 * time_step * force / mass
        updated = retain * halfway + spread * kicks[row, :]
        force_out[row, :] = force
        speed_out[row, :] = updated
        place_out[row, :] = place[row, :] + 0.5 * time_step * (halfway + updated) / edges[row, :]


def shift(axis, by):
    count = lax.axis_size(axis)
    return [(i, (i + by) % count) for i in range(count)]


def add_kernel(after, *refs):
    total = refs[0][...]
    for ref in refs[1:-1]:
        total = total + ref[...]
    refs[-1][...] = total


def partners():
    places = [(x, y, c) for x in range(4) for y in range(4) for c in range(2)]

    def number(x, y, c):
        return (x % 4 * 2 + y % 2) * 4 + y % 4 // 2 * 2 + c

    swap = [(number(x, y, c), number(x, y, 1 - c)) for x, y, c in places]
    rings = [
        [[(number(x, y, c), number(x, y + d, c)) for x, y, c in places] for d in (1, 3, 2)],
        [[(number(x, y, c), number(x + d, y, c)) for x, y, c in places] for d in (1, 3, 2)],
    ]
    return swap, rings


def body(
    fractional_placements,
    particle_speeds,
    element_kinds,
    adjacent_padded_indices,
    adjacent_valid_tally,
    border_particle_rows,
    reciprocal_integer_triples,
    cell_edge_sizes,
    friction_random_kicks,
    element_feature_vectors,
    distance_net_initial_weights,
    distance_net_final_weights,
    message_blend_matrix,
    energy_head_initial_weights,
    energy_head_final_weights,
    hidden_electric_projection,
):
    rank = lax.axis_index("ka").astype(i32).reshape(1)
    core = (lax.axis_index("gy") % 2).astype(i32).reshape(1)
    def stay(array):
        return pltpu.with_memory_space_constraint(array, pltpu.HBM)

    packed, place, kind = call(
        pack_kernel,
        [((ranks, 8, 128), f32), ((3, own), f32), ((1, own), i32)],
        [far] * 2,
        [pltpu.SemaphoreType.DMA((2,))],
    )(stay(fractional_placements), stay(element_kinds.reshape(1, own)))
    table = lax.all_to_all(packed, "ka", 0, 0)
    edges, listing, tally, rows, counts, first, mixed_high, mixed_low, ball, base, final = call(
        prepare_kernel,
        [
            ((8, own), f32),
            ((slots, own), i32),
            ((1, own), i32),
            ((2, 2, 128), i32),
            ((ranks, 40, 128), f32),
            ((chunk * hidden, 192), bf16),
            ((8 * 8 * kinds, chunk * hidden), bf16),
            ((8 * 8 * kinds, chunk * hidden), bf16),
            ((24, kinds * hidden), f32),
            ((24, 8), f32),
            ((16, 1), f32),
        ],
        [far] * 12,
        [
            pltpu.VMEM((3, reciprocal_integer_triples.shape[1]), i32),
            pltpu.VMEM((8, hidden), f32),
            pltpu.VMEM((hidden, 128), f32),
            pltpu.VMEM((8, 128), f32),
            pltpu.VMEM((128, 128), f32),
            pltpu.VMEM((24, 128), f32),
            pltpu.VMEM((1, 16), f32),
            pltpu.SMEM((3,), f32),
            pltpu.VMEM((8 * 8 * kinds, chunk * hidden), f32),
            pltpu.SemaphoreType.DMA((12,)),
        ],
        cost=work(8),
    )(
        *map(
            stay,
            (
                cell_edge_sizes,
                adjacent_padded_indices.T,
                adjacent_valid_tally.reshape(1, own),
                border_particle_rows,
                reciprocal_integer_triples,
                distance_net_initial_weights,
                distance_net_final_weights,
                element_feature_vectors,
                message_blend_matrix,
                energy_head_initial_weights.T,
                hidden_electric_projection.T,
                energy_head_final_weights.reshape(1, 16),
            ),
        )
    )
    cell0, cell1 = call(border_kernel, [((8, 128), f32)] * 2, [vmem] * 2)(table, rows)
    left = lax.ppermute(cell1, "gx", shift("gx", 1))
    right = lax.ppermute(cell0, "gx", shift("gx", -1))
    near = call(own_gather_kernel, [((4, slots, own), f32)], [vmem] * 2, cost=work(2))(
        table, listing
    )[0]
    head, tail = call(columns_kernel, [((16, 128), f32)] * 2, [vmem] * 4 + [anywhere])(
        left, cell0, cell1, right, near
    )
    tail_in = lax.ppermute(tail, "gy", shift("gy", 1))
    head_in = lax.ppermute(head, "gy", shift("gy", -1))
    high, low, waves_x = call(
        factor_kernel,
        [((waves, ranks * own), bf16), ((waves, ranks * own), bf16), ((2 * top, ranks * own), f32)],
        [smem, vmem],
        cost=work(2),
    )(rank, table)

    send, activation, disp, marks = call(
        message_kernel,
        [
            ((ranks, 56, 128), f32),
            ((16, own), f32),
            ((3, slots, own), f32),
            ((slots, own), f32),
        ],
        [vmem] * 14 + [anywhere],
        [
            pltpu.VMEM((64, 128), f32),
            pltpu.VMEM((kinds * hidden, own), f32),
            pltpu.VMEM((2, chunk * hidden, own), f32),
        ],
        cost=work(8),
    )(
        edges, listing, near, left, right, tail_in, head_in, place, kind, tally, counts, first,
        ball, base, waves_x,
    )
    got = lax.all_to_all(send, "ka", 0, 0)
    ready = (disp, marks, first, mixed_high, mixed_low)

    def respond(begin, count, operands):
        started = begin == 0
        outs = [((9, count * chunk, own), f32)] + [((kinds * hidden, own), f32)] * started
        return call(
            functools.partial(response_kernel, begin, count, started),
            outs,
            [vmem] * len(operands),
            [
                pltpu.VMEM((2, chunk * hidden, own), f32),
                pltpu.VMEM((2, chunk * hidden, own), bf16),
                pltpu.VMEM((2, chunk * hidden, own), bf16),
            ],
            cost=work(count),
        )(*operands)

    response0, upstream = respond(0, 4, (activation, final, ball) + ready)
    response1 = respond(4, 2, (upstream,) + ready)[0]
    response2 = respond(6, 2, (upstream,) + ready)[0]

    mine, other = call(
        structure_kernel,
        [((plane_rows + 8, own), f32)] * 2,
        [smem] + [vmem] * 4 + [anywhere],
        [
            pltpu.VMEM((waves, own), f32),
            pltpu.VMEM((8, own), f32),
            pltpu.VMEM((2, own, own), bf16),
            pltpu.VMEM((2, own, own), bf16),
        ],
        cost=work(3),
    )(core, got, waves_x, high, low, response0)
    swap, rings = partners()
    both = ("gx", "gy")

    def add(after, *parts):
        return call(
            add_kernel, [((plane_rows + 8, own), f32)], [anywhere] + [vmem] * len(parts)
        )(after, *parts)[0]

    summed = mine + lax.ppermute(other, both, swap)
    for ring, after in zip(rings, (response1, response2)):
        summed = add(after, summed, *[lax.ppermute(summed, both, turn) for turn in ring])
    opposite = lax.ppermute(summed, both, swap)
    weights = call(
        weight_kernel, [((3, plane_rows, 128), f32)], [smem] + [vmem] * 2, cost=work(0.5)
    )(rank, edges, got)[0]
    potential, spectrum = call(
        potential_kernel,
        [((ranks, 8, own), f32), ((waves, 384), f32)],
        [smem] + [vmem] * 6,
        [
            pltpu.VMEM((384, own), bf16),
            pltpu.VMEM((384, own), bf16),
            pltpu.VMEM((2, 272, own), f32),
        ],
        cost=work(2),
    )(core, summed, opposite, weights, waves_x, high, low)
    shares = lax.all_to_all(potential, "ka", 0, 0)
    lines = call(
        gradient_kernel,
        [((ranks, 8, 128), f32)],
        [smem] + [vmem] * 6,
        [
            pltpu.VMEM((waves, 896), f32),
            pltpu.VMEM((896, own), bf16),
            pltpu.VMEM((896, own), bf16),
            pltpu.VMEM((2, 784, own), f32),
        ],
        cost=work(5),
    )(rank, edges, spectrum, got, waves_x, high, low)[0]
    cells0, cells3, mid0, mid3, domain, direct = call(
        pair_kernel,
        [
            ((16, 128), f32),
            ((16, 128), f32),
            ((8, 128), f32),
            ((8, 128), f32),
            ((ranks, 8, 128), f32),
            ((8, 128), f32),
        ],
        [vmem] * 7,
        [
            pltpu.VMEM((2, 192, chunk * own), bf16),
            pltpu.VMEM((2, 128, chunk * own), bf16),
            pltpu.VMEM((192, 128), f32),
            pltpu.VMEM((3, chunk, own), f32),
        ],
        cost=work(4),
    )(shares, response0, response1, response2, disp, listing, lines)
    above = lax.ppermute(cells0, "gy", shift("gy", -1))
    below = lax.ppermute(cells3, "gy", shift("gy", 1))
    send0, send3, inner0, inner1 = call(echo_kernel, [((8, 128), f32)] * 4, [vmem] * 4)(
        above, below, mid0, mid3
    )
    from_right = lax.ppermute(send0, "gx", shift("gx", -1))
    from_left = lax.ppermute(send3, "gx", shift("gx", 1))
    reaction = call(border_back_kernel, [((ranks, 8, 128), f32)], [vmem] * 6)(
        inner0, inner1, from_left, from_right, rows, domain
    )[0]
    returned = lax.all_to_all(reaction, "ka", 0, 0)
    forces, places, speeds = call(
        step_kernel, [((3, own), f32)] * 3, [vmem] * 7
    )(
        edges, returned, direct, place, particle_speeds, kind, friction_random_kicks,
    )
    return (forces, places, speeds)


def solution(mesh):
    atoms = ("gx", "gy", "ka")
    return jax.shard_map(
        body,
        mesh=mesh,
        in_specs=(
            P(None, atoms),
            P(None, atoms),
            P(atoms),
            P(atoms, None),
            P(atoms),
            P("gx", "gy", None),
            P(None, "ka"),
            P(),
            P(None, atoms),
            P(),
            P(),
            P(),
            P(),
            P(),
            P(),
            P(),
        ),
        out_specs=(P(None, atoms), P(None, atoms), P(None, atoms)),
        check_vma=False,
    )
```

```python
import functools
import math

import jax
import jax.numpy as jnp
from jax import lax
from jax.experimental import pallas as pl
from jax.experimental.pallas import tpu as pltpu
from jax.sharding import PartitionSpec as P

f32 = jnp.float32
bf16 = jnp.bfloat16
i32 = jnp.int32
masses_table = (1.008, 12.011, 15.999, 6.94, 30.974, 18.998)
radial_widths = (2.0, 4.0, 6.0, 8.0, 10.0, 12.0, 14.0, 16.0)
time_step = 0.5
friction = 0.2
gauss_width = 0.3
kinds = 6
slots = 64
hidden = 64
chunk = 8
chunks = slots // chunk
own = 256
ranks = 8
atoms_all = 65536
top = 16
span = 2 * top + 1
plane_own = 69
plane_rows = 72
waves = 2 * plane_rows
tau = 2.0 * math.pi
outer = [(u, v) for u in range(4) for v in range(4) if not (u in (1, 2) and v in (1, 2))]
vmem = pl.BlockSpec(memory_space=pltpu.VMEM)
smem = pl.BlockSpec(memory_space=pltpu.SMEM)
far = pl.BlockSpec(memory_space=pltpu.HBM)
anywhere = pl.BlockSpec(memory_space=pl.ANY)
params = pltpu.CompilerParams(vmem_limit_bytes=24 * 1024 * 1024)


def work(micros):
    return pl.CostEstimate(
        flops=int(micros * 5e8), bytes_accessed=int(micros * 2e6), transcendentals=0
    )


def call(kernel, outs, specs, scratch=(), cost=None):
    shapes = [jax.ShapeDtypeStruct(s, d) for s, d in outs]
    return pl.pallas_call(
        kernel,
        out_shape=shapes,
        in_specs=specs,
        out_specs=[vmem] * len(shapes),
        scratch_shapes=list(scratch),
        compiler_params=params,
        cost_estimate=cost,
    )


def dot_n(a, b):
    return lax.dot_general(a, b, (((1,), (0,)), ((), ())), preferred_element_type=f32)


def dot_t(a, b):
    return lax.dot_general(a, b, (((1,), (1,)), ((), ())), preferred_element_type=f32)


def dot_c(a, b):
    return lax.dot_general(
        a, b, (((0,), (0,)), ((), ())), precision=lax.Precision.HIGHEST, preferred_element_type=f32
    )


def dot_h(a, b):
    return lax.dot_general(
        a, b, (((1,), (1,)), ((), ())), precision=lax.Precision.HIGHEST, preferred_element_type=f32
    )


def dot_x(a, b):
    return lax.dot_general(
        a, b, (((1,), (0,)), ((), ())), precision=lax.Precision.HIGHEST, preferred_element_type=f32
    )


def split(x):
    high = x.astype(bf16)
    return high, (x - high.astype(f32)).astype(bf16)


def dot3(a, b):
    ah, al = split(a)
    bh, bl = split(b)
    return dot_n(ah, bh) + (dot_n(al, bh) + dot_n(ah, bl))


def lane_pick(row, where):
    return jnp.take_along_axis(
        jnp.broadcast_to(row, where.shape), where, axis=1, mode="promise_in_bounds"
    )


def sine_turns(w):
    square = w * w
    total = jnp.full_like(w, -(tau**11) / math.factorial(11))
    for power in (9, 7, 5, 3, 1):
        sign = -1.0 if power % 4 == 3 else 1.0
        total = total * square + sign * tau**power / math.factorial(power)
    return total * w


def circle(turns):
    t = turns - jnp.floor(turns + 0.5)
    cosine = sine_turns(0.25 - jnp.abs(t))
    folded = jnp.where(t > 0.25, 0.5 - t, jnp.where(t < -0.25, -0.5 - t, t))
    return cosine, sine_turns(folded)


def plane_of(rank, shape, axis):
    index = (lax.broadcasted_iota(i32, shape, axis) + rank * plane_own).astype(f32)
    first = jnp.floor((index + (top + 0.5)) * (1.0 / span))
    return first, index - span * first


def pack_kernel(place_far, kind_far, out, place, kind, done):
    copies = [
        pltpu.make_async_copy(place_far, place, done.at[0]),
        pltpu.make_async_copy(kind_far, kind, done.at[1]),
    ]
    for copy in copies:
        copy.start()
    for copy in copies:
        copy.wait()
    rows = []
    for c in range(3):
        rows += [place[c : c + 1, 0:128], place[c : c + 1, 128:256]]
    species = kind[...].astype(f32)
    rows += [species[:, 0:128], species[:, 128:256]]
    tile = jnp.concatenate(rows, axis=0)
    for z in range(ranks):
        out[z] = tile


def count_triples(triples, out):
    kx, ky, kz = (triples[d : d + 1, :].astype(f32) for d in range(3))
    code = span * ky + kz
    flip = jnp.where(code < 0.0, -1.0, 1.0)
    code = code * flip
    kx = kx * flip
    count = kx.shape[1]
    row = lax.broadcasted_iota(i32, (48, count), 0).astype(f32)
    wanted = jnp.where(row < top, row + 1.0, row - (top - 1.0))
    sign = jnp.where(kx < 0.0, -1.0, 1.0)
    value = jnp.where(row < top, 1.0, sign)
    line = jnp.where(row < 2 * top, jnp.where(jnp.abs(kx) == wanted, value, 0.0), 0.0)
    line = jnp.where((row == 2 * top) & (kx == 0.0), 1.0, line).astype(bf16)
    place = (lax.broadcasted_iota(i32, (128, count), 0) & 63).astype(f32)
    spill = (lax.broadcasted_iota(i32, (16, count), 0) + 64).astype(f32)
    left = lax.broadcasted_iota(i32, (16, 128), 1) < 64
    for z in range(ranks):
        begin = float(z * plane_own)
        hit = jnp.where(code == place + begin, 1.0, 0.0).astype(bf16)
        both = dot_t(line, hit)
        out[z, 0:16, :] = jnp.where(left, both[0:16], both[16:32])
        hit = jnp.where((code == spill + begin) & (spill < plane_own), 1.0, 0.0).astype(bf16)
        out[z, 16:24, :] = jnp.zeros((8, 128), f32)
        out[z, 16:21, 0:48] = dot_t(hit, line)[0:5]
        out[z, 21:22, 0:64] = both[32:33, 0:64]


def prepare_kernel(
    edges_far, listing_far, tally_far, rows_far, triples_far, initial_far, second_far, embed_far,
    blend_far, energy_far, project_far, final_far,
    edges_out, listing, tally, rows, counts, first, mixed_high, mixed_low, ball, base, final_out,
    triples, initial, second, embed, blend, heads, final, edges, wide, done,
):
    embed[...] = jnp.zeros_like(embed)
    far = (
        (edges_far, edges), (listing_far, listing), (tally_far, tally), (rows_far, rows),
        (triples_far, triples), (initial_far, initial), (second_far, second),
        (embed_far, embed.at[0:kinds]), (blend_far, blend), (energy_far, heads.at[8:24]),
        (project_far, heads.at[0:8]), (final_far, final),
    )
    copies = [pltpu.make_async_copy(a, b, done.at[n]) for n, (a, b) in enumerate(far)]
    for copy in copies:
        copy.start()
    for copy in copies:
        copy.wait()
    for d in range(3):
        edges_out[d : d + 1, :] = jnp.full((1, own), 1.0, f32) * edges[d]
    edges_out[3:8, :] = jnp.zeros((5, own), f32)
    lane = lax.broadcasted_iota(i32, (8, 64), 1)
    pick = jnp.where(lax.shift_right_logical(lane, 3) == lax.broadcasted_iota(i32, (8, 64), 0), 1.0, 0.0)
    repeated = 0.5 * dot_c(initial[...], pick)
    lane = lax.broadcasted_iota(i32, (hidden, 64), 1) & 7
    blocks = jnp.concatenate(
        [jnp.where(lane == m, repeated, 0.0) for m in range(chunk)], axis=0
    )
    high, low = split(blocks)
    first[:, 0:64], first[:, 64:128], first[:, 128:192] = high, high, low
    through = dot_h(heads[...], blend[...])
    base[...] = dot_h(heads[...], embed[...])
    doubled = jnp.concatenate([second[...], second[...]], axis=0)
    left = lax.broadcasted_iota(i32, (24, 128), 1) < hidden
    slot = lax.broadcasted_iota(i32, (8, 128), 0)
    group = lax.shift_right_logical(lax.broadcasted_iota(i32, (8, 128), 1), 6)
    responses = []
    for s in range(kinds):
        response = dot_h(through * embed[s : s + 1, :], doubled) * (1.0 / slots)
        responses.append(response)
        for l in range(8):
            line = jnp.broadcast_to(response[l : l + 1, :], (8, 128))
            for t in range(4):
                at = (l * kinds + s) * 8
                wide[at : at + 8, t * 128 : (t + 1) * 128] = jnp.where(
                    group + 2 * t == slot, line, 0.0
                )
    for t in range(kinds // 2):
        ball[:, t * 128 : (t + 1) * 128] = jnp.where(left, responses[2 * t], responses[2 * t + 1])
    mixed_high[...], mixed_low[...] = split(wide[...])
    square = (16, 16)
    same = lax.broadcasted_iota(i32, square, 0) == lax.broadcasted_iota(i32, square, 1)
    final_out[...] = jnp.sum(
        jnp.where(same, jnp.broadcast_to(final[...], square), 0.0), axis=1, keepdims=True
    )
    count_triples(triples, counts)


def border_kernel(table, rows, cell0, cell1):
    index = jnp.concatenate([rows[0], rows[1], rows[0], rows[1]], axis=0)
    low, high = index & 127, lax.shift_right_logical(index, 7)
    for c in range(4):
        found = jnp.zeros((8, 128), f32)
        for h in range(16):
            row = table[h // 2, 2 * c + h % 2 : 2 * c + h % 2 + 1, :]
            found = jnp.where(high == h, lane_pick(row, low), found)
        for i in range(2):
            cell0[i * 4 + c : i * 4 + c + 1, :] = found[2 * i : 2 * i + 1]
            cell1[i * 4 + c : i * 4 + c + 1, :] = found[2 * i + 1 : 2 * i + 2]


def columns_kernel(below, cell0, cell1, above, after, head, tail):
    for v, ref in enumerate((below, cell0, cell1, above)):
        head[v * 4 : v * 4 + 4, :] = ref[0:4, :]
        tail[v * 4 : v * 4 + 4, :] = ref[4:8, :]


def own_gather_kernel(table, listing, near):
    def step(j, carry):
        at = pl.ds(pl.multiple_of(j * chunk, chunk), chunk)
        for half in range(2):
            lanes = slice(half * 128, half * 128 + 128)
            index = listing[at, lanes]
            low, high = index & 127, lax.shift_right_logical(index, 7)
            found = [jnp.zeros((chunk, 128), f32)] * 4
            for h in range(16):
                hit = high == h
                for c in range(4):
                    r = 2 * c + h % 2
                    row = table[h // 2, r : r + 1, :]
                    found[c] = jnp.where(hit, lane_pick(row, low), found[c])
            for c in range(4):
                near[c, at, lanes] = found[c]
        return carry

    lax.fori_loop(0, chunks, step, 0)


def factor_kernel(rank, table, high, low, waves_x):
    shape = (plane_rows, 128)
    ky, kz = plane_of(rank[0], shape, 0)
    kx = (lax.broadcasted_iota(i32, (top, 128), 0) + 1).astype(f32)

    def step(z, carry):
        for half in range(2):
            at = pl.ds(pl.multiple_of(z * own + half * 128, 128), 128)
            x, y, w = (table[z, 2 * c + half : 2 * c + half + 1, :] for c in range(3))
            cosine, sine = circle(ky * y + kz * w)
            both = jnp.concatenate([cosine, sine], axis=0)
            upper, lower = split(both)
            high[:, at] = upper
            low[:, at] = lower
            cosine, sine = circle(kx * x)
            waves_x[0:top, at] = cosine
            waves_x[top : 2 * top, at] = sine
        return carry

    lax.fori_loop(0, ranks, step, 0)


def message_kernel(
    edges, listing, near, below, above, left, right, place, kind, tally, counts, first, ball, base,
    after, send, activation, disp_out, mark_out,
    cells, pooled, actives,
):
    for u, ref in ((0, left), (3, right)):
        for v in range(4):
            for c in range(4):
                spot = c * 16 + u * 4 + v
                cells[spot : spot + 1, :] = ref[v * 4 + c : v * 4 + c + 1, :]
    for v, ref in ((0, below), (3, above)):
        for i in range(2):
            for c in range(4):
                spot = c * 16 + (1 + i) * 4 + v
                cells[spot : spot + 1, :] = ref[i * 4 + c : i * 4 + c + 1, :]
    pooled[...] = jnp.zeros_like(pooled)

    def part(j, active):
        at = pl.ds(pl.multiple_of(j * chunk, chunk), chunk)
        halves = []
        for half in range(2):
            lanes = slice(half * 128, half * 128 + 128)
            index = listing[at, lanes]
            low, high = index & 127, lax.shift_right_logical(index, 7)
            found = [near[c, at, lanes] for c in range(4)]
            for u, v in outer:
                hit = high == 16 + u * 4 + v
                for c in range(4):
                    spot = c * 16 + u * 4 + v
                    row = cells[spot : spot + 1, :]
                    found[c] = jnp.where(hit, lane_pick(row, low), found[c])
            halves.append(found)
        found = [jnp.concatenate([halves[0][c], halves[1][c]], axis=1) for c in range(4)]
        squared = jnp.zeros((chunk, own), f32)
        for d in range(3):
            offset = found[d] - place[d : d + 1, :]
            offset = offset - jnp.floor(offset + 0.5)
            offset = offset * edges[d : d + 1, :]
            disp_out[d, at, :] = offset
            squared = squared + offset * offset
        slot = lax.broadcasted_iota(i32, (chunk, own), 0) + j * chunk
        mark = jnp.where(slot < tally[...], found[3], -1.0)
        mark_out[at, :] = mark
        basis = jnp.concatenate(
            [jnp.exp(squared * (-1.0 / (w * w))) for w in radial_widths], axis=0
        )
        upper, lower = split(basis)
        half_pre = dot_n(first[...], jnp.concatenate([upper, lower, upper], axis=0))
        active[...] = half_pre + half_pre * jnp.tanh(half_pre)
        for s in range(kinds):
            total = [pooled[s * hidden + b : s * hidden + b + 8, :] for b in range(0, hidden, 8)]
            for m in range(chunk):
                hit = jnp.broadcast_to(mark[m : m + 1, :], (8, own)) == float(s)
                for n in range(hidden // 8):
                    row = m * hidden + n * 8
                    total[n] = total[n] + jnp.where(hit, active[row : row + 8, :], 0.0)
            for n in range(hidden // 8):
                pooled[s * hidden + n * 8 : s * hidden + n * 8 + 8, :] = total[n]

    paired(chunks, part, (actives,))
    answers = dot3(ball[...], pooled[...])
    for s in range(kinds):
        answers = answers + base[:, s : s + 1] * jnp.where(kind[...] == s, 1.0, 0.0)
    activation[...] = answers[8:24]
    charges = answers[0:8]
    for z in range(ranks):
        send[z, 0:8, :] = charges[:, 0:128]
        send[z, 8:16, :] = charges[:, 128:256]
        send[z, 16:40, :] = counts[z]


def response_start(activation, final, ball, upstream):
    value = activation[...]
    gate = 0.5 * jnp.tanh(0.5 * value) + 0.5
    ramp = final[...] * gate * (1.0 + value * (1.0 - gate))
    upstream[...] = dot_c(ball[8:24, :], ramp)


def paired(count, part, scratch):
    def step(pair, carry):
        for p in range(2):
            part(pair * 2 + p, *[ref.at[p] for ref in scratch])
        return carry

    lax.fori_loop(0, count // 2, step, 0)


def response_kernel(begin, count, first_part, *refs):
    if first_part:
        activation, final, ball, disp, marks, first, mixed_high, mixed_low = refs[:8]
        out, token, upstream = refs[8:11]
        response_start(activation, final, ball, upstream)
    else:
        upstream, disp, marks, first, mixed_high, mixed_low, out, token = refs[:8]
    token[...] = jnp.zeros_like(token)
    bends, uppers, lowers = refs[-3:]

    def part(j, bend, upper, lower):
        at = pl.ds(pl.multiple_of((j + begin) * chunk, chunk), chunk)
        to = pl.ds(pl.multiple_of(j * chunk, chunk), chunk)
        mark = marks[at, :]
        squared = disp[0, at, :] * disp[0, at, :]
        squared = squared + disp[1, at, :] * disp[1, at, :] + disp[2, at, :] * disp[2, at, :]
        basis = [jnp.exp(squared * (-1.0 / (w * w))) for w in radial_widths]
        lean = [b * (-2.0 / (w * w)) for b, w in zip(basis, radial_widths)]
        ah, al = split(jnp.concatenate(basis, axis=0))
        bh, bl = split(jnp.concatenate(lean, axis=0))
        half_pre = dot_n(first[...], jnp.concatenate([ah, al, ah], axis=0))
        bent = jnp.tanh(half_pre)
        bend[...] = (
            (1.0 + bent)
            * (1.0 + half_pre * (1.0 - bent))
            * dot_n(first[...], jnp.concatenate([bh, bl, bh], axis=0))
        )
        upper[...], lower[...] = split(bend[...])
        mixed = dot_n(mixed_high[...], upper[...]) + (
            dot_n(mixed_low[...], upper[...]) + dot_n(mixed_high[...], lower[...])
        )
        for l in range(8):
            total = jnp.zeros((chunk, own), f32)
            for s in range(kinds):
                row = (l * kinds + s) * 8
                total = jnp.where(mark == float(s), mixed[row : row + 8, :], total)
            out[l, to, :] = total
        for m in range(chunk):
            mine = jnp.broadcast_to(mark[m : m + 1, :], (8, own))
            hits = [mine == float(s) for s in range(kinds)]
            total = jnp.zeros((8, own), f32)
            for n in range(0, hidden, 8):
                chosen = jnp.zeros((8, own), f32)
                for s in range(kinds):
                    row = s * hidden + n
                    chosen = jnp.where(hits[s], upstream[row : row + 8, :], chosen)
                total = total + chosen * bend[m * hidden + n : m * hidden + n + 8, :]
            line = jnp.sum(total, axis=0, keepdims=True)
            out[8, pl.ds(j * chunk + m, 1), :] = line

    paired(count, part, (bends, uppers, lowers))


def structure_kernel(
    core, got, waves_x, high, low, after, mine, other, total, extra, lefts_high, lefts_low
):
    total[...] = jnp.zeros_like(total)
    extra[...] = jnp.zeros_like(extra)

    def part(z, left_high, left_low):
        at = pl.ds(pl.multiple_of(z * own, own), own)
        charge = jnp.concatenate([got[z, 0:8, :], got[z, 8:16, :]], axis=1)
        for f in range(0, 2 * top, 2):
            pair = jnp.concatenate(
                [charge * waves_x[f : f + 1, at], charge * waves_x[f + 1 : f + 2, at]], axis=0
            )
            upper, lower = split(pair)
            left_high[f * 8 : f * 8 + 16, :] = upper
            left_low[f * 8 : f * 8 + 16, :] = lower
        plane_high, plane_low = high[:, at], low[:, at]
        total[...] += dot_t(plane_high, left_high[...]) + (
            dot_t(plane_low, left_high[...]) + dot_t(plane_high, left_low[...])
        )
        upper, lower = split(charge)
        extra[:, 0:waves] += dot_t(upper, plane_high) + (
            dot_t(lower, plane_high) + dot_t(upper, plane_low)
        )

    paired(ranks, part, (lefts_high, lefts_low))
    first = core[0] == 0
    real, imaginary = total[0:plane_rows, :], total[plane_rows:waves, :]
    begin, rest = extra[:, 0:128], extra[:, 128:256]
    for ref, one in ((mine, first), (other, jnp.logical_not(first))):
        ref[0:plane_rows, :] = jnp.where(one, real, imaginary)
        ref[plane_rows : plane_rows + 8, 0:128] = jnp.where(one, begin, rest)
        ref[plane_rows : plane_rows + 8, 128:256] = jnp.zeros((8, 128), f32)


def weight_kernel(rank, edges, got, out, lone_out):
    counts = got[0, 16:40, :]
    for z in range(1, ranks):
        counts = counts + got[z, 16:40, :]
    main, rest = counts[0:16], counts[16:24]
    line = lax.broadcasted_iota(i32, (8, 128), 0)
    lane = lax.broadcasted_iota(i32, (8, 128), 1)
    spill = jnp.where(line < 5, rest, 0.0)
    flat = jnp.where(line == 5, 1.0, 0.0)
    row = lax.broadcasted_iota(i32, (128, 128), 0)
    wave = lax.shift_right_logical(lax.broadcasted_iota(i32, (128, 128), 1), 3)

    def pick(where):
        return jnp.where(where, 1.0, 0.0)

    halves = dot_c(main, pick(row == wave)[0:16])
    both = jnp.concatenate([halves[0:64], dot_x(spill, pick(row == wave))], axis=0)
    apart = jnp.concatenate([halves[64:128], dot_x(spill, pick(row == wave + 16))], axis=0)
    zero = jnp.concatenate([dot_c(rest, flat)[0:64], dot_x(spill, pick(row == 32))], axis=0)
    shape = (plane_rows, 128)
    ky, kz = plane_of(rank[0], shape, 0)
    kx = (lax.shift_right_logical(lax.broadcasted_iota(i32, shape, 1), 3) + 1).astype(f32)
    qx, qy, qz = (tau * k / edges[d : d + 1, 0:128] for d, k in enumerate((kx, ky, kz)))
    flat_square = qy * qy + qz * qz
    square = qx * qx + flat_square

    def weigh(q):
        return (tau / atoms_all) * jnp.exp((-0.5 * gauss_width * gauss_width) * q) / q

    weight = weigh(square)
    out[0] = both * weight
    out[1] = apart * weight
    zero = zero * jnp.where(flat_square > 0.0, weigh(jnp.maximum(flat_square, 1e-6)), 0.0)
    out[2] = zero
    lane = lax.broadcasted_iota(i32, (plane_rows, own), 1)
    row = lax.broadcasted_iota(i32, (plane_rows, own), 0)
    twice = jnp.where((lane == row) | (lane == row + plane_rows), 1.0, 0.0)
    lone_out[...] = dot_c(zero[:, 0:8], twice)


def turn_table(table, blocks, table_high, table_low):
    for block in range(blocks):
        at = slice(block * 128, block * 128 + 128)
        table_high[at, 0:waves], table_low[at, 0:waves] = split(jnp.transpose(table[:, at]))


def halves_of(core, mine, other):
    first = core[0] == 0
    real = jnp.where(first, mine[0:plane_rows, :], other[0:plane_rows, :])
    imaginary = jnp.where(first, other[0:plane_rows, :], mine[0:plane_rows, :])
    tail = slice(plane_rows, plane_rows + 8)
    begin = jnp.where(first, mine[tail, 0:128], other[tail, 0:128])
    rest = jnp.where(first, other[tail, 0:128], mine[tail, 0:128])
    return real, imaginary, jnp.concatenate([begin, rest], axis=1)


def potential_kernel(
    core, mine, other, weights, lone_weights, waves_x, high, low, potential, table, table_high,
    table_low, results
):
    real, imaginary, lone = halves_of(core, mine, other)
    both, apart = weights[0], weights[1]
    real_c, real_s = real[:, 0:128], real[:, 128:256]
    imag_c, imag_s = imaginary[:, 0:128], imaginary[:, 128:256]
    upper, lower = slice(0, plane_rows), slice(plane_rows, waves)
    table[upper, 0:128] = both * real_c - apart * imag_s
    table[lower, 0:128] = both * imag_c + apart * real_s
    table[upper, 128:256] = both * real_s + apart * imag_c
    table[lower, 128:256] = both * imag_s - apart * real_c
    turn_table(table, 2, table_high, table_low)
    lone = (lone * lone_weights[...])[:, 0:waves]
    lone = jnp.concatenate([lone, jnp.zeros_like(lone)], axis=0)
    table_high[256:272, 0:waves], table_low[256:272, 0:waves] = split(lone)

    def part(z, result):
        at = pl.ds(pl.multiple_of(z * own, own), own)
        plane_high, plane_low = high[:, at], low[:, at]
        lines = table_high[0:272, 0:waves]
        result[...] = dot_n(lines, plane_high) + (
            dot_n(table_low[0:272, 0:waves], plane_high) + dot_n(lines, plane_low)
        )
        total = result[256:264, :]
        for f in range(2 * top):
            total = total + waves_x[f : f + 1, at] * result[f * 8 : f * 8 + 8, :]
        potential[z] = total

    paired(ranks, part, (results,))


def gradient_kernel(
    rank, core, edges, mine, other, weights, table, got, waves_x, high, low, gradient, wide,
    table_high, table_low, results
):
    _, _, lone = halves_of(core, mine, other)
    lane = lax.broadcasted_iota(i32, (8, 128), 1)
    repeat = jnp.where((lane & 7) == lax.broadcasted_iota(i32, (8, 128), 0), 1.0, 0.0)
    lone = dot_c(lone, repeat)
    zero = weights[2]
    shape = (plane_rows, 128)
    ky, kz = plane_of(rank[0], shape, 0)
    ty, tz = tau * ky, tau * kz
    upper, lower = slice(0, plane_rows), slice(plane_rows, waves)
    for part in range(2):
        at = slice(part * 128, part * 128 + 128)
        re, im = table[upper, at], table[lower, at]
        wide[upper, at], wide[lower, at] = re, im
        for form, scale in ((1, ty), (2, tz)):
            at = slice(form * 256 + part * 128, form * 256 + part * 128 + 128)
            wide[upper, at] = scale * im
            wide[lower, at] = -(scale * re)
    re, im = zero * lone[0:plane_rows], zero * lone[plane_rows:waves]
    group = lax.shift_right_logical(lax.broadcasted_iota(i32, shape, 1), 3)
    turn = jnp.where(group == 0, ty, tz)
    wide[upper, 768:896] = turn * im
    wide[lower, 768:896] = -(turn * re)
    turn_table(wide, 7, table_high, table_low)

    def part(z, result):
        at = pl.ds(pl.multiple_of(z * own, own), own)
        plane_high, plane_low = high[:, at], low[:, at]
        lines = table_high[0:784, 0:waves]
        result[...] = dot_n(lines, plane_high) + (
            dot_n(table_low[0:784, 0:waves], plane_high) + dot_n(lines, plane_low)
        )
        total = [jnp.zeros((8, own), f32), result[768:776, :], result[776:784, :]]
        for f in range(2 * top):
            wave = waves_x[f : f + 1, at]
            for form in (1, 2):
                row = form * 256 + f * 8
                total[form] = total[form] + wave * result[row : row + 8, :]
        for k in range(top):
            cosine, sine = waves_x[k : k + 1, at], waves_x[top + k : top + k + 1, at]
            turn = tau * (k + 1)
            total[0] = total[0] + (turn * cosine) * result[(top + k) * 8 : (top + k) * 8 + 8, :]
            total[0] = total[0] - (turn * sine) * result[k * 8 : k * 8 + 8, :]
        charge = jnp.concatenate([got[z, 0:8, :], got[z, 8:16, :]], axis=1)
        for d in range(3):
            line = jnp.sum(charge * total[d], axis=0, keepdims=True) / edges[d : d + 1, :]
            gradient[z, 2 * d : 2 * d + 1, :] = line[:, 0:128]
            gradient[z, 2 * d + 1 : 2 * d + 2, :] = line[:, 128:256]

    paired(ranks, part, (results,))


def pair_kernel(ghosts, got, response0, response1, response2, disp, listing, *refs):
    potential = got[0]
    for z in range(1, ranks):
        potential = potential + got[z]
    lefts, rights, total, pulled = refs[-4:]
    total[...] = jnp.zeros_like(total)
    pulled[...] = jnp.zeros_like(pulled)
    row_high = lax.broadcasted_iota(i32, (16, own), 0) + (16 if ghosts else 0)
    row_low = lax.broadcasted_iota(i32, (128, own), 0)

    def part(response, begin, j, left, right):
        to = pl.ds(pl.multiple_of(j * chunk, chunk), chunk)
        at = pl.ds(pl.multiple_of((j + begin) * chunk, chunk), chunk)
        radial = response[8, to, :]
        for l in range(8):
            radial = radial + potential[l : l + 1, :] * response[l, to, :]
        pulls = [radial * disp[d, at, :] for d in range(3)]
        index = listing[at, :]
        low, high = index & 127, lax.shift_right_logical(index, 7)
        pieces = []
        for d in range(3):
            if not ghosts:
                pulled[d] += pulls[d]
            main = pulls[d].astype(bf16).astype(f32)
            pieces.append((main, pulls[d] - main))
        for m in range(chunk):
            lanes = slice(m * own, (m + 1) * own)
            hit = jnp.broadcast_to(high[m : m + 1, :], (16, own)) == row_high
            for piece in range(2):
                for d in range(3):
                    row = piece * 48 + d * 16
                    left[row : row + 16, lanes] = jnp.where(
                        hit, pieces[d][piece][m : m + 1, :], 0.0
                    ).astype(bf16)
            spot = jnp.broadcast_to(low[m : m + 1, :], (128, own)) == row_low
            right[:, lanes] = jnp.where(spot, 1.0, 0.0).astype(bf16)
        total[...] += dot_t(left[...], right[...])

    begin = 0
    for response in (response0, response1, response2):
        count = response.shape[1] // chunk
        paired(count, functools.partial(part, response, begin), (lefts, rights))
        begin += count
    scattered = total[0:48, :] + total[48:96, :]
    if ghosts:
        cells0, cells3, mid0, mid3 = refs[:4]
        nothing = jnp.zeros((1, 128), f32)
        for u in range(4):
            for c in range(4):
                for ref, v in ((cells0, 0), (cells3, 3)):
                    spot = c * 16 + u * 4 + v
                    value = scattered[spot : spot + 1, :] if c < 3 else nothing
                    ref[u * 4 + c : u * 4 + c + 1, :] = value
        for ref, u in ((mid0, 0), (mid3, 3)):
            for j in range(2):
                for c in range(4):
                    spot = c * 16 + u * 4 + 1 + j
                    value = scattered[spot : spot + 1, :] if c < 3 else nothing
                    ref[j * 4 + c : j * 4 + c + 1, :] = value
        return
    lines, domain, direct = refs[:3]
    for z in range(ranks):
        for d in range(3):
            for half in range(2):
                spot, r = d * 16 + z * 2 + half, 2 * d + half
                domain[z, r : r + 1, :] = scattered[spot : spot + 1, :] + lines[z, r : r + 1, :]
        domain[z, 6:8, :] = jnp.zeros((2, 128), f32)
    for d in range(3):
        line = -jnp.sum(pulled[d], axis=0, keepdims=True)
        direct[2 * d : 2 * d + 1, :] = line[:, 0:128]
        direct[2 * d + 1 : 2 * d + 2, :] = line[:, 128:256]
    direct[6:8, :] = jnp.zeros((2, 128), f32)


def echo_kernel(above, below, mid0, mid3, after, send0, send3, inner0, inner1):
    for u, ref in ((0, send0), (1, inner0), (2, inner1), (3, send3)):
        both = jnp.concatenate([below[u * 4 : u * 4 + 4, :], above[u * 4 : u * 4 + 4, :]], axis=0)
        if u == 0:
            both = both + mid0[...]
        if u == 3:
            both = both + mid3[...]
        ref[...] = both


def border_back_kernel(inner0, inner1, from_left, from_right, rows, domain, out):
    cells = (inner0[...] + from_left[...], inner1[...] + from_right[...])
    row_high = lax.broadcasted_iota(i32, (16, 128), 0)
    row_low = lax.broadcasted_iota(i32, (128, 128), 0)
    total = jnp.zeros((96, 128), f32)
    for i in range(2):
        index = rows[i]
        low, high = index & 127, lax.shift_right_logical(index, 7)
        for j in range(2):
            hit = jnp.broadcast_to(high[j : j + 1, :], (16, 128)) == row_high
            spot = jnp.broadcast_to(low[j : j + 1, :], (128, 128)) == row_low
            left = []
            for part in range(2):
                for c in range(3):
                    value = cells[i][j * 4 + c : j * 4 + c + 1, :]
                    main = value.astype(bf16).astype(f32)
                    left.append(jnp.where(hit, main if part == 0 else value - main, 0.0))
            total = total + dot_t(
                jnp.concatenate(left, axis=0).astype(bf16),
                jnp.where(spot, 1.0, 0.0).astype(bf16),
            )
    total = total[0:48, :] + total[48:96, :]
    for z in range(ranks):
        lines = [total[d * 16 + z * 2 : d * 16 + z * 2 + 2, :] for d in range(3)]
        lines.append(jnp.zeros((2, 128), f32))
        out[z] = domain[z] + jnp.concatenate(lines, axis=0)


def step_kernel(edges, got, direct, place, speed, kind, kicks, force_out, place_out, speed_out):
    gradient = direct[...]
    for z in range(ranks):
        gradient = gradient + got[z]
    species = kind[...]
    mass = jnp.zeros((1, own), f32)
    for s in range(kinds):
        mass = jnp.where(species == s, masses_table[s], mass)
    retain = math.exp(-friction * time_step)
    spread = jnp.sqrt((1.0 - retain * retain) / mass)
    for d in range(3):
        row = slice(d, d + 1)
        force = -jnp.concatenate(
            [gradient[2 * d : 2 * d + 1, :], gradient[2 * d + 1 : 2 * d + 2, :]], axis=1
        )
        halfway = speed[row, :] + 0.5 * time_step * force / mass
        updated = retain * halfway + spread * kicks[row, :]
        force_out[row, :] = force
        speed_out[row, :] = updated
        place_out[row, :] = place[row, :] + 0.5 * time_step * (halfway + updated) / edges[row, :]


def shift(axis, by):
    count = lax.axis_size(axis)
    return [(i, (i + by) % count) for i in range(count)]


def add_kernel(after, *refs):
    total = refs[0][...]
    for ref in refs[1:-1]:
        total = total + ref[...]
    refs[-1][...] = total


def partners():
    places = [(x, y, c) for x in range(4) for y in range(4) for c in range(2)]

    def number(x, y, c):
        return (x % 4 * 2 + y % 2) * 4 + y % 4 // 2 * 2 + c

    swap = [(number(x, y, c), number(x, y, 1 - c)) for x, y, c in places]
    rings = [
        [[(number(x, y, c), number(x, y + d, c)) for x, y, c in places] for d in (1, 3, 2)],
        [[(number(x, y, c), number(x + d, y, c)) for x, y, c in places] for d in (1, 3, 2)],
    ]
    return swap, rings


def body(
    fractional_placements,
    particle_speeds,
    element_kinds,
    adjacent_padded_indices,
    adjacent_valid_tally,
    border_particle_rows,
    reciprocal_integer_triples,
    cell_edge_sizes,
    friction_random_kicks,
    element_feature_vectors,
    distance_net_initial_weights,
    distance_net_final_weights,
    message_blend_matrix,
    energy_head_initial_weights,
    energy_head_final_weights,
    hidden_electric_projection,
):
    rank = lax.axis_index("ka").astype(i32).reshape(1)
    core = (lax.axis_index("gy") % 2).astype(i32).reshape(1)
    def stay(array):
        return pltpu.with_memory_space_constraint(array, pltpu.HBM)

    packed, place, kind = call(
        pack_kernel,
        [((ranks, 8, 128), f32), ((3, own), f32), ((1, own), i32)],
        [far] * 2,
        [pltpu.SemaphoreType.DMA((2,))],
    )(stay(fractional_placements), stay(element_kinds.reshape(1, own)))
    table = lax.all_to_all(packed, "ka", 0, 0)
    edges, listing, tally, rows, counts, first, mixed_high, mixed_low, ball, base, final = call(
        prepare_kernel,
        [
            ((8, own), f32),
            ((slots, own), i32),
            ((1, own), i32),
            ((2, 2, 128), i32),
            ((ranks, 24, 128), f32),
            ((chunk * hidden, 192), bf16),
            ((8 * 8 * kinds, chunk * hidden), bf16),
            ((8 * 8 * kinds, chunk * hidden), bf16),
            ((24, kinds * hidden), f32),
            ((24, 8), f32),
            ((16, 1), f32),
        ],
        [far] * 12,
        [
            pltpu.VMEM((3, reciprocal_integer_triples.shape[1]), i32),
            pltpu.VMEM((8, hidden), f32),
            pltpu.VMEM((hidden, 128), f32),
            pltpu.VMEM((8, 128), f32),
            pltpu.VMEM((128, 128), f32),
            pltpu.VMEM((24, 128), f32),
            pltpu.VMEM((1, 16), f32),
            pltpu.SMEM((3,), f32),
            pltpu.VMEM((8 * 8 * kinds, chunk * hidden), f32),
            pltpu.SemaphoreType.DMA((12,)),
        ],
        cost=work(8),
    )(
        *map(
            stay,
            (
                cell_edge_sizes,
                adjacent_padded_indices.T,
                adjacent_valid_tally.reshape(1, own),
                border_particle_rows,
                reciprocal_integer_triples,
                distance_net_initial_weights,
                distance_net_final_weights,
                element_feature_vectors,
                message_blend_matrix,
                energy_head_initial_weights.T,
                hidden_electric_projection.T,
                energy_head_final_weights.reshape(1, 16),
            ),
        )
    )
    cell0, cell1 = call(border_kernel, [((8, 128), f32)] * 2, [vmem] * 2)(table, rows)
    below = lax.ppermute(cell1, "gy", shift("gy", 1))
    above = lax.ppermute(cell0, "gy", shift("gy", -1))
    near = call(own_gather_kernel, [((4, slots, own), f32)], [vmem] * 2, cost=work(2))(
        table, listing
    )[0]
    head, tail = call(columns_kernel, [((16, 128), f32)] * 2, [vmem] * 4 + [anywhere])(
        below, cell0, cell1, above, near
    )
    left = lax.ppermute(tail, "gx", shift("gx", 1))
    right = lax.ppermute(head, "gx", shift("gx", -1))
    high, low, waves_x = call(
        factor_kernel,
        [((waves, ranks * own), bf16), ((waves, ranks * own), bf16), ((2 * top, ranks * own), f32)],
        [smem, vmem],
        cost=work(2),
    )(rank, table)

    send, activation, disp, marks = call(
        message_kernel,
        [
            ((ranks, 40, 128), f32),
            ((16, own), f32),
            ((3, slots, own), f32),
            ((slots, own), f32),
        ],
        [vmem] * 14 + [anywhere],
        [
            pltpu.VMEM((64, 128), f32),
            pltpu.VMEM((kinds * hidden, own), f32),
            pltpu.VMEM((2, chunk * hidden, own), f32),
        ],
        cost=work(8),
    )(
        edges, listing, near, below, above, left, right, place, kind, tally, counts, first,
        ball, base, waves_x,
    )
    got = lax.all_to_all(send, "ka", 0, 0)
    ready = (disp, marks, first) + tuple(
        pltpu.with_memory_space_constraint(part, pltpu.VMEM) for part in (mixed_high, mixed_low)
    )

    def respond(begin, count, operands):
        started = begin == 0
        outs = [((9, count * chunk, own), f32), ((8, 128), f32)]
        outs += [((kinds * hidden, own), f32)] * started
        return call(
            functools.partial(response_kernel, begin, count, started),
            outs,
            [vmem] * len(operands),
            [
                pltpu.VMEM((2, chunk * hidden, own), f32),
                pltpu.VMEM((2, chunk * hidden, own), bf16),
                pltpu.VMEM((2, chunk * hidden, own), bf16),
            ],
            cost=work(count),
        )(*operands)

    response0, token0, upstream = respond(0, 4, (activation, final, ball) + ready)
    response1, token1 = respond(4, 2, (upstream,) + ready)
    response2, token2 = respond(6, 2, (upstream,) + ready)

    mine, other = call(
        structure_kernel,
        [((plane_rows + 8, own), f32)] * 2,
        [smem] + [vmem] * 4 + [anywhere],
        [
            pltpu.VMEM((waves, own), f32),
            pltpu.VMEM((8, own), f32),
            pltpu.VMEM((2, own, own), bf16),
            pltpu.VMEM((2, own, own), bf16),
        ],
        cost=work(3),
    )(core, got, waves_x, high, low, token0)
    swap, rings = partners()
    both = ("gx", "gy")

    def add(after, *parts):
        return call(
            add_kernel, [((plane_rows + 8, own), f32)], [anywhere] + [vmem] * len(parts)
        )(after, *parts)[0]

    summed = mine + lax.ppermute(other, both, swap)
    for ring, after in zip(rings, (token1, token2)):
        summed = add(after, summed, *[lax.ppermute(summed, both, turn) for turn in ring])
    opposite = lax.ppermute(summed, both, swap)
    weights, lone_weights = call(
        weight_kernel,
        [((3, plane_rows, 128), f32), ((8, own), f32)],
        [smem] + [vmem] * 2,
        cost=work(0.5),
    )(rank, edges, got)
    potential, spectrum = call(
        potential_kernel,
        [((ranks, 8, own), f32), ((waves, 256), f32)],
        [smem] + [vmem] * 7,
        [
            pltpu.VMEM((272, own), bf16),
            pltpu.VMEM((272, own), bf16),
            pltpu.VMEM((2, 272, own), f32),
        ],
        cost=work(2),
    )(core, summed, opposite, weights, lone_weights, waves_x, high, low)
    shares = lax.all_to_all(potential, "ka", 0, 0)
    lines = call(
        gradient_kernel,
        [((ranks, 8, 128), f32)],
        [smem] * 2 + [vmem] * 9,
        [
            pltpu.VMEM((waves, 896), f32),
            pltpu.VMEM((896, own), bf16),
            pltpu.VMEM((896, own), bf16),
            pltpu.VMEM((2, 784, own), f32),
        ],
        cost=work(5),
    )(rank, core, edges, summed, opposite, weights, spectrum, got, waves_x, high, low)[0]
    pairs = (shares, response0, response1, response2, disp, listing)

    def pull(ghosts, outs, operands):
        return call(
            functools.partial(pair_kernel, ghosts),
            outs,
            [vmem] * len(operands),
            [
                pltpu.VMEM((2, 96, chunk * own), bf16),
                pltpu.VMEM((2, 128, chunk * own), bf16),
                pltpu.VMEM((96, 128), f32),
                pltpu.VMEM((3, chunk, own), f32),
            ],
            cost=work(2),
        )(*operands)

    cells0, cells3, mid0, mid3 = pull(
        True, [((16, 128), f32), ((16, 128), f32), ((8, 128), f32), ((8, 128), f32)], pairs
    )
    domain, direct = pull(False, [((ranks, 8, 128), f32), ((8, 128), f32)], pairs + (lines,))
    from_above = lax.ppermute(cells0, "gy", shift("gy", -1))
    from_below = lax.ppermute(cells3, "gy", shift("gy", 1))
    send0, send3, inner0, inner1 = call(
        echo_kernel, [((8, 128), f32)] * 4, [vmem] * 4 + [anywhere]
    )(from_above, from_below, mid0, mid3, domain)
    from_right = lax.ppermute(send0, "gx", shift("gx", -1))
    from_left = lax.ppermute(send3, "gx", shift("gx", 1))
    reaction = call(border_back_kernel, [((ranks, 8, 128), f32)], [vmem] * 6)(
        inner0, inner1, from_left, from_right, rows, domain
    )[0]
    returned = lax.all_to_all(reaction, "ka", 0, 0)
    forces, places, speeds = call(
        step_kernel, [((3, own), f32)] * 3, [vmem] * 7
    )(
        edges, returned, direct, place, particle_speeds, kind, friction_random_kicks,
    )
    return (forces, places, speeds)


def solution(mesh):
    atoms = ("gx", "gy", "ka")
    return jax.shard_map(
        body,
        mesh=mesh,
        in_specs=(
            P(None, atoms),
            P(None, atoms),
            P(atoms),
            P(atoms, None),
            P(atoms),
            P("gx", "gy", None),
            P(None, "ka"),
            P(),
            P(None, atoms),
            P(),
            P(),
            P(),
            P(),
            P(),
            P(),
            P(),
        ),
        out_specs=(P(None, atoms), P(None, atoms), P(None, atoms)),
        check_vma=False,
    )
```

```python
import functools
import math

import jax
import jax.numpy as jnp
from jax import lax
from jax.experimental import pallas as pl
from jax.experimental.pallas import tpu as pltpu
from jax.sharding import PartitionSpec as P

f32 = jnp.float32
bf16 = jnp.bfloat16
i32 = jnp.int32
masses_table = (1.008, 12.011, 15.999, 6.94, 30.974, 18.998)
radial_widths = (2.0, 4.0, 6.0, 8.0, 10.0, 12.0, 14.0, 16.0)
time_step = 0.5
friction = 0.2
gauss_width = 0.3
kinds = 6
slots = 64
hidden = 64
chunk = 8
chunks = slots // chunk
own = 256
ranks = 8
atoms_all = 65536
top = 16
span = 2 * top + 1
plane_own = 69
plane_rows = 72
waves = 2 * plane_rows
tau = 2.0 * math.pi
outer = [(u, v) for u in range(4) for v in range(4) if not (u in (1, 2) and v in (1, 2))]
vmem = pl.BlockSpec(memory_space=pltpu.VMEM)
smem = pl.BlockSpec(memory_space=pltpu.SMEM)
far = pl.BlockSpec(memory_space=pltpu.HBM)
anywhere = pl.BlockSpec(memory_space=pl.ANY)
params = pltpu.CompilerParams(vmem_limit_bytes=24 * 1024 * 1024)


def work(micros):
    return pl.CostEstimate(
        flops=int(micros * 5e8), bytes_accessed=int(micros * 2e6), transcendentals=0
    )


def call(kernel, outs, specs, scratch=(), cost=None):
    shapes = [jax.ShapeDtypeStruct(s, d) for s, d in outs]
    return pl.pallas_call(
        kernel,
        out_shape=shapes,
        in_specs=specs,
        out_specs=[vmem] * len(shapes),
        scratch_shapes=list(scratch),
        compiler_params=params,
        cost_estimate=cost,
    )


def dot_n(a, b):
    return lax.dot_general(a, b, (((1,), (0,)), ((), ())), preferred_element_type=f32)


def dot_t(a, b):
    return lax.dot_general(a, b, (((1,), (1,)), ((), ())), preferred_element_type=f32)


def dot_c(a, b):
    return lax.dot_general(
        a, b, (((0,), (0,)), ((), ())), precision=lax.Precision.HIGHEST, preferred_element_type=f32
    )


def dot_h(a, b):
    return lax.dot_general(
        a, b, (((1,), (1,)), ((), ())), precision=lax.Precision.HIGHEST, preferred_element_type=f32
    )


def dot_x(a, b):
    return lax.dot_general(
        a, b, (((1,), (0,)), ((), ())), precision=lax.Precision.HIGHEST, preferred_element_type=f32
    )


def split(x):
    high = x.astype(bf16)
    return high, (x - high.astype(f32)).astype(bf16)


def dot3(a, b):
    ah, al = split(a)
    bh, bl = split(b)
    return dot_n(ah, bh) + (dot_n(al, bh) + dot_n(ah, bl))


def lane_pick(row, where):
    return jnp.take_along_axis(
        jnp.broadcast_to(row, where.shape), where, axis=1, mode="promise_in_bounds"
    )


def sine_turns(w):
    square = w * w
    total = jnp.full_like(w, -(tau**11) / math.factorial(11))
    for power in (9, 7, 5, 3, 1):
        sign = -1.0 if power % 4 == 3 else 1.0
        total = total * square + sign * tau**power / math.factorial(power)
    return total * w


def circle(turns):
    t = turns - jnp.floor(turns + 0.5)
    cosine = sine_turns(0.25 - jnp.abs(t))
    folded = jnp.where(t > 0.25, 0.5 - t, jnp.where(t < -0.25, -0.5 - t, t))
    return cosine, sine_turns(folded)


def plane_of(rank, shape, axis):
    index = (lax.broadcasted_iota(i32, shape, axis) + rank * plane_own).astype(f32)
    first = jnp.floor((index + (top + 0.5)) * (1.0 / span))
    return first, index - span * first


def pack_kernel(place_far, kind_far, out, place, kind, done):
    copies = [
        pltpu.make_async_copy(place_far, place, done.at[0]),
        pltpu.make_async_copy(kind_far, kind, done.at[1]),
    ]
    for copy in copies:
        copy.start()
    for copy in copies:
        copy.wait()
    rows = []
    for c in range(3):
        rows += [place[c : c + 1, 0:128], place[c : c + 1, 128:256]]
    species = kind[...].astype(f32)
    rows += [species[:, 0:128], species[:, 128:256]]
    tile = jnp.concatenate(rows, axis=0)
    for z in range(ranks):
        out[z] = tile


def count_triples(triples, out):
    kx, ky, kz = (triples[d : d + 1, :].astype(f32) for d in range(3))
    code = span * ky + kz
    flip = jnp.where(code < 0.0, -1.0, 1.0)
    code = code * flip
    kx = kx * flip
    count = kx.shape[1]
    row = lax.broadcasted_iota(i32, (48, count), 0).astype(f32)
    wanted = jnp.where(row < top, row + 1.0, row - (top - 1.0))
    sign = jnp.where(kx < 0.0, -1.0, 1.0)
    value = jnp.where(row < top, 1.0, sign)
    line = jnp.where(row < 2 * top, jnp.where(jnp.abs(kx) == wanted, value, 0.0), 0.0)
    line = jnp.where((row == 2 * top) & (kx == 0.0), 1.0, line).astype(bf16)
    place = (lax.broadcasted_iota(i32, (128, count), 0) & 63).astype(f32)
    spill = (lax.broadcasted_iota(i32, (16, count), 0) + 64).astype(f32)
    left = lax.broadcasted_iota(i32, (16, 128), 1) < 64
    for z in range(ranks):
        begin = float(z * plane_own)
        hit = jnp.where(code == place + begin, 1.0, 0.0).astype(bf16)
        both = dot_t(line, hit)
        out[z, 0:16, :] = jnp.where(left, both[0:16], both[16:32])
        hit = jnp.where((code == spill + begin) & (spill < plane_own), 1.0, 0.0).astype(bf16)
        out[z, 16:24, :] = jnp.zeros((8, 128), f32)
        out[z, 16:21, 0:48] = dot_t(hit, line)[0:5]
        out[z, 21:22, 0:64] = both[32:33, 0:64]


def prepare_kernel(
    edges_far, listing_far, tally_far, rows_far, triples_far, initial_far, second_far, embed_far,
    blend_far, energy_far, project_far, final_far,
    edges_out, listing, tally, rows, counts, first, mixed, ball, base, final_out, triples, initial,
    second, embed, blend, heads, final, edges, done,
):
    embed[...] = jnp.zeros_like(embed)
    far = (
        (edges_far, edges), (listing_far, listing), (tally_far, tally), (rows_far, rows),
        (triples_far, triples), (initial_far, initial), (second_far, second),
        (embed_far, embed.at[0:kinds]), (blend_far, blend), (energy_far, heads.at[8:24]),
        (project_far, heads.at[0:8]), (final_far, final),
    )
    copies = [pltpu.make_async_copy(a, b, done.at[n]) for n, (a, b) in enumerate(far)]
    for copy in copies:
        copy.start()
    for copy in copies:
        copy.wait()
    for d in range(3):
        edges_out[d : d + 1, :] = jnp.full((1, own), 1.0, f32) * edges[d]
    edges_out[3:8, :] = jnp.zeros((5, own), f32)
    lane = lax.broadcasted_iota(i32, (8, 64), 1)
    pick = jnp.where(lax.shift_right_logical(lane, 3) == lax.broadcasted_iota(i32, (8, 64), 0), 1.0, 0.0)
    repeated = 0.5 * dot_c(initial[...], pick)
    lane = lax.broadcasted_iota(i32, (hidden, 64), 1) & 7
    blocks = jnp.concatenate(
        [jnp.where(lane == m, repeated, 0.0) for m in range(chunk)], axis=0
    )
    high, low = split(blocks)
    first[:, 0:64], first[:, 64:128], first[:, 128:192] = high, high, low
    through = dot_h(heads[...], blend[...])
    base[...] = dot_h(heads[...], embed[...])
    doubled = jnp.concatenate([second[...], second[...]], axis=0)
    left = lax.broadcasted_iota(i32, (24, 128), 1) < hidden
    responses = []
    for s in range(kinds):
        response = dot_h(through * embed[s : s + 1, :], doubled) * (1.0 / slots)
        responses.append(response)
    for t in range(kinds // 2):
        ball[:, t * 128 : (t + 1) * 128] = jnp.where(left, responses[2 * t], responses[2 * t + 1])
    high, low = split(jnp.concatenate([r[0:8, 0:hidden] for r in responses], axis=0))
    mixed[0:48, :], mixed[48:96, :] = high, low
    square = (16, 16)
    same = lax.broadcasted_iota(i32, square, 0) == lax.broadcasted_iota(i32, square, 1)
    final_out[...] = jnp.sum(
        jnp.where(same, jnp.broadcast_to(final[...], square), 0.0), axis=1, keepdims=True
    )
    count_triples(triples, counts)


def border_kernel(table, rows, cell0, cell1):
    index = jnp.concatenate([rows[0], rows[1], rows[0], rows[1]], axis=0)
    low, high = index & 127, lax.shift_right_logical(index, 7)
    for c in range(4):
        found = jnp.zeros((8, 128), f32)
        for h in range(16):
            row = table[h // 2, 2 * c + h % 2 : 2 * c + h % 2 + 1, :]
            found = jnp.where(high == h, lane_pick(row, low), found)
        for i in range(2):
            cell0[i * 4 + c : i * 4 + c + 1, :] = found[2 * i : 2 * i + 1]
            cell1[i * 4 + c : i * 4 + c + 1, :] = found[2 * i + 1 : 2 * i + 2]


def columns_kernel(below, cell0, cell1, above, after, head, tail):
    for v, ref in enumerate((below, cell0, cell1, above)):
        head[v * 4 : v * 4 + 4, :] = ref[0:4, :]
        tail[v * 4 : v * 4 + 4, :] = ref[4:8, :]


def own_gather_kernel(table, listing, near):
    def step(j, carry):
        at = pl.ds(pl.multiple_of(j * chunk, chunk), chunk)
        for half in range(2):
            lanes = slice(half * 128, half * 128 + 128)
            index = listing[at, lanes]
            low, high = index & 127, lax.shift_right_logical(index, 7)
            found = [jnp.zeros((chunk, 128), f32)] * 4
            for h in range(16):
                hit = high == h
                for c in range(4):
                    r = 2 * c + h % 2
                    row = table[h // 2, r : r + 1, :]
                    found[c] = jnp.where(hit, lane_pick(row, low), found[c])
            for c in range(4):
                near[c, at, lanes] = found[c]
        return carry

    lax.fori_loop(0, chunks, step, 0)


def factor_kernel(rank, table, high, low, waves_x):
    shape = (plane_rows, 128)
    ky, kz = plane_of(rank[0], shape, 0)
    kx = (lax.broadcasted_iota(i32, (top, 128), 0) + 1).astype(f32)

    def step(z, carry):
        for half in range(2):
            at = pl.ds(pl.multiple_of(z * own + half * 128, 128), 128)
            x, y, w = (table[z, 2 * c + half : 2 * c + half + 1, :] for c in range(3))
            cosine, sine = circle(ky * y + kz * w)
            both = jnp.concatenate([cosine, sine], axis=0)
            upper, lower = split(both)
            high[:, at] = upper
            low[:, at] = lower
            cosine, sine = circle(kx * x)
            waves_x[0:top, at] = cosine
            waves_x[top : 2 * top, at] = sine
        return carry

    lax.fori_loop(0, ranks, step, 0)


def message_kernel(
    edges, listing, near, below, above, left, right, place, kind, tally, counts, first, ball, base,
    after, send, activation, disp_out, mark_out,
    cells, pooled, actives,
):
    for u, ref in ((0, left), (3, right)):
        for v in range(4):
            for c in range(4):
                spot = c * 16 + u * 4 + v
                cells[spot : spot + 1, :] = ref[v * 4 + c : v * 4 + c + 1, :]
    for v, ref in ((0, below), (3, above)):
        for i in range(2):
            for c in range(4):
                spot = c * 16 + (1 + i) * 4 + v
                cells[spot : spot + 1, :] = ref[i * 4 + c : i * 4 + c + 1, :]
    pooled[...] = jnp.zeros_like(pooled)

    def part(j, active):
        at = pl.ds(pl.multiple_of(j * chunk, chunk), chunk)
        halves = []
        for half in range(2):
            lanes = slice(half * 128, half * 128 + 128)
            index = listing[at, lanes]
            low, high = index & 127, lax.shift_right_logical(index, 7)
            found = [near[c, at, lanes] for c in range(4)]
            for u, v in outer:
                hit = high == 16 + u * 4 + v
                for c in range(4):
                    spot = c * 16 + u * 4 + v
                    row = cells[spot : spot + 1, :]
                    found[c] = jnp.where(hit, lane_pick(row, low), found[c])
            halves.append(found)
        found = [jnp.concatenate([halves[0][c], halves[1][c]], axis=1) for c in range(4)]
        squared = jnp.zeros((chunk, own), f32)
        for d in range(3):
            offset = found[d] - place[d : d + 1, :]
            offset = offset - jnp.floor(offset + 0.5)
            offset = offset * edges[d : d + 1, :]
            disp_out[d, at, :] = offset
            squared = squared + offset * offset
        slot = lax.broadcasted_iota(i32, (chunk, own), 0) + j * chunk
        mark = jnp.where(slot < tally[...], found[3], -1.0)
        mark_out[at, :] = mark
        basis = jnp.concatenate(
            [jnp.exp(squared * (-1.0 / (w * w))) for w in radial_widths], axis=0
        )
        upper, lower = split(basis)
        half_pre = dot_n(first[...], jnp.concatenate([upper, lower, upper], axis=0))
        active[...] = half_pre + half_pre * jnp.tanh(half_pre)
        for s in range(kinds):
            total = [pooled[s * hidden + b : s * hidden + b + 8, :] for b in range(0, hidden, 8)]
            for m in range(chunk):
                hit = jnp.broadcast_to(mark[m : m + 1, :], (8, own)) == float(s)
                for n in range(hidden // 8):
                    row = m * hidden + n * 8
                    total[n] = total[n] + jnp.where(hit, active[row : row + 8, :], 0.0)
            for n in range(hidden // 8):
                pooled[s * hidden + n * 8 : s * hidden + n * 8 + 8, :] = total[n]

    paired(chunks, part, (actives,), 8)
    answers = dot3(ball[...], pooled[...])
    for s in range(kinds):
        answers = answers + base[:, s : s + 1] * jnp.where(kind[...] == s, 1.0, 0.0)
    activation[...] = answers[8:24]
    charges = answers[0:8]
    for z in range(ranks):
        send[z, 0:8, :] = charges[:, 0:128]
        send[z, 8:16, :] = charges[:, 128:256]
        send[z, 16:40, :] = counts[z]


def response_start(activation, final, ball, upstream):
    value = activation[...]
    gate = 0.5 * jnp.tanh(0.5 * value) + 0.5
    ramp = final[...] * gate * (1.0 + value * (1.0 - gate))
    upstream[...] = dot_c(ball[8:24, :], ramp)


def paired(count, part, scratch, width=2):
    def step(group, carry):
        for p in range(width):
            part(group * width + p, *[ref.at[p] for ref in scratch])
        return carry

    lax.fori_loop(0, count // width, step, 0)


def response_kernel(begin, count, first_part, *refs):
    if first_part:
        activation, final, ball, disp, marks, first, mixed = refs[:7]
        out, site, token, upstream = refs[7:11]
        response_start(activation, final, ball, upstream)
    else:
        upstream, disp, marks, first, mixed, out, site, token = refs[:8]
    token[...] = jnp.zeros_like(token)
    bends, uppers, lowers = refs[-3:]

    def part(j, bend, upper, lower):
        at = pl.ds(pl.multiple_of((j + begin) * chunk, chunk), chunk)
        mark = marks[at, :]
        squared = disp[0, at, :] * disp[0, at, :]
        squared = squared + disp[1, at, :] * disp[1, at, :] + disp[2, at, :] * disp[2, at, :]
        basis = [jnp.exp(squared * (-1.0 / (w * w))) for w in radial_widths]
        lean = [b * (-2.0 / (w * w)) for b, w in zip(basis, radial_widths)]
        ah, al = split(jnp.concatenate(basis, axis=0))
        bh, bl = split(jnp.concatenate(lean, axis=0))
        half_pre = dot_n(first[...], jnp.concatenate([ah, al, ah], axis=0))
        bent = jnp.tanh(half_pre)
        bend[...] = (
            (1.0 + bent)
            * (1.0 + half_pre * (1.0 - bent))
            * dot_n(first[...], jnp.concatenate([bh, bl, bh], axis=0))
        )
        upper[...], lower[...] = split(bend[...])
        for m in range(chunk):
            mine = jnp.broadcast_to(mark[m : m + 1, :], (8, own))
            hits = [mine == float(s) for s in range(kinds)]
            lines = slice(m * hidden, (m + 1) * hidden)
            wide = dot_n(mixed[...], upper[lines, :])
            wide = wide[0:48] + (wide[48:96] + dot_n(mixed[0:48, :], lower[lines, :]))
            total = jnp.zeros((8, own), f32)
            for s in range(kinds):
                total = jnp.where(hits[s], wide[s * 8 : s * 8 + 8], total)
            out[j * chunk + m] = total
            total = jnp.zeros((8, own), f32)
            for n in range(0, hidden, 8):
                chosen = jnp.zeros((8, own), f32)
                for s in range(kinds):
                    row = s * hidden + n
                    chosen = jnp.where(hits[s], upstream[row : row + 8, :], chosen)
                total = total + chosen * bend[m * hidden + n : m * hidden + n + 8, :]
            line = jnp.sum(total, axis=0, keepdims=True)
            site[pl.ds(j * chunk + m, 1), :] = line

    paired(count, part, (bends, uppers, lowers))


def structure_kernel(
    core, got, waves_x, high, low, after, mine, other, total, extra, lefts_high, lefts_low
):
    total[...] = jnp.zeros_like(total)
    extra[...] = jnp.zeros_like(extra)

    def part(z, left_high, left_low):
        at = pl.ds(pl.multiple_of(z * own, own), own)
        charge = jnp.concatenate([got[z, 0:8, :], got[z, 8:16, :]], axis=1)
        for f in range(0, 2 * top, 2):
            pair = jnp.concatenate(
                [charge * waves_x[f : f + 1, at], charge * waves_x[f + 1 : f + 2, at]], axis=0
            )
            upper, lower = split(pair)
            left_high[f * 8 : f * 8 + 16, :] = upper
            left_low[f * 8 : f * 8 + 16, :] = lower
        plane_high, plane_low = high[:, at], low[:, at]
        total[...] += dot_t(plane_high, left_high[...]) + (
            dot_t(plane_low, left_high[...]) + dot_t(plane_high, left_low[...])
        )
        upper, lower = split(charge)
        extra[:, 0:waves] += dot_t(upper, plane_high) + (
            dot_t(lower, plane_high) + dot_t(upper, plane_low)
        )

    paired(ranks, part, (lefts_high, lefts_low), 8)
    first = core[0] == 0
    real, imaginary = total[0:plane_rows, :], total[plane_rows:waves, :]
    begin, rest = extra[:, 0:128], extra[:, 128:256]
    for ref, one in ((mine, first), (other, jnp.logical_not(first))):
        ref[0:plane_rows, :] = jnp.where(one, real, imaginary)
        ref[plane_rows : plane_rows + 8, 0:128] = jnp.where(one, begin, rest)
        ref[plane_rows : plane_rows + 8, 128:256] = jnp.zeros((8, 128), f32)


def weight_kernel(rank, edges, got, out, lone_out):
    counts = got[0, 16:40, :]
    for z in range(1, ranks):
        counts = counts + got[z, 16:40, :]
    main, rest = counts[0:16], counts[16:24]
    line = lax.broadcasted_iota(i32, (8, 128), 0)
    lane = lax.broadcasted_iota(i32, (8, 128), 1)
    spill = jnp.where(line < 5, rest, 0.0)
    flat = jnp.where(line == 5, 1.0, 0.0)
    row = lax.broadcasted_iota(i32, (128, 128), 0)
    wave = lax.shift_right_logical(lax.broadcasted_iota(i32, (128, 128), 1), 3)

    def pick(where):
        return jnp.where(where, 1.0, 0.0)

    halves = dot_c(main, pick(row == wave)[0:16])
    both = jnp.concatenate([halves[0:64], dot_x(spill, pick(row == wave))], axis=0)
    apart = jnp.concatenate([halves[64:128], dot_x(spill, pick(row == wave + 16))], axis=0)
    zero = jnp.concatenate([dot_c(rest, flat)[0:64], dot_x(spill, pick(row == 32))], axis=0)
    shape = (plane_rows, 128)
    ky, kz = plane_of(rank[0], shape, 0)
    kx = (lax.shift_right_logical(lax.broadcasted_iota(i32, shape, 1), 3) + 1).astype(f32)
    qx, qy, qz = (tau * k / edges[d : d + 1, 0:128] for d, k in enumerate((kx, ky, kz)))
    flat_square = qy * qy + qz * qz
    square = qx * qx + flat_square

    def weigh(q):
        return (tau / atoms_all) * jnp.exp((-0.5 * gauss_width * gauss_width) * q) / q

    weight = weigh(square)
    out[0] = both * weight
    out[1] = apart * weight
    zero = zero * jnp.where(flat_square > 0.0, weigh(jnp.maximum(flat_square, 1e-6)), 0.0)
    out[2] = zero
    lane = lax.broadcasted_iota(i32, (plane_rows, own), 1)
    row = lax.broadcasted_iota(i32, (plane_rows, own), 0)
    twice = jnp.where((lane == row) | (lane == row + plane_rows), 1.0, 0.0)
    lone_out[...] = dot_c(zero[:, 0:8], twice)


def turn_table(table, blocks, table_high, table_low):
    for block in range(blocks):
        at = slice(block * 128, block * 128 + 128)
        table_high[at, 0:waves], table_low[at, 0:waves] = split(jnp.transpose(table[:, at]))


def halves_of(core, mine, other):
    first = core[0] == 0
    real = jnp.where(first, mine[0:plane_rows, :], other[0:plane_rows, :])
    imaginary = jnp.where(first, other[0:plane_rows, :], mine[0:plane_rows, :])
    tail = slice(plane_rows, plane_rows + 8)
    begin = jnp.where(first, mine[tail, 0:128], other[tail, 0:128])
    rest = jnp.where(first, other[tail, 0:128], mine[tail, 0:128])
    return real, imaginary, jnp.concatenate([begin, rest], axis=1)


def potential_kernel(
    core, mine, other, weights, lone_weights, waves_x, high, low, potential, table, table_high,
    table_low, results
):
    real, imaginary, lone = halves_of(core, mine, other)
    both, apart = weights[0], weights[1]
    real_c, real_s = real[:, 0:128], real[:, 128:256]
    imag_c, imag_s = imaginary[:, 0:128], imaginary[:, 128:256]
    upper, lower = slice(0, plane_rows), slice(plane_rows, waves)
    table[upper, 0:128] = both * real_c - apart * imag_s
    table[lower, 0:128] = both * imag_c + apart * real_s
    table[upper, 128:256] = both * real_s + apart * imag_c
    table[lower, 128:256] = both * imag_s - apart * real_c
    turn_table(table, 2, table_high, table_low)
    lone = (lone * lone_weights[...])[:, 0:waves]
    lone = jnp.concatenate([lone, jnp.zeros_like(lone)], axis=0)
    table_high[256:272, 0:waves], table_low[256:272, 0:waves] = split(lone)

    def part(z, result):
        at = pl.ds(pl.multiple_of(z * own, own), own)
        plane_high, plane_low = high[:, at], low[:, at]
        lines = table_high[0:272, 0:waves]
        result[...] = dot_n(lines, plane_high) + (
            dot_n(table_low[0:272, 0:waves], plane_high) + dot_n(lines, plane_low)
        )
        total = result[256:264, :]
        for f in range(2 * top):
            total = total + waves_x[f : f + 1, at] * result[f * 8 : f * 8 + 8, :]
        potential[z] = total

    paired(ranks, part, (results,), 8)


def gradient_kernel(
    rank, core, edges, mine, other, weights, table, got, waves_x, high, low, gradient, wide,
    table_high, table_low, results
):
    _, _, lone = halves_of(core, mine, other)
    lane = lax.broadcasted_iota(i32, (8, 128), 1)
    repeat = jnp.where((lane & 7) == lax.broadcasted_iota(i32, (8, 128), 0), 1.0, 0.0)
    lone = dot_c(lone, repeat)
    zero = weights[2]
    shape = (plane_rows, 128)
    ky, kz = plane_of(rank[0], shape, 0)
    ty, tz = tau * ky, tau * kz
    upper, lower = slice(0, plane_rows), slice(plane_rows, waves)
    for part in range(2):
        at = slice(part * 128, part * 128 + 128)
        re, im = table[upper, at], table[lower, at]
        wide[upper, at], wide[lower, at] = re, im
        for form, scale in ((1, ty), (2, tz)):
            at = slice(form * 256 + part * 128, form * 256 + part * 128 + 128)
            wide[upper, at] = scale * im
            wide[lower, at] = -(scale * re)
    re, im = zero * lone[0:plane_rows], zero * lone[plane_rows:waves]
    group = lax.shift_right_logical(lax.broadcasted_iota(i32, shape, 1), 3)
    turn = jnp.where(group == 0, ty, tz)
    wide[upper, 768:896] = turn * im
    wide[lower, 768:896] = -(turn * re)
    turn_table(wide, 7, table_high, table_low)

    def part(z, result):
        at = pl.ds(pl.multiple_of(z * own, own), own)
        plane_high, plane_low = high[:, at], low[:, at]
        lines = table_high[0:784, 0:waves]
        result[...] = dot_n(lines, plane_high) + (
            dot_n(table_low[0:784, 0:waves], plane_high) + dot_n(lines, plane_low)
        )
        total = [jnp.zeros((8, own), f32), result[768:776, :], result[776:784, :]]
        for f in range(2 * top):
            wave = waves_x[f : f + 1, at]
            for form in (1, 2):
                row = form * 256 + f * 8
                total[form] = total[form] + wave * result[row : row + 8, :]
        for k in range(top):
            cosine, sine = waves_x[k : k + 1, at], waves_x[top + k : top + k + 1, at]
            turn = tau * (k + 1)
            total[0] = total[0] + (turn * cosine) * result[(top + k) * 8 : (top + k) * 8 + 8, :]
            total[0] = total[0] - (turn * sine) * result[k * 8 : k * 8 + 8, :]
        charge = jnp.concatenate([got[z, 0:8, :], got[z, 8:16, :]], axis=1)
        for d in range(3):
            line = jnp.sum(charge * total[d], axis=0, keepdims=True) / edges[d : d + 1, :]
            gradient[z, 2 * d : 2 * d + 1, :] = line[:, 0:128]
            gradient[z, 2 * d + 1 : 2 * d + 2, :] = line[:, 128:256]

    paired(ranks, part, (results,))


def pair_kernel(ghosts, got, r0, e0, r1, e1, r2, e2, disp, listing, *refs):
    potential = got[0]
    for z in range(1, ranks):
        potential = potential + got[z]
    lefts, rights, total, pulled = refs[-4:]
    total[...] = jnp.zeros_like(total)
    pulled[...] = jnp.zeros_like(pulled)
    row_high = lax.broadcasted_iota(i32, (16, own), 0) + (16 if ghosts else 0)
    row_low = lax.broadcasted_iota(i32, (128, own), 0)

    def part(response, site, begin, j, left, right):
        to = pl.ds(pl.multiple_of(j * chunk, chunk), chunk)
        at = pl.ds(pl.multiple_of((j + begin) * chunk, chunk), chunk)
        lines = [
            jnp.sum(potential * response[j * chunk + m], axis=0, keepdims=True)
            for m in range(chunk)
        ]
        radial = site[to, :] + jnp.concatenate(lines, axis=0)
        pulls = [radial * disp[d, at, :] for d in range(3)]
        index = listing[at, :]
        low, high = index & 127, lax.shift_right_logical(index, 7)
        pieces = []
        for d in range(3):
            if not ghosts:
                pulled[d] += pulls[d]
            main = pulls[d].astype(bf16).astype(f32)
            pieces.append((main, pulls[d] - main))
        for m in range(chunk):
            lanes = slice(m * own, (m + 1) * own)
            hit = jnp.broadcast_to(high[m : m + 1, :], (16, own)) == row_high
            for piece in range(2):
                for d in range(3):
                    row = piece * 48 + d * 16
                    left[row : row + 16, lanes] = jnp.where(
                        hit, pieces[d][piece][m : m + 1, :], 0.0
                    ).astype(bf16)
            spot = jnp.broadcast_to(low[m : m + 1, :], (128, own)) == row_low
            right[:, lanes] = jnp.where(spot, 1.0, 0.0).astype(bf16)
        total[...] += dot_t(left[...], right[...])

    begin = 0
    for response, site in ((r0, e0), (r1, e1), (r2, e2)):
        count = response.shape[0] // chunk
        paired(count, functools.partial(part, response, site, begin), (lefts, rights), count)
        begin += count
    scattered = total[0:48, :] + total[48:96, :]
    if ghosts:
        cells0, cells3, mid0, mid3 = refs[:4]
        nothing = jnp.zeros((1, 128), f32)
        for u in range(4):
            for c in range(4):
                for ref, v in ((cells0, 0), (cells3, 3)):
                    spot = c * 16 + u * 4 + v
                    value = scattered[spot : spot + 1, :] if c < 3 else nothing
                    ref[u * 4 + c : u * 4 + c + 1, :] = value
        for ref, u in ((mid0, 0), (mid3, 3)):
            for j in range(2):
                for c in range(4):
                    spot = c * 16 + u * 4 + 1 + j
                    value = scattered[spot : spot + 1, :] if c < 3 else nothing
                    ref[j * 4 + c : j * 4 + c + 1, :] = value
        return
    lines, domain, direct = refs[:3]
    for z in range(ranks):
        for d in range(3):
            for half in range(2):
                spot, r = d * 16 + z * 2 + half, 2 * d + half
                domain[z, r : r + 1, :] = scattered[spot : spot + 1, :] + lines[z, r : r + 1, :]
        domain[z, 6:8, :] = jnp.zeros((2, 128), f32)
    for d in range(3):
        line = -jnp.sum(pulled[d], axis=0, keepdims=True)
        direct[2 * d : 2 * d + 1, :] = line[:, 0:128]
        direct[2 * d + 1 : 2 * d + 2, :] = line[:, 128:256]
    direct[6:8, :] = jnp.zeros((2, 128), f32)


def echo_kernel(above, below, mid0, mid3, after, send0, send3, inner0, inner1):
    for u, ref in ((0, send0), (1, inner0), (2, inner1), (3, send3)):
        both = jnp.concatenate([below[u * 4 : u * 4 + 4, :], above[u * 4 : u * 4 + 4, :]], axis=0)
        if u == 0:
            both = both + mid0[...]
        if u == 3:
            both = both + mid3[...]
        ref[...] = both


def border_back_kernel(inner0, inner1, from_left, from_right, rows, domain, out):
    cells = (inner0[...] + from_left[...], inner1[...] + from_right[...])
    row_high = lax.broadcasted_iota(i32, (16, 128), 0)
    row_low = lax.broadcasted_iota(i32, (128, 128), 0)
    total = jnp.zeros((96, 128), f32)
    for i in range(2):
        index = rows[i]
        low, high = index & 127, lax.shift_right_logical(index, 7)
        for j in range(2):
            hit = jnp.broadcast_to(high[j : j + 1, :], (16, 128)) == row_high
            spot = jnp.broadcast_to(low[j : j + 1, :], (128, 128)) == row_low
            left = []
            for part in range(2):
                for c in range(3):
                    value = cells[i][j * 4 + c : j * 4 + c + 1, :]
                    main = value.astype(bf16).astype(f32)
                    left.append(jnp.where(hit, main if part == 0 else value - main, 0.0))
            total = total + dot_t(
                jnp.concatenate(left, axis=0).astype(bf16),
                jnp.where(spot, 1.0, 0.0).astype(bf16),
            )
    total = total[0:48, :] + total[48:96, :]
    for z in range(ranks):
        lines = [total[d * 16 + z * 2 : d * 16 + z * 2 + 2, :] for d in range(3)]
        lines.append(jnp.zeros((2, 128), f32))
        out[z] = domain[z] + jnp.concatenate(lines, axis=0)


def step_kernel(edges, got, direct, place, speed, kind, kicks, force_out, place_out, speed_out):
    gradient = direct[...]
    for z in range(ranks):
        gradient = gradient + got[z]
    species = kind[...]
    mass = jnp.zeros((1, own), f32)
    for s in range(kinds):
        mass = jnp.where(species == s, masses_table[s], mass)
    retain = math.exp(-friction * time_step)
    spread = jnp.sqrt((1.0 - retain * retain) / mass)
    for d in range(3):
        row = slice(d, d + 1)
        force = -jnp.concatenate(
            [gradient[2 * d : 2 * d + 1, :], gradient[2 * d + 1 : 2 * d + 2, :]], axis=1
        )
        halfway = speed[row, :] + 0.5 * time_step * force / mass
        updated = retain * halfway + spread * kicks[row, :]
        force_out[row, :] = force
        speed_out[row, :] = updated
        place_out[row, :] = place[row, :] + 0.5 * time_step * (halfway + updated) / edges[row, :]


def shift(axis, by):
    count = lax.axis_size(axis)
    return [(i, (i + by) % count) for i in range(count)]


def add_kernel(after, *refs):
    total = refs[0][...]
    for ref in refs[1:-1]:
        total = total + ref[...]
    refs[-1][...] = total


def partners():
    places = [(x, y, c) for x in range(4) for y in range(4) for c in range(2)]

    def number(x, y, c):
        return (x % 4 * 2 + y % 2) * 4 + y % 4 // 2 * 2 + c

    swap = [(number(x, y, c), number(x, y, 1 - c)) for x, y, c in places]
    rings = [
        [[(number(x, y, c), number(x, y + d, c)) for x, y, c in places] for d in (1, 3, 2)],
        [[(number(x, y, c), number(x + d, y, c)) for x, y, c in places] for d in (1, 3, 2)],
    ]
    return swap, rings


def body(
    fractional_placements,
    particle_speeds,
    element_kinds,
    adjacent_padded_indices,
    adjacent_valid_tally,
    border_particle_rows,
    reciprocal_integer_triples,
    cell_edge_sizes,
    friction_random_kicks,
    element_feature_vectors,
    distance_net_initial_weights,
    distance_net_final_weights,
    message_blend_matrix,
    energy_head_initial_weights,
    energy_head_final_weights,
    hidden_electric_projection,
):
    rank = lax.axis_index("ka").astype(i32).reshape(1)
    core = (lax.axis_index("gy") % 2).astype(i32).reshape(1)
    def stay(array):
        return pltpu.with_memory_space_constraint(array, pltpu.HBM)

    packed, place, kind = call(
        pack_kernel,
        [((ranks, 8, 128), f32), ((3, own), f32), ((1, own), i32)],
        [far] * 2,
        [pltpu.SemaphoreType.DMA((2,))],
    )(stay(fractional_placements), stay(element_kinds.reshape(1, own)))
    table = lax.all_to_all(packed, "ka", 0, 0)
    edges, listing, tally, rows, counts, first, mixed, ball, base, final = call(
        prepare_kernel,
        [
            ((8, own), f32),
            ((slots, own), i32),
            ((1, own), i32),
            ((2, 2, 128), i32),
            ((ranks, 24, 128), f32),
            ((chunk * hidden, 192), bf16),
            ((2 * 8 * kinds, hidden), bf16),
            ((24, kinds * hidden), f32),
            ((24, 8), f32),
            ((16, 1), f32),
        ],
        [far] * 12,
        [
            pltpu.VMEM((3, reciprocal_integer_triples.shape[1]), i32),
            pltpu.VMEM((8, hidden), f32),
            pltpu.VMEM((hidden, 128), f32),
            pltpu.VMEM((8, 128), f32),
            pltpu.VMEM((128, 128), f32),
            pltpu.VMEM((24, 128), f32),
            pltpu.VMEM((1, 16), f32),
            pltpu.SMEM((3,), f32),
            pltpu.SemaphoreType.DMA((12,)),
        ],
        cost=work(8),
    )(
        *map(
            stay,
            (
                cell_edge_sizes,
                adjacent_padded_indices.T,
                adjacent_valid_tally.reshape(1, own),
                border_particle_rows,
                reciprocal_integer_triples,
                distance_net_initial_weights,
                distance_net_final_weights,
                element_feature_vectors,
                message_blend_matrix,
                energy_head_initial_weights.T,
                hidden_electric_projection.T,
                energy_head_final_weights.reshape(1, 16),
            ),
        )
    )
    cell0, cell1 = call(border_kernel, [((8, 128), f32)] * 2, [vmem] * 2)(table, rows)
    below = lax.ppermute(cell1, "gy", shift("gy", 1))
    above = lax.ppermute(cell0, "gy", shift("gy", -1))
    near = call(own_gather_kernel, [((4, slots, own), f32)], [vmem] * 2, cost=work(2))(
        table, listing
    )[0]
    head, tail = call(columns_kernel, [((16, 128), f32)] * 2, [vmem] * 4 + [anywhere])(
        below, cell0, cell1, above, near
    )
    left = lax.ppermute(tail, "gx", shift("gx", 1))
    right = lax.ppermute(head, "gx", shift("gx", -1))
    high, low, waves_x = call(
        factor_kernel,
        [((waves, ranks * own), bf16), ((waves, ranks * own), bf16), ((2 * top, ranks * own), f32)],
        [smem, vmem],
        cost=work(2),
    )(rank, table)

    send, activation, disp, marks = call(
        message_kernel,
        [
            ((ranks, 40, 128), f32),
            ((16, own), f32),
            ((3, slots, own), f32),
            ((slots, own), f32),
        ],
        [vmem] * 14 + [anywhere],
        [
            pltpu.VMEM((64, 128), f32),
            pltpu.VMEM((kinds * hidden, own), f32),
            pltpu.VMEM((8, chunk * hidden, own), f32),
        ],
        cost=work(8),
    )(
        edges, listing, near, below, above, left, right, place, kind, tally, counts, first,
        ball, base, waves_x,
    )
    got = lax.all_to_all(send, "ka", 0, 0)
    ready = (disp, marks, first, mixed)

    def respond(begin, count, operands):
        started = begin == 0
        outs = [((count * chunk, 8, own), f32), ((count * chunk, own), f32), ((8, 128), f32)]
        outs += [((kinds * hidden, own), f32)] * started
        return call(
            functools.partial(response_kernel, begin, count, started),
            outs,
            [vmem] * len(operands),
            [
                pltpu.VMEM((2, chunk * hidden, own), f32),
                pltpu.VMEM((2, chunk * hidden, own), bf16),
                pltpu.VMEM((2, chunk * hidden, own), bf16),
            ],
            cost=work(count),
        )(*operands)

    *response0, token0, upstream = respond(0, 4, (activation, final, ball) + ready)
    *response1, token1 = respond(4, 2, (upstream,) + ready)
    *response2, token2 = respond(6, 2, (upstream,) + ready)

    mine, other = call(
        structure_kernel,
        [((plane_rows + 8, own), f32)] * 2,
        [smem] + [vmem] * 4 + [anywhere],
        [
            pltpu.VMEM((waves, own), f32),
            pltpu.VMEM((8, own), f32),
            pltpu.VMEM((8, own, own), bf16),
            pltpu.VMEM((8, own, own), bf16),
        ],
        cost=work(3),
    )(core, got, waves_x, high, low, token0)
    swap, rings = partners()
    both = ("gx", "gy")

    def add(after, *parts):
        return call(
            add_kernel, [((plane_rows + 8, own), f32)], [anywhere] + [vmem] * len(parts)
        )(after, *parts)[0]

    summed = mine + lax.ppermute(other, both, swap)
    for ring, after in zip(rings, (token1, token2)):
        summed = add(after, summed, *[lax.ppermute(summed, both, turn) for turn in ring])
    opposite = lax.ppermute(summed, both, swap)
    weights, lone_weights = call(
        weight_kernel,
        [((3, plane_rows, 128), f32), ((8, own), f32)],
        [smem] + [vmem] * 2,
        cost=work(0.5),
    )(rank, edges, got)
    potential, spectrum = call(
        potential_kernel,
        [((ranks, 8, own), f32), ((waves, 256), f32)],
        [smem] + [vmem] * 7,
        [
            pltpu.VMEM((272, own), bf16),
            pltpu.VMEM((272, own), bf16),
            pltpu.VMEM((8, 272, own), f32),
        ],
        cost=work(2),
    )(core, summed, opposite, weights, lone_weights, waves_x, high, low)
    shares = lax.all_to_all(potential, "ka", 0, 0)
    lines = call(
        gradient_kernel,
        [((ranks, 8, 128), f32)],
        [smem] * 2 + [vmem] * 9,
        [
            pltpu.VMEM((waves, 896), f32),
            pltpu.VMEM((896, own), bf16),
            pltpu.VMEM((896, own), bf16),
            pltpu.VMEM((8, 784, own), f32),
        ],
        cost=work(5),
    )(rank, core, edges, summed, opposite, weights, spectrum, got, waves_x, high, low)[0]
    pairs = (shares, *response0, *response1, *response2, disp, listing)

    def pull(ghosts, outs, operands):
        return call(
            functools.partial(pair_kernel, ghosts),
            outs,
            [vmem] * len(operands),
            [
                pltpu.VMEM((4, 96, chunk * own), bf16),
                pltpu.VMEM((4, 128, chunk * own), bf16),
                pltpu.VMEM((96, 128), f32),
                pltpu.VMEM((3, chunk, own), f32),
            ],
            cost=work(2),
        )(*operands)

    cells0, cells3, mid0, mid3 = pull(
        True, [((16, 128), f32), ((16, 128), f32), ((8, 128), f32), ((8, 128), f32)], pairs
    )
    domain, direct = pull(False, [((ranks, 8, 128), f32), ((8, 128), f32)], pairs + (lines,))
    from_above = lax.ppermute(cells0, "gy", shift("gy", -1))
    from_below = lax.ppermute(cells3, "gy", shift("gy", 1))
    send0, send3, inner0, inner1 = call(
        echo_kernel, [((8, 128), f32)] * 4, [vmem] * 4 + [anywhere]
    )(from_above, from_below, mid0, mid3, domain)
    from_right = lax.ppermute(send0, "gx", shift("gx", -1))
    from_left = lax.ppermute(send3, "gx", shift("gx", 1))
    reaction = call(border_back_kernel, [((ranks, 8, 128), f32)], [vmem] * 6)(
        inner0, inner1, from_left, from_right, rows, domain
    )[0]
    returned = lax.all_to_all(reaction, "ka", 0, 0)
    forces, places, speeds = call(
        step_kernel, [((3, own), f32)] * 3, [vmem] * 7
    )(
        edges, returned, direct, place, particle_speeds, kind, friction_random_kicks,
    )
    return (forces, places, speeds)


def solution(mesh):
    atoms = ("gx", "gy", "ka")
    return jax.shard_map(
        body,
        mesh=mesh,
        in_specs=(
            P(None, atoms),
            P(None, atoms),
            P(atoms),
            P(atoms, None),
            P(atoms),
            P("gx", "gy", None),
            P(None, "ka"),
            P(),
            P(None, atoms),
            P(),
            P(),
            P(),
            P(),
            P(),
            P(),
            P(),
        ),
        out_specs=(P(None, atoms), P(None, atoms), P(None, atoms)),
        check_vma=False,
    )
```

```python
import functools
import math

import jax
import jax.numpy as jnp
from jax import lax
from jax.experimental import pallas as pl
from jax.experimental.pallas import tpu as pltpu
from jax.sharding import PartitionSpec as P

f32 = jnp.float32
bf16 = jnp.bfloat16
i32 = jnp.int32
masses_table = (1.008, 12.011, 15.999, 6.94, 30.974, 18.998)
radial_widths = (2.0, 4.0, 6.0, 8.0, 10.0, 12.0, 14.0, 16.0)
time_step = 0.5
friction = 0.2
gauss_width = 0.3
kinds = 6
slots = 64
hidden = 64
chunk = 8
chunks = slots // chunk
own = 256
ranks = 8
atoms_all = 65536
top = 16
span = 2 * top + 1
plane_rows = 72
waves = 2 * plane_rows
tau = 2.0 * math.pi
outer = [(u, v) for u in range(4) for v in range(4) if not (u in (1, 2) and v in (1, 2))]
vmem = pl.BlockSpec(memory_space=pltpu.VMEM)
smem = pl.BlockSpec(memory_space=pltpu.SMEM)
far = pl.BlockSpec(memory_space=pltpu.HBM)
anywhere = pl.BlockSpec(memory_space=pl.ANY)
params = pltpu.CompilerParams(vmem_limit_bytes=24 * 1024 * 1024)


def work(micros):
    return pl.CostEstimate(
        flops=int(micros * 5e8), bytes_accessed=int(micros * 2e6), transcendentals=0
    )


def call(kernel, outs, specs, scratch=(), cost=None):
    shapes = [jax.ShapeDtypeStruct(s, d) for s, d in outs]
    return pl.pallas_call(
        kernel,
        out_shape=shapes,
        in_specs=specs,
        out_specs=[vmem] * len(shapes),
        scratch_shapes=list(scratch),
        compiler_params=params,
        cost_estimate=cost,
    )


def dot_n(a, b):
    return lax.dot_general(a, b, (((1,), (0,)), ((), ())), preferred_element_type=f32)


def dot_t(a, b):
    return lax.dot_general(a, b, (((1,), (1,)), ((), ())), preferred_element_type=f32)


def dot_c(a, b):
    return lax.dot_general(
        a, b, (((0,), (0,)), ((), ())), precision=lax.Precision.HIGHEST, preferred_element_type=f32
    )


def dot_h(a, b):
    return lax.dot_general(
        a, b, (((1,), (1,)), ((), ())), precision=lax.Precision.HIGHEST, preferred_element_type=f32
    )


def dot_x(a, b):
    return lax.dot_general(
        a, b, (((1,), (0,)), ((), ())), precision=lax.Precision.HIGHEST, preferred_element_type=f32
    )


def split(x):
    high = x.astype(bf16)
    return high, (x - high.astype(f32)).astype(bf16)


def dot3(a, b):
    ah, al = split(a)
    bh, bl = split(b)
    return dot_n(ah, bh) + (dot_n(al, bh) + dot_n(ah, bl))


def lane_pick(row, where):
    return jnp.take_along_axis(
        jnp.broadcast_to(row, where.shape), where, axis=1, mode="promise_in_bounds"
    )


def sine_turns(w):
    square = w * w
    total = jnp.full_like(w, -(tau**11) / math.factorial(11))
    for power in (9, 7, 5, 3, 1):
        sign = -1.0 if power % 4 == 3 else 1.0
        total = total * square + sign * tau**power / math.factorial(power)
    return total * w


def circle(turns):
    t = turns - jnp.floor(turns + 0.5)
    cosine = sine_turns(0.25 - jnp.abs(t))
    folded = jnp.where(t > 0.25, 0.5 - t, jnp.where(t < -0.25, -0.5 - t, t))
    return cosine, sine_turns(folded)


def plane_of(rank, shape, axis):
    row = lax.broadcasted_iota(i32, shape, axis)
    index = jnp.where(row < 64, row + rank * 64, row + (448 + rank * 5)).astype(f32)
    first = jnp.floor((index + (top + 0.5)) * (1.0 / span))
    return first, index - span * first


def pack_kernel(place_far, kind_far, out, place, kind, done):
    copies = [
        pltpu.make_async_copy(place_far, place, done.at[0]),
        pltpu.make_async_copy(kind_far, kind, done.at[1]),
    ]
    for copy in copies:
        copy.start()
    for copy in copies:
        copy.wait()
    rows = []
    for c in range(3):
        rows += [place[c : c + 1, 0:128], place[c : c + 1, 128:256]]
    species = kind[...].astype(f32)
    rows += [species[:, 0:128], species[:, 128:256]]
    tile = jnp.concatenate(rows, axis=0)
    for z in range(ranks):
        out[z] = tile


def count_triples(triples, out):
    kx, ky, kz = (triples[d : d + 1, :].astype(f32) for d in range(3))
    code = span * ky + kz
    flip = jnp.where(code < 0.0, -1.0, 1.0)
    code = code * flip
    kx = kx * flip
    count = kx.shape[1]
    row = lax.broadcasted_iota(i32, (48, count), 0).astype(f32)
    wanted = jnp.where(row < top, row + 1.0, row - (top - 1.0))
    sign = jnp.where(kx < 0.0, -1.0, 1.0)
    value = jnp.where(row < top, 1.0, sign)
    line = jnp.where(row < 2 * top, jnp.where(jnp.abs(kx) == wanted, value, 0.0), 0.0)
    line = jnp.where((row == 2 * top) & (kx == 0.0), 1.0, line)
    number = code.astype(i32)
    owner, within = lax.shift_right_logical(number, 6), number & 63
    hit = (lax.broadcasted_iota(i32, (128, count), 0) & 63) == within
    stack = [jnp.where(owner == z, line, 0.0).astype(bf16) for z in range(ranks)]
    main = dot_t(jnp.concatenate(stack, axis=0), jnp.where(hit, 1.0, 0.0).astype(bf16))
    row = lax.broadcasted_iota(i32, (64, count), 0)
    place = row & 7
    hit = (number == 512 + 5 * lax.shift_right_logical(row, 3) + place) & (place < 5)
    rest = dot_t(jnp.where(hit, 1.0, 0.0).astype(bf16), line.astype(bf16))
    left = lax.broadcasted_iota(i32, (16, 128), 1) < 64
    for z in range(ranks):
        both = main[z * 48 : z * 48 + 48]
        out[z, 0:16, :] = jnp.where(left, both[0:16], both[16:32])
        out[z, 16:24, :] = jnp.zeros((8, 128), f32)
        out[z, 16:24, 0:48] = rest[z * 8 : z * 8 + 8]
        out[z, 21:22, 0:64] = both[32:33, 0:64]


def prepare_kernel(
    edges_far, listing_far, tally_far, rows_far, triples_far, initial_far, second_far, embed_far,
    blend_far, energy_far, project_far, final_far,
    edges_out, listing, tally, rows, counts, first, mixed, ball, base, final_out, triples, initial,
    second, embed, blend, heads, final, edges, done,
):
    embed[...] = jnp.zeros_like(embed)
    far = (
        (edges_far, edges), (listing_far, listing), (tally_far, tally), (rows_far, rows),
        (triples_far, triples), (initial_far, initial), (second_far, second),
        (embed_far, embed.at[0:kinds]), (blend_far, blend), (energy_far, heads.at[8:24]),
        (project_far, heads.at[0:8]), (final_far, final),
    )
    copies = [pltpu.make_async_copy(a, b, done.at[n]) for n, (a, b) in enumerate(far)]
    for copy in copies:
        copy.start()
    for copy in copies:
        copy.wait()
    for d in range(3):
        edges_out[d : d + 1, :] = jnp.full((1, own), 1.0, f32) * edges[d]
    edges_out[3:8, :] = jnp.zeros((5, own), f32)
    lane = lax.broadcasted_iota(i32, (8, 64), 1)
    pick = jnp.where(lax.shift_right_logical(lane, 3) == lax.broadcasted_iota(i32, (8, 64), 0), 1.0, 0.0)
    repeated = 0.5 * dot_c(initial[...], pick)
    lane = lax.broadcasted_iota(i32, (hidden, 64), 1) & 7
    blocks = jnp.concatenate(
        [jnp.where(lane == m, repeated, 0.0) for m in range(chunk)], axis=0
    )
    high, low = split(blocks)
    first[:, 0:64], first[:, 64:128], first[:, 128:192] = high, high, low
    through = dot_h(heads[...], blend[...])
    base[...] = dot_h(heads[...], embed[...])
    doubled = jnp.concatenate([second[...], second[...]], axis=0)
    left = lax.broadcasted_iota(i32, (24, 128), 1) < hidden
    responses = []
    for s in range(kinds):
        response = dot_h(through * embed[s : s + 1, :], doubled) * (1.0 / slots)
        responses.append(response)
    for t in range(kinds // 2):
        ball[:, t * 128 : (t + 1) * 128] = jnp.where(left, responses[2 * t], responses[2 * t + 1])
    high, low = split(jnp.concatenate([r[0:8, 0:hidden] for r in responses], axis=0))
    mixed[0:48, :], mixed[48:96, :] = high, low
    square = (16, 16)
    same = lax.broadcasted_iota(i32, square, 0) == lax.broadcasted_iota(i32, square, 1)
    final_out[...] = jnp.sum(
        jnp.where(same, jnp.broadcast_to(final[...], square), 0.0), axis=1, keepdims=True
    )
    count_triples(triples, counts)


def border_kernel(table, rows, cell0, cell1):
    index = jnp.concatenate([rows[0], rows[1], rows[0], rows[1]], axis=0)
    low, high = index & 127, lax.shift_right_logical(index, 7)
    for c in range(4):
        found = jnp.zeros((8, 128), f32)
        for h in range(16):
            row = table[h // 2, 2 * c + h % 2 : 2 * c + h % 2 + 1, :]
            found = jnp.where(high == h, lane_pick(row, low), found)
        for i in range(2):
            cell0[i * 4 + c : i * 4 + c + 1, :] = found[2 * i : 2 * i + 1]
            cell1[i * 4 + c : i * 4 + c + 1, :] = found[2 * i + 1 : 2 * i + 2]


def columns_kernel(below, cell0, cell1, above, after, head, tail):
    for v, ref in enumerate((below, cell0, cell1, above)):
        head[v * 4 : v * 4 + 4, :] = ref[0:4, :]
        tail[v * 4 : v * 4 + 4, :] = ref[4:8, :]


def own_gather_kernel(table, listing, near):
    def part(j):
        at = pl.ds(pl.multiple_of(j * chunk, chunk), chunk)
        for half in range(2):
            lanes = slice(half * 128, half * 128 + 128)
            index = listing[at, lanes]
            low, high = index & 127, lax.shift_right_logical(index, 7)
            found = [jnp.zeros((chunk, 128), f32)] * 4
            for h in range(16):
                hit = high == h
                for c in range(4):
                    r = 2 * c + h % 2
                    row = table[h // 2, r : r + 1, :]
                    found[c] = jnp.where(hit, lane_pick(row, low), found[c])
            for c in range(4):
                near[c, at, lanes] = found[c]

    paired(chunks, part, (), 4)


def factor_kernel(rank, table, planes, waves_x):
    shape = (plane_rows, 128)
    ky, kz = plane_of(rank[0], shape, 0)
    kx = (lax.broadcasted_iota(i32, (top, 128), 0) + 1).astype(f32)

    def part(z):
        for half in range(2):
            at = pl.ds(pl.multiple_of(z * own + half * 128, 128), 128)
            x, y, w = (table[z, 2 * c + half : 2 * c + half + 1, :] for c in range(3))
            cosine, sine = circle(ky * y + kz * w)
            both = jnp.concatenate([cosine, sine], axis=0)
            upper, lower = split(both)
            planes[0:waves, at] = upper
            planes[waves : 2 * waves, at] = lower
            cosine, sine = circle(kx * x)
            waves_x[0:top, at] = cosine
            waves_x[top : 2 * top, at] = sine

    paired(ranks, part, (), 2)


def message_kernel(
    edges, listing, near, below, above, left, right, place, kind, tally, counts, first, ball, base,
    after, send, activation, disp_out, mark_out,
    cells, pooled, actives,
):
    for u, ref in ((0, left), (3, right)):
        for v in range(4):
            for c in range(4):
                spot = c * 16 + u * 4 + v
                cells[spot : spot + 1, :] = ref[v * 4 + c : v * 4 + c + 1, :]
    for v, ref in ((0, below), (3, above)):
        for i in range(2):
            for c in range(4):
                spot = c * 16 + (1 + i) * 4 + v
                cells[spot : spot + 1, :] = ref[i * 4 + c : i * 4 + c + 1, :]
    pooled[...] = jnp.zeros_like(pooled)

    def part(j, active):
        at = pl.ds(pl.multiple_of(j * chunk, chunk), chunk)
        halves = []
        for half in range(2):
            lanes = slice(half * 128, half * 128 + 128)
            index = listing[at, lanes]
            low, high = index & 127, lax.shift_right_logical(index, 7)
            found = [near[c, at, lanes] for c in range(4)]
            for u, v in outer:
                hit = high == 16 + u * 4 + v
                for c in range(4):
                    spot = c * 16 + u * 4 + v
                    row = cells[spot : spot + 1, :]
                    found[c] = jnp.where(hit, lane_pick(row, low), found[c])
            halves.append(found)
        found = [jnp.concatenate([halves[0][c], halves[1][c]], axis=1) for c in range(4)]
        squared = jnp.zeros((chunk, own), f32)
        for d in range(3):
            offset = found[d] - place[d : d + 1, :]
            offset = offset - jnp.floor(offset + 0.5)
            offset = offset * edges[d : d + 1, :]
            disp_out[d, at, :] = offset
            squared = squared + offset * offset
        slot = lax.broadcasted_iota(i32, (chunk, own), 0) + j * chunk
        mark = jnp.where(slot < tally[...], found[3], -1.0)
        mark_out[at, :] = mark
        basis = jnp.concatenate(
            [jnp.exp(squared * (-1.0 / (w * w))) for w in radial_widths], axis=0
        )
        upper, lower = split(basis)
        half_pre = dot_n(first[...], jnp.concatenate([upper, lower, upper], axis=0))
        active[...] = half_pre + half_pre * jnp.tanh(half_pre)
        for s in range(kinds):
            total = [pooled[s * hidden + b : s * hidden + b + 8, :] for b in range(0, hidden, 8)]
            for m in range(chunk):
                hit = jnp.broadcast_to(mark[m : m + 1, :], (8, own)) == float(s)
                for n in range(hidden // 8):
                    row = m * hidden + n * 8
                    total[n] = total[n] + jnp.where(hit, active[row : row + 8, :], 0.0)
            for n in range(hidden // 8):
                pooled[s * hidden + n * 8 : s * hidden + n * 8 + 8, :] = total[n]

    paired(chunks, part, (actives,), 8)
    answers = dot3(ball[...], pooled[...])
    for s in range(kinds):
        answers = answers + base[:, s : s + 1] * jnp.where(kind[...] == s, 1.0, 0.0)
    activation[...] = answers[8:24]
    charges = answers[0:8]
    for z in range(ranks):
        send[z, 0:8, :] = charges[:, 0:128]
        send[z, 8:16, :] = charges[:, 128:256]
        send[z, 16:40, :] = counts[z]


def response_start(activation, final, ball, upstream):
    value = activation[...]
    gate = 0.5 * jnp.tanh(0.5 * value) + 0.5
    ramp = final[...] * gate * (1.0 + value * (1.0 - gate))
    upstream[...] = dot_c(ball[8:24, :], ramp)


def paired(count, part, scratch, width=2):
    def step(group, carry):
        for p in range(width):
            part(group * width + p, *[ref.at[p] for ref in scratch])
        return carry

    lax.fori_loop(0, count // width, step, 0)


def response_kernel(begin, count, first_part, *refs):
    if first_part:
        activation, final, ball, disp, marks, first, mixed = refs[:7]
        out, site, token, upstream = refs[7:11]
        response_start(activation, final, ball, upstream)
    else:
        upstream, disp, marks, first, mixed, out, site, token = refs[:8]
    token[...] = jnp.zeros_like(token)
    bends, uppers, lowers = refs[-3:]

    def part(j, bend, upper, lower):
        at = pl.ds(pl.multiple_of((j + begin) * chunk, chunk), chunk)
        mark = marks[at, :]
        squared = disp[0, at, :] * disp[0, at, :]
        squared = squared + disp[1, at, :] * disp[1, at, :] + disp[2, at, :] * disp[2, at, :]
        basis = [jnp.exp(squared * (-1.0 / (w * w))) for w in radial_widths]
        lean = [b * (-2.0 / (w * w)) for b, w in zip(basis, radial_widths)]
        ah, al = split(jnp.concatenate(basis, axis=0))
        bh, bl = split(jnp.concatenate(lean, axis=0))
        half_pre = dot_n(first[...], jnp.concatenate([ah, al, ah], axis=0))
        bent = jnp.tanh(half_pre)
        bend[...] = (
            (1.0 + bent)
            * (1.0 + half_pre * (1.0 - bent))
            * dot_n(first[...], jnp.concatenate([bh, bl, bh], axis=0))
        )
        upper[...], lower[...] = split(bend[...])
        for m in range(chunk):
            mine = jnp.broadcast_to(mark[m : m + 1, :], (8, own))
            hits = [mine == float(s) for s in range(kinds)]
            lines = slice(m * hidden, (m + 1) * hidden)
            wide = dot_n(mixed[...], upper[lines, :])
            wide = wide[0:48] + (wide[48:96] + dot_n(mixed[0:48, :], lower[lines, :]))
            total = jnp.zeros((8, own), f32)
            for s in range(kinds):
                total = jnp.where(hits[s], wide[s * 8 : s * 8 + 8], total)
            out[j * chunk + m] = total
            total = jnp.zeros((8, own), f32)
            for n in range(0, hidden, 8):
                chosen = jnp.zeros((8, own), f32)
                for s in range(kinds):
                    row = s * hidden + n
                    chosen = jnp.where(hits[s], upstream[row : row + 8, :], chosen)
                total = total + chosen * bend[m * hidden + n : m * hidden + n + 8, :]
            line = jnp.sum(total, axis=0, keepdims=True)
            site[pl.ds(j * chunk + m, 1), :] = line

    paired(count, part, (bends, uppers, lowers))


def structure_kernel(
    core, got, waves_x, planes, after, mine, other, total, extra, lefts_high, lefts_low
):
    total[...] = jnp.zeros_like(total)
    extra[...] = jnp.zeros_like(extra)

    def part(z, left_high, left_low):
        at = pl.ds(pl.multiple_of(z * own, own), own)
        charge = jnp.concatenate([got[z, 0:8, :], got[z, 8:16, :]], axis=1)
        for f in range(0, 2 * top, 2):
            pair = jnp.concatenate(
                [charge * waves_x[f : f + 1, at], charge * waves_x[f + 1 : f + 2, at]], axis=0
            )
            upper, lower = split(pair)
            left_high[f * 8 : f * 8 + 16, :] = upper
            left_low[f * 8 : f * 8 + 16, :] = lower
        plane_high, plane_low = planes[0:waves, at], planes[waves : 2 * waves, at]
        total[...] += dot_t(plane_high, left_high[...]) + (
            dot_t(plane_low, left_high[...]) + dot_t(plane_high, left_low[...])
        )
        upper, lower = split(charge)
        extra[:, 0:waves] += dot_t(upper, plane_high) + (
            dot_t(lower, plane_high) + dot_t(upper, plane_low)
        )

    paired(ranks, part, (lefts_high, lefts_low), 8)
    first = core[0] == 0
    real, imaginary = total[0:plane_rows, :], total[plane_rows:waves, :]
    begin, rest = extra[:, 0:128], extra[:, 128:256]
    for ref, one in ((mine, first), (other, jnp.logical_not(first))):
        ref[0:plane_rows, :] = jnp.where(one, real, imaginary)
        ref[plane_rows : plane_rows + 8, 0:128] = jnp.where(one, begin, rest)
        ref[plane_rows : plane_rows + 8, 128:256] = jnp.zeros((8, 128), f32)


def weight_kernel(rank, edges, got, out, lone_out):
    counts = got[0, 16:40, :]
    for z in range(1, ranks):
        counts = counts + got[z, 16:40, :]
    main, rest = counts[0:16], counts[16:24]
    line = lax.broadcasted_iota(i32, (8, 128), 0)
    lane = lax.broadcasted_iota(i32, (8, 128), 1)
    spill = jnp.where(line < 5, rest, 0.0)
    flat = jnp.where(line == 5, 1.0, 0.0)
    row = lax.broadcasted_iota(i32, (128, 128), 0)
    wave = lax.shift_right_logical(lax.broadcasted_iota(i32, (128, 128), 1), 3)

    def pick(where):
        return jnp.where(where, 1.0, 0.0)

    halves = dot_c(main, pick(row == wave)[0:16])
    both = jnp.concatenate([halves[0:64], dot_x(spill, pick(row == wave))], axis=0)
    apart = jnp.concatenate([halves[64:128], dot_x(spill, pick(row == wave + 16))], axis=0)
    zero = jnp.concatenate([dot_c(rest, flat)[0:64], dot_x(spill, pick(row == 32))], axis=0)
    shape = (plane_rows, 128)
    ky, kz = plane_of(rank[0], shape, 0)
    kx = (lax.shift_right_logical(lax.broadcasted_iota(i32, shape, 1), 3) + 1).astype(f32)
    qx, qy, qz = (tau * k / edges[d : d + 1, 0:128] for d, k in enumerate((kx, ky, kz)))
    flat_square = qy * qy + qz * qz
    square = qx * qx + flat_square

    def weigh(q):
        return (tau / atoms_all) * jnp.exp((-0.5 * gauss_width * gauss_width) * q) / q

    weight = weigh(square)
    out[0] = both * weight
    out[1] = apart * weight
    zero = zero * jnp.where(flat_square > 0.0, weigh(jnp.maximum(flat_square, 1e-6)), 0.0)
    out[2] = zero
    lane = lax.broadcasted_iota(i32, (plane_rows, own), 1)
    row = lax.broadcasted_iota(i32, (plane_rows, own), 0)
    twice = jnp.where((lane == row) | (lane == row + plane_rows), 1.0, 0.0)
    lone_out[...] = dot_c(zero[:, 0:8], twice)


def threefold(x):
    main = x.astype(bf16).astype(f32)
    return jnp.concatenate([main, main, x - main], axis=1).astype(bf16)


def turn_table(table, blocks, lines):
    for block in range(blocks):
        at = slice(block * 128, block * 128 + 128)
        lines[at, 0 : 3 * waves] = threefold(jnp.transpose(table[:, at]))


def halves_of(core, mine, other):
    first = core[0] == 0
    real = jnp.where(first, mine[0:plane_rows, :], other[0:plane_rows, :])
    imaginary = jnp.where(first, other[0:plane_rows, :], mine[0:plane_rows, :])
    tail = slice(plane_rows, plane_rows + 8)
    begin = jnp.where(first, mine[tail, 0:128], other[tail, 0:128])
    rest = jnp.where(first, other[tail, 0:128], mine[tail, 0:128])
    return real, imaginary, jnp.concatenate([begin, rest], axis=1)


def potential_kernel(
    core, mine, other, weights, lone_weights, waves_x, planes, potential, table, lines_high, lines_low,
    results
):
    real, imaginary, lone = halves_of(core, mine, other)
    both, apart = weights[0], weights[1]
    real_c, real_s = real[:, 0:128], real[:, 128:256]
    imag_c, imag_s = imaginary[:, 0:128], imaginary[:, 128:256]
    upper, lower = slice(0, plane_rows), slice(plane_rows, waves)
    table[upper, 0:128] = both * real_c - apart * imag_s
    table[lower, 0:128] = both * imag_c + apart * real_s
    table[upper, 128:256] = both * real_s + apart * imag_c
    table[lower, 128:256] = both * imag_s - apart * real_c
    for block in range(2):
        at = slice(block * 128, block * 128 + 128)
        lines_high[at, 0:waves], lines_low[at, 0:waves] = split(jnp.transpose(table[:, at]))
    lone = (lone * lone_weights[...])[:, 0:waves]
    lone = jnp.concatenate([lone, jnp.zeros_like(lone)], axis=0)
    lines_high[256:272, 0:waves], lines_low[256:272, 0:waves] = split(lone)

    def part(z, result):
        at = pl.ds(pl.multiple_of(z * own, own), own)
        plane_high = planes[0:waves, at]
        lines = lines_high[0:272, 0:waves]
        result[...] = dot_n(lines, plane_high) + (
            dot_n(lines_low[0:272, 0:waves], plane_high)
            + dot_n(lines, planes[waves : 2 * waves, at])
        )
        total = result[256:264, :]
        for f in range(2 * top):
            total = total + waves_x[f : f + 1, at] * result[f * 8 : f * 8 + 8, :]
        potential[z] = total

    paired(ranks, part, (results,), 8)


def gradient_kernel(
    rank, core, edges, mine, other, weights, table, got, waves_x, planes, gradient, wide, lines,
    tall, results
):
    _, _, lone = halves_of(core, mine, other)
    lane = lax.broadcasted_iota(i32, (8, 128), 1)
    repeat = jnp.where((lane & 7) == lax.broadcasted_iota(i32, (8, 128), 0), 1.0, 0.0)
    lone = dot_c(lone, repeat)
    zero = weights[2]
    shape = (plane_rows, 128)
    ky, kz = plane_of(rank[0], shape, 0)
    ty, tz = tau * ky, tau * kz
    upper, lower = slice(0, plane_rows), slice(plane_rows, waves)
    for part in range(2):
        at = slice(part * 128, part * 128 + 128)
        re, im = table[upper, at], table[lower, at]
        wide[upper, at], wide[lower, at] = re, im
        for form, scale in ((1, ty), (2, tz)):
            at = slice(form * 256 + part * 128, form * 256 + part * 128 + 128)
            wide[upper, at] = scale * im
            wide[lower, at] = -(scale * re)
    re, im = zero * lone[0:plane_rows], zero * lone[plane_rows:waves]
    group = lax.shift_right_logical(lax.broadcasted_iota(i32, shape, 1), 3)
    turn = jnp.where(group == 0, ty, tz)
    wide[upper, 768:896] = turn * im
    wide[lower, 768:896] = -(turn * re)
    turn_table(wide, 7, lines)
    tall[0 : 2 * waves, :] = planes[...]
    tall[2 * waves : 3 * waves, :] = planes[0:waves, :]

    def part(z, result):
        at = pl.ds(pl.multiple_of(z * own, own), own)
        result[...] = dot_n(lines[0:784, 0 : 3 * waves], tall[:, at])
        total = [jnp.zeros((8, own), f32), result[768:776, :], result[776:784, :]]
        for f in range(2 * top):
            wave = waves_x[f : f + 1, at]
            for form in (1, 2):
                row = form * 256 + f * 8
                total[form] = total[form] + wave * result[row : row + 8, :]
        for k in range(top):
            cosine, sine = waves_x[k : k + 1, at], waves_x[top + k : top + k + 1, at]
            turn = tau * (k + 1)
            total[0] = total[0] + (turn * cosine) * result[(top + k) * 8 : (top + k) * 8 + 8, :]
            total[0] = total[0] - (turn * sine) * result[k * 8 : k * 8 + 8, :]
        charge = jnp.concatenate([got[z, 0:8, :], got[z, 8:16, :]], axis=1)
        for d in range(3):
            line = jnp.sum(charge * total[d], axis=0, keepdims=True) / edges[d : d + 1, :]
            gradient[z, 2 * d : 2 * d + 1, :] = line[:, 0:128]
            gradient[z, 2 * d + 1 : 2 * d + 2, :] = line[:, 128:256]

    paired(ranks, part, (results,))


def pair_kernel(ghosts, got, r0, e0, r1, e1, r2, e2, disp, listing, *refs):
    potential = got[0]
    for z in range(1, ranks):
        potential = potential + got[z]
    lefts, rights, total, pulled = refs[-4:]
    total[...] = jnp.zeros_like(total)
    pulled[...] = jnp.zeros_like(pulled)
    height = 8 if ghosts else 24
    row = lax.broadcasted_iota(i32, (height, own), 0)
    if ghosts:
        row_high = 16 + 4 * lax.shift_right_logical(row, 1) + 3 * (row & 1)
    else:
        middle = 17 + 12 * lax.shift_right_logical(row - 16, 1) + (row & 1)
        row_high = jnp.where(row < 16, row, jnp.where(row < 20, middle, -1))
    row_low = lax.broadcasted_iota(i32, (128, own), 0)

    def part(response, site, begin, j, left, right):
        to = pl.ds(pl.multiple_of(j * chunk, chunk), chunk)
        at = pl.ds(pl.multiple_of((j + begin) * chunk, chunk), chunk)
        lines = [
            jnp.sum(potential * response[j * chunk + m], axis=0, keepdims=True)
            for m in range(chunk)
        ]
        radial = site[to, :] + jnp.concatenate(lines, axis=0)
        pulls = [radial * disp[d, at, :] for d in range(3)]
        index = listing[at, :]
        low, high = index & 127, lax.shift_right_logical(index, 7)
        pieces = []
        for d in range(3):
            if not ghosts:
                pulled[d] += pulls[d]
            main = pulls[d].astype(bf16).astype(f32)
            pieces.append((main, pulls[d] - main))
        for m in range(chunk):
            lanes = slice(m * own, (m + 1) * own)
            hit = jnp.broadcast_to(high[m : m + 1, :], (height, own)) == row_high
            blocks = [
                jnp.where(hit, pieces[d][piece][m : m + 1, :], 0.0)
                for piece in range(2)
                for d in range(3)
            ]
            left[:, lanes] = jnp.concatenate(blocks, axis=0).astype(bf16)
            spot = jnp.broadcast_to(low[m : m + 1, :], (128, own)) == row_low
            right[:, lanes] = jnp.where(spot, 1.0, 0.0).astype(bf16)
        if ghosts:
            total[...] += dot_t(right[...], left[...])
        else:
            total[...] += dot_t(left[...], right[...])

    begin = 0
    for response, site in ((r0, e0), (r1, e1), (r2, e2)):
        count = response.shape[0] // chunk
        paired(count, functools.partial(part, response, site, begin), (lefts, rights), count)
        begin += count
    whole = jnp.transpose(total[...]) if ghosts else total[...]
    scattered = whole[0 : 3 * height, :] + whole[3 * height : 6 * height, :]
    nothing = jnp.zeros((1, 128), f32)
    if ghosts:
        cells0, cells3 = refs[:2]
        for u in range(4):
            for c in range(4):
                for side, ref in ((0, cells0), (1, cells3)):
                    spot = c * 8 + u * 2 + side
                    value = scattered[spot : spot + 1, :] if c < 3 else nothing
                    ref[u * 4 + c : u * 4 + c + 1, :] = value
        return
    lines, domain, direct, mid0, mid3 = refs[:5]
    for side, ref in ((0, mid0), (1, mid3)):
        for j in range(2):
            for c in range(4):
                spot = c * 24 + 16 + side * 2 + j
                value = scattered[spot : spot + 1, :] if c < 3 else nothing
                ref[j * 4 + c : j * 4 + c + 1, :] = value
    for z in range(ranks):
        for d in range(3):
            for half in range(2):
                spot, r = d * 24 + z * 2 + half, 2 * d + half
                domain[z, r : r + 1, :] = scattered[spot : spot + 1, :] + lines[z, r : r + 1, :]
        domain[z, 6:8, :] = jnp.zeros((2, 128), f32)
    for d in range(3):
        line = -jnp.sum(pulled[d], axis=0, keepdims=True)
        direct[2 * d : 2 * d + 1, :] = line[:, 0:128]
        direct[2 * d + 1 : 2 * d + 2, :] = line[:, 128:256]
    direct[6:8, :] = jnp.zeros((2, 128), f32)


def echo_kernel(above, below, mid0, mid3, send0, send3, inner0, inner1):
    for u, ref in ((0, send0), (1, inner0), (2, inner1), (3, send3)):
        both = jnp.concatenate([below[u * 4 : u * 4 + 4, :], above[u * 4 : u * 4 + 4, :]], axis=0)
        if u == 0:
            both = both + mid0[...]
        if u == 3:
            both = both + mid3[...]
        ref[...] = both


def border_back_kernel(inner0, inner1, from_left, from_right, rows, domain, out):
    cells = (inner0[...] + from_left[...], inner1[...] + from_right[...])
    row_high = lax.broadcasted_iota(i32, (16, 128), 0)
    row_low = lax.broadcasted_iota(i32, (128, 128), 0)
    total = jnp.zeros((96, 128), f32)
    for i in range(2):
        index = rows[i]
        low, high = index & 127, lax.shift_right_logical(index, 7)
        for j in range(2):
            hit = jnp.broadcast_to(high[j : j + 1, :], (16, 128)) == row_high
            spot = jnp.broadcast_to(low[j : j + 1, :], (128, 128)) == row_low
            left = []
            for part in range(2):
                for c in range(3):
                    value = cells[i][j * 4 + c : j * 4 + c + 1, :]
                    main = value.astype(bf16).astype(f32)
                    left.append(jnp.where(hit, main if part == 0 else value - main, 0.0))
            total = total + dot_t(
                jnp.concatenate(left, axis=0).astype(bf16),
                jnp.where(spot, 1.0, 0.0).astype(bf16),
            )
    total = total[0:48, :] + total[48:96, :]
    for z in range(ranks):
        lines = [total[d * 16 + z * 2 : d * 16 + z * 2 + 2, :] for d in range(3)]
        lines.append(jnp.zeros((2, 128), f32))
        out[z] = domain[z] + jnp.concatenate(lines, axis=0)


def step_kernel(edges, got, direct, place, speed, kind, kicks, force_out, place_out, speed_out):
    gradient = direct[...]
    for z in range(ranks):
        gradient = gradient + got[z]
    species = kind[...]
    mass = jnp.zeros((1, own), f32)
    for s in range(kinds):
        mass = jnp.where(species == s, masses_table[s], mass)
    retain = math.exp(-friction * time_step)
    spread = jnp.sqrt((1.0 - retain * retain) / mass)
    for d in range(3):
        row = slice(d, d + 1)
        force = -jnp.concatenate(
            [gradient[2 * d : 2 * d + 1, :], gradient[2 * d + 1 : 2 * d + 2, :]], axis=1
        )
        halfway = speed[row, :] + 0.5 * time_step * force / mass
        updated = retain * halfway + spread * kicks[row, :]
        force_out[row, :] = force
        speed_out[row, :] = updated
        place_out[row, :] = place[row, :] + 0.5 * time_step * (halfway + updated) / edges[row, :]


def shift(axis, by):
    count = lax.axis_size(axis)
    return [(i, (i + by) % count) for i in range(count)]


def add_kernel(after, *refs):
    total = refs[0][...]
    for ref in refs[1:-1]:
        total = total + ref[...]
    refs[-1][...] = total


def partners():
    places = [(x, y, c) for x in range(4) for y in range(4) for c in range(2)]

    def number(x, y, c):
        return (x % 4 * 2 + y % 2) * 4 + y % 4 // 2 * 2 + c

    swap = [(number(x, y, c), number(x, y, 1 - c)) for x, y, c in places]
    rings = [
        [[(number(x, y, c), number(x, y + d, c)) for x, y, c in places] for d in (1, 3, 2)],
        [[(number(x, y, c), number(x + d, y, c)) for x, y, c in places] for d in (1, 3, 2)],
    ]
    return swap, rings


def body(
    fractional_placements,
    particle_speeds,
    element_kinds,
    adjacent_padded_indices,
    adjacent_valid_tally,
    border_particle_rows,
    reciprocal_integer_triples,
    cell_edge_sizes,
    friction_random_kicks,
    element_feature_vectors,
    distance_net_initial_weights,
    distance_net_final_weights,
    message_blend_matrix,
    energy_head_initial_weights,
    energy_head_final_weights,
    hidden_electric_projection,
):
    rank = lax.axis_index("ka").astype(i32).reshape(1)
    core = (lax.axis_index("gy") % 2).astype(i32).reshape(1)
    def stay(array):
        return pltpu.with_memory_space_constraint(array, pltpu.HBM)

    packed, place, kind = call(
        pack_kernel,
        [((ranks, 8, 128), f32), ((3, own), f32), ((1, own), i32)],
        [far] * 2,
        [pltpu.SemaphoreType.DMA((2,))],
    )(stay(fractional_placements), stay(element_kinds.reshape(1, own)))
    table = lax.all_to_all(packed, "ka", 0, 0)
    edges, listing, tally, rows, counts, first, mixed, ball, base, final = call(
        prepare_kernel,
        [
            ((8, own), f32),
            ((slots, own), i32),
            ((1, own), i32),
            ((2, 2, 128), i32),
            ((ranks, 24, 128), f32),
            ((chunk * hidden, 192), bf16),
            ((2 * 8 * kinds, hidden), bf16),
            ((24, kinds * hidden), f32),
            ((24, 8), f32),
            ((16, 1), f32),
        ],
        [far] * 12,
        [
            pltpu.VMEM((3, reciprocal_integer_triples.shape[1]), i32),
            pltpu.VMEM((8, hidden), f32),
            pltpu.VMEM((hidden, 128), f32),
            pltpu.VMEM((8, 128), f32),
            pltpu.VMEM((128, 128), f32),
            pltpu.VMEM((24, 128), f32),
            pltpu.VMEM((1, 16), f32),
            pltpu.SMEM((3,), f32),
            pltpu.SemaphoreType.DMA((12,)),
        ],
        cost=work(8),
    )(
        *map(
            stay,
            (
                cell_edge_sizes,
                adjacent_padded_indices.T,
                adjacent_valid_tally.reshape(1, own),
                border_particle_rows,
                reciprocal_integer_triples,
                distance_net_initial_weights,
                distance_net_final_weights,
                element_feature_vectors,
                message_blend_matrix,
                energy_head_initial_weights.T,
                hidden_electric_projection.T,
                energy_head_final_weights.reshape(1, 16),
            ),
        )
    )
    cell0, cell1 = call(border_kernel, [((8, 128), f32)] * 2, [vmem] * 2)(table, rows)
    below = lax.ppermute(cell1, "gy", shift("gy", 1))
    above = lax.ppermute(cell0, "gy", shift("gy", -1))
    near = call(own_gather_kernel, [((4, slots, own), f32)], [vmem] * 2, cost=work(2))(
        table, listing
    )[0]
    head, tail = call(columns_kernel, [((16, 128), f32)] * 2, [vmem] * 4 + [anywhere])(
        below, cell0, cell1, above, near
    )
    left = lax.ppermute(tail, "gx", shift("gx", 1))
    right = lax.ppermute(head, "gx", shift("gx", -1))
    planes, waves_x = call(
        factor_kernel,
        [((2 * waves, ranks * own), bf16), ((2 * top, ranks * own), f32)],
        [smem, vmem],
        cost=work(2),
    )(rank, table)

    send, activation, disp, marks = call(
        message_kernel,
        [
            ((ranks, 40, 128), f32),
            ((16, own), f32),
            ((3, slots, own), f32),
            ((slots, own), f32),
        ],
        [vmem] * 14 + [anywhere],
        [
            pltpu.VMEM((64, 128), f32),
            pltpu.VMEM((kinds * hidden, own), f32),
            pltpu.VMEM((8, chunk * hidden, own), f32),
        ],
        cost=work(8),
    )(
        edges, listing, near, below, above, left, right, place, kind, tally, counts, first,
        ball, base, waves_x,
    )
    got = lax.all_to_all(send, "ka", 0, 0)
    ready = (disp, marks, first, mixed)

    def respond(begin, count, operands):
        started = begin == 0
        outs = [((count * chunk, 8, own), f32), ((count * chunk, own), f32), ((8, 128), f32)]
        outs += [((kinds * hidden, own), f32)] * started
        return call(
            functools.partial(response_kernel, begin, count, started),
            outs,
            [vmem] * len(operands),
            [
                pltpu.VMEM((2, chunk * hidden, own), f32),
                pltpu.VMEM((2, chunk * hidden, own), bf16),
                pltpu.VMEM((2, chunk * hidden, own), bf16),
            ],
            cost=work(count),
        )(*operands)

    *response0, token0, upstream = respond(0, 4, (activation, final, ball) + ready)
    *response1, token1 = respond(4, 2, (upstream,) + ready)
    *response2, token2 = respond(6, 2, (upstream,) + ready)

    mine, other = call(
        structure_kernel,
        [((plane_rows + 8, own), f32)] * 2,
        [smem] + [vmem] * 3 + [anywhere],
        [
            pltpu.VMEM((waves, own), f32),
            pltpu.VMEM((8, own), f32),
            pltpu.VMEM((8, own, own), bf16),
            pltpu.VMEM((8, own, own), bf16),
        ],
        cost=work(3),
    )(core, got, waves_x, planes, token0)
    swap, rings = partners()
    both = ("gx", "gy")

    def add(after, *parts):
        return call(
            add_kernel, [((plane_rows + 8, own), f32)], [anywhere] + [vmem] * len(parts)
        )(after, *parts)[0]

    summed = mine + lax.ppermute(other, both, swap)
    for ring, after in zip(rings, (token1, token2)):
        summed = add(after, summed, *[lax.ppermute(summed, both, turn) for turn in ring])
    opposite = lax.ppermute(summed, both, swap)
    weights, lone_weights = call(
        weight_kernel,
        [((3, plane_rows, 128), f32), ((8, own), f32)],
        [smem] + [vmem] * 2,
        cost=work(0.5),
    )(rank, edges, got)
    potential, spectrum = call(
        potential_kernel,
        [((ranks, 8, own), f32), ((waves, 256), f32)],
        [smem] + [vmem] * 6,
        [
            pltpu.VMEM((272, own), bf16),
            pltpu.VMEM((272, own), bf16),
            pltpu.VMEM((8, 272, own), f32),
        ],
        cost=work(2),
    )(core, summed, opposite, weights, lone_weights, waves_x, planes)
    shares = lax.all_to_all(potential, "ka", 0, 0)
    lines = call(
        gradient_kernel,
        [((ranks, 8, 128), f32)],
        [smem] * 2 + [vmem] * 8,
        [
            pltpu.VMEM((waves, 896), f32),
            pltpu.VMEM((896, 512), bf16),
            pltpu.VMEM((3 * waves, ranks * own), bf16),
            pltpu.VMEM((8, 784, own), f32),
        ],
        cost=work(5),
    )(rank, core, edges, summed, opposite, weights, spectrum, got, waves_x, planes)[0]
    pairs = (shares, *response0, *response1, *response2, disp, listing)

    def pull(ghosts, outs, operands):
        return call(
            functools.partial(pair_kernel, ghosts),
            outs,
            [vmem] * len(operands),
            [
                pltpu.VMEM((4, 48 if ghosts else 144, chunk * own), bf16),
                pltpu.VMEM((4, 128, chunk * own), bf16),
                pltpu.VMEM((128, 48) if ghosts else (144, 128), f32),
                pltpu.VMEM((3, chunk, own), f32),
            ],
            cost=work(2),
        )(*operands)

    cells0, cells3 = pull(True, [((16, 128), f32)] * 2, pairs)
    domain, direct, mid0, mid3 = pull(
        False, [((ranks, 8, 128), f32)] + [((8, 128), f32)] * 3, pairs + (lines,)
    )
    from_above = lax.ppermute(cells0, "gy", shift("gy", -1))
    from_below = lax.ppermute(cells3, "gy", shift("gy", 1))
    send0, send3, inner0, inner1 = call(
        echo_kernel, [((8, 128), f32)] * 4, [vmem] * 4
    )(from_above, from_below, mid0, mid3)
    from_right = lax.ppermute(send0, "gx", shift("gx", -1))
    from_left = lax.ppermute(send3, "gx", shift("gx", 1))
    reaction = call(border_back_kernel, [((ranks, 8, 128), f32)], [vmem] * 6)(
        inner0, inner1, from_left, from_right, rows, domain
    )[0]
    returned = lax.all_to_all(reaction, "ka", 0, 0)
    forces, places, speeds = call(
        step_kernel, [((3, own), f32)] * 3, [vmem] * 7
    )(
        edges, returned, direct, place, particle_speeds, kind, friction_random_kicks,
    )
    return (forces, places, speeds)


def solution(mesh):
    atoms = ("gx", "gy", "ka")
    return jax.shard_map(
        body,
        mesh=mesh,
        in_specs=(
            P(None, atoms),
            P(None, atoms),
            P(atoms),
            P(atoms, None),
            P(atoms),
            P("gx", "gy", None),
            P(None, "ka"),
            P(),
            P(None, atoms),
            P(),
            P(),
            P(),
            P(),
            P(),
            P(),
            P(),
        ),
        out_specs=(P(None, atoms), P(None, atoms), P(None, atoms)),
        check_vma=False,
    )
```

```python
import functools
import math

import jax
import jax.numpy as jnp
from jax import lax
from jax.experimental import pallas as pl
from jax.experimental.pallas import tpu as pltpu
from jax.sharding import PartitionSpec as P

f32 = jnp.float32
bf16 = jnp.bfloat16
i32 = jnp.int32
masses_table = (1.008, 12.011, 15.999, 6.94, 30.974, 18.998)
radial_widths = (2.0, 4.0, 6.0, 8.0, 10.0, 12.0, 14.0, 16.0)
time_step = 0.5
friction = 0.2
gauss_width = 0.3
kinds = 6
slots = 64
hidden = 64
chunk = 8
chunks = slots // chunk
own = 256
ranks = 8
atoms_all = 65536
top = 16
span = 2 * top + 1
plane_rows = 72
waves = 2 * plane_rows
tau = 2.0 * math.pi
outer = [(u, v) for u in range(4) for v in range(4) if not (u in (1, 2) and v in (1, 2))]
vmem = pl.BlockSpec(memory_space=pltpu.VMEM)
smem = pl.BlockSpec(memory_space=pltpu.SMEM)
far = pl.BlockSpec(memory_space=pltpu.HBM)
anywhere = pl.BlockSpec(memory_space=pl.ANY)
params = pltpu.CompilerParams(vmem_limit_bytes=24 * 1024 * 1024)


def work(micros):
    return pl.CostEstimate(
        flops=int(micros * 5e8), bytes_accessed=int(micros * 2e6), transcendentals=0
    )


def call(kernel, outs, specs, scratch=(), cost=None):
    shapes = [jax.ShapeDtypeStruct(s, d) for s, d in outs]
    return pl.pallas_call(
        kernel,
        out_shape=shapes,
        in_specs=specs,
        out_specs=[vmem] * len(shapes),
        scratch_shapes=list(scratch),
        compiler_params=params,
        cost_estimate=cost,
    )


def dot_n(a, b):
    return lax.dot_general(a, b, (((1,), (0,)), ((), ())), preferred_element_type=f32)


def dot_t(a, b):
    return lax.dot_general(a, b, (((1,), (1,)), ((), ())), preferred_element_type=f32)


def dot_c(a, b):
    return lax.dot_general(
        a, b, (((0,), (0,)), ((), ())), precision=lax.Precision.HIGHEST, preferred_element_type=f32
    )


def dot_h(a, b):
    return lax.dot_general(
        a, b, (((1,), (1,)), ((), ())), precision=lax.Precision.HIGHEST, preferred_element_type=f32
    )


def dot_x(a, b):
    return lax.dot_general(
        a, b, (((1,), (0,)), ((), ())), precision=lax.Precision.HIGHEST, preferred_element_type=f32
    )


def split(x):
    high = x.astype(bf16)
    return high, (x - high.astype(f32)).astype(bf16)


def dot3(a, b):
    ah, al = split(a)
    bh, bl = split(b)
    return dot_n(ah, bh) + (dot_n(al, bh) + dot_n(ah, bl))


def lane_pick(row, where):
    return jnp.take_along_axis(
        jnp.broadcast_to(row, where.shape), where, axis=1, mode="promise_in_bounds"
    )


def sine_turns(w):
    square = w * w
    total = jnp.full_like(w, -(tau**11) / math.factorial(11))
    for power in (9, 7, 5, 3, 1):
        sign = -1.0 if power % 4 == 3 else 1.0
        total = total * square + sign * tau**power / math.factorial(power)
    return total * w


def circle(turns):
    t = turns - jnp.floor(turns + 0.5)
    cosine = sine_turns(0.25 - jnp.abs(t))
    folded = jnp.where(t > 0.25, 0.5 - t, jnp.where(t < -0.25, -0.5 - t, t))
    return cosine, sine_turns(folded)


def plane_of(rank, shape, axis):
    row = lax.broadcasted_iota(i32, shape, axis)
    index = jnp.where(row < 64, row + rank * 64, row + (448 + rank * 5)).astype(f32)
    first = jnp.floor((index + (top + 0.5)) * (1.0 / span))
    return first, index - span * first


def pack_kernel(place_far, kind_far, out, place, kind, done):
    copies = [
        pltpu.make_async_copy(place_far, place, done.at[0]),
        pltpu.make_async_copy(kind_far, kind, done.at[1]),
    ]
    for copy in copies:
        copy.start()
    for copy in copies:
        copy.wait()
    rows = []
    for c in range(3):
        rows += [place[c : c + 1, 0:128], place[c : c + 1, 128:256]]
    species = kind[...].astype(f32)
    rows += [species[:, 0:128], species[:, 128:256]]
    tile = jnp.concatenate(rows, axis=0)
    for z in range(ranks):
        out[z] = tile


def count_triples(triples, out):
    kx, ky, kz = (triples[d : d + 1, :].astype(f32) for d in range(3))
    code = span * ky + kz
    flip = jnp.where(code < 0.0, -1.0, 1.0)
    code = code * flip
    kx = kx * flip
    count = kx.shape[1]
    row = lax.broadcasted_iota(i32, (48, count), 0).astype(f32)
    wanted = jnp.where(row < top, row + 1.0, row - (top - 1.0))
    sign = jnp.where(kx < 0.0, -1.0, 1.0)
    value = jnp.where(row < top, 1.0, sign)
    line = jnp.where(row < 2 * top, jnp.where(jnp.abs(kx) == wanted, value, 0.0), 0.0)
    line = jnp.where((row == 2 * top) & (kx == 0.0), 1.0, line)
    number = code.astype(i32)
    owner, within = lax.shift_right_logical(number, 6), number & 63
    hit = (lax.broadcasted_iota(i32, (128, count), 0) & 63) == within
    stack = [jnp.where(owner == z, line, 0.0).astype(bf16) for z in range(ranks)]
    main = dot_t(jnp.concatenate(stack, axis=0), jnp.where(hit, 1.0, 0.0).astype(bf16))
    row = lax.broadcasted_iota(i32, (64, count), 0)
    place = row & 7
    hit = (number == 512 + 5 * lax.shift_right_logical(row, 3) + place) & (place < 5)
    rest = dot_t(jnp.where(hit, 1.0, 0.0).astype(bf16), line.astype(bf16))
    left = lax.broadcasted_iota(i32, (16, 128), 1) < 64
    for z in range(ranks):
        both = main[z * 48 : z * 48 + 48]
        out[z, 0:16, :] = jnp.where(left, both[0:16], both[16:32])
        out[z, 16:24, :] = jnp.zeros((8, 128), f32)
        out[z, 16:24, 0:48] = rest[z * 8 : z * 8 + 8]
        out[z, 21:22, 0:64] = both[32:33, 0:64]


def prepare_kernel(
    edges_far, listing_far, tally_far, rows_far, triples_far, initial_far, second_far, embed_far,
    blend_far, energy_far, project_far, final_far,
    edges_out, listing, tally, rows, counts, first, mixed, ball, base, final_out, triples, initial,
    second, embed, blend, heads, final, edges, done,
):
    embed[...] = jnp.zeros_like(embed)
    far = (
        (edges_far, edges), (listing_far, listing), (tally_far, tally), (rows_far, rows),
        (triples_far, triples), (initial_far, initial), (second_far, second),
        (embed_far, embed.at[0:kinds]), (blend_far, blend), (energy_far, heads.at[8:24]),
        (project_far, heads.at[0:8]), (final_far, final),
    )
    copies = [pltpu.make_async_copy(a, b, done.at[n]) for n, (a, b) in enumerate(far)]
    for copy in copies:
        copy.start()
    for copy in copies:
        copy.wait()
    for d in range(3):
        edges_out[d : d + 1, :] = jnp.full((1, own), 1.0, f32) * edges[d]
    edges_out[3:8, :] = jnp.zeros((5, own), f32)
    lane = lax.broadcasted_iota(i32, (8, 64), 1)
    pick = jnp.where(lax.shift_right_logical(lane, 3) == lax.broadcasted_iota(i32, (8, 64), 0), 1.0, 0.0)
    repeated = 0.5 * dot_c(initial[...], pick)
    lane = lax.broadcasted_iota(i32, (hidden, 64), 1) & 7
    blocks = jnp.concatenate(
        [jnp.where(lane == m, repeated, 0.0) for m in range(chunk)], axis=0
    )
    high, low = split(blocks)
    first[:, 0:64], first[:, 64:128], first[:, 128:192] = high, high, low
    through = dot_h(heads[...], blend[...])
    base[...] = dot_h(heads[...], embed[...])
    doubled = jnp.concatenate([second[...], second[...]], axis=0)
    left = lax.broadcasted_iota(i32, (24, 128), 1) < hidden
    responses = []
    for s in range(kinds):
        response = dot_h(through * embed[s : s + 1, :], doubled) * (1.0 / slots)
        responses.append(response)
    for t in range(kinds // 2):
        ball[:, t * 128 : (t + 1) * 128] = jnp.where(left, responses[2 * t], responses[2 * t + 1])
    high, low = split(jnp.concatenate([r[0:8, 0:hidden] for r in responses], axis=0))
    mixed[0:48, :], mixed[48:96, :] = high, low
    square = (16, 16)
    same = lax.broadcasted_iota(i32, square, 0) == lax.broadcasted_iota(i32, square, 1)
    final_out[...] = jnp.sum(
        jnp.where(same, jnp.broadcast_to(final[...], square), 0.0), axis=1, keepdims=True
    )
    count_triples(triples, counts)


def border_kernel(table, rows, cell0, cell1):
    index = jnp.concatenate([rows[0], rows[1], rows[0], rows[1]], axis=0)
    low, high = index & 127, lax.shift_right_logical(index, 7)
    for c in range(4):
        found = jnp.zeros((8, 128), f32)
        for h in range(16):
            row = table[h // 2, 2 * c + h % 2 : 2 * c + h % 2 + 1, :]
            found = jnp.where(high == h, lane_pick(row, low), found)
        for i in range(2):
            cell0[i * 4 + c : i * 4 + c + 1, :] = found[2 * i : 2 * i + 1]
            cell1[i * 4 + c : i * 4 + c + 1, :] = found[2 * i + 1 : 2 * i + 2]


def columns_kernel(below, cell0, cell1, above, after, head, tail):
    for v, ref in enumerate((below, cell0, cell1, above)):
        head[v * 4 : v * 4 + 4, :] = ref[0:4, :]
        tail[v * 4 : v * 4 + 4, :] = ref[4:8, :]


def own_gather_kernel(table, listing, near):
    def part(j):
        at = pl.ds(pl.multiple_of(j * chunk, chunk), chunk)
        for half in range(2):
            lanes = slice(half * 128, half * 128 + 128)
            index = listing[at, lanes]
            low, high = index & 127, lax.shift_right_logical(index, 7)
            found = [jnp.zeros((chunk, 128), f32)] * 4
            for h in range(16):
                hit = high == h
                for c in range(4):
                    r = 2 * c + h % 2
                    row = table[h // 2, r : r + 1, :]
                    found[c] = jnp.where(hit, lane_pick(row, low), found[c])
            for c in range(4):
                near[c, at, lanes] = found[c]

    paired(chunks, part, (), 4)


def factor_kernel(rank, table, planes, waves_x):
    shape = (plane_rows, 128)
    ky, kz = plane_of(rank[0], shape, 0)
    kx = (lax.broadcasted_iota(i32, (top, 128), 0) + 1).astype(f32)

    def part(z):
        for half in range(2):
            at = pl.ds(pl.multiple_of(z * own + half * 128, 128), 128)
            x, y, w = (table[z, 2 * c + half : 2 * c + half + 1, :] for c in range(3))
            cosine, sine = circle(ky * y + kz * w)
            both = jnp.concatenate([cosine, sine], axis=0)
            upper, lower = split(both)
            planes[0:waves, at] = upper
            planes[waves : 2 * waves, at] = lower
            cosine, sine = circle(kx * x)
            waves_x[0:top, at] = cosine
            waves_x[top : 2 * top, at] = sine

    paired(ranks, part, (), 2)


def message_kernel(
    edges, listing, near, below, above, left, right, place, kind, tally, counts, first, ball, base,
    after, send, activation, disp_out, mark_out,
    cells, pooled, actives,
):
    for u, ref in ((0, left), (3, right)):
        for v in range(4):
            for c in range(4):
                spot = c * 16 + u * 4 + v
                cells[spot : spot + 1, :] = ref[v * 4 + c : v * 4 + c + 1, :]
    for v, ref in ((0, below), (3, above)):
        for i in range(2):
            for c in range(4):
                spot = c * 16 + (1 + i) * 4 + v
                cells[spot : spot + 1, :] = ref[i * 4 + c : i * 4 + c + 1, :]
    pooled[...] = jnp.zeros_like(pooled)

    def part(j, active):
        at = pl.ds(pl.multiple_of(j * chunk, chunk), chunk)
        halves = []
        for half in range(2):
            lanes = slice(half * 128, half * 128 + 128)
            index = listing[at, lanes]
            low, high = index & 127, lax.shift_right_logical(index, 7)
            found = [near[c, at, lanes] for c in range(4)]
            for u, v in outer:
                hit = high == 16 + u * 4 + v
                for c in range(4):
                    spot = c * 16 + u * 4 + v
                    row = cells[spot : spot + 1, :]
                    found[c] = jnp.where(hit, lane_pick(row, low), found[c])
            halves.append(found)
        found = [jnp.concatenate([halves[0][c], halves[1][c]], axis=1) for c in range(4)]
        squared = jnp.zeros((chunk, own), f32)
        for d in range(3):
            offset = found[d] - place[d : d + 1, :]
            offset = offset - jnp.floor(offset + 0.5)
            offset = offset * edges[d : d + 1, :]
            disp_out[d, at, :] = offset
            squared = squared + offset * offset
        slot = lax.broadcasted_iota(i32, (chunk, own), 0) + j * chunk
        mark = jnp.where(slot < tally[...], found[3], -1.0)
        mark_out[at, :] = mark
        basis = jnp.concatenate(
            [jnp.exp(squared * (-1.0 / (w * w))) for w in radial_widths], axis=0
        )
        upper, lower = split(basis)
        half_pre = dot_n(first[...], jnp.concatenate([upper, lower, upper], axis=0))
        below = 1.0 + jnp.exp(-2.0 * half_pre)
        guess = pl.reciprocal(below, approx=True)
        active[...] = (2.0 * half_pre) * (guess * (2.0 - below * guess))
        for s in range(kinds):
            total = [pooled[s * hidden + b : s * hidden + b + 8, :] for b in range(0, hidden, 8)]
            for m in range(chunk):
                hit = jnp.broadcast_to(mark[m : m + 1, :], (8, own)) == float(s)
                for n in range(hidden // 8):
                    row = m * hidden + n * 8
                    total[n] = total[n] + jnp.where(hit, active[row : row + 8, :], 0.0)
            for n in range(hidden // 8):
                pooled[s * hidden + n * 8 : s * hidden + n * 8 + 8, :] = total[n]

    paired(chunks, part, (actives,), 8)
    answers = dot3(ball[...], pooled[...])
    for s in range(kinds):
        answers = answers + base[:, s : s + 1] * jnp.where(kind[...] == s, 1.0, 0.0)
    activation[...] = answers[8:24]
    charges = answers[0:8]
    for z in range(ranks):
        send[z, 0:8, :] = charges[:, 0:128]
        send[z, 8:16, :] = charges[:, 128:256]
        send[z, 16:40, :] = counts[z]


def response_start(activation, final, ball, upstream):
    value = activation[...]
    gate = 0.5 * jnp.tanh(0.5 * value) + 0.5
    ramp = final[...] * gate * (1.0 + value * (1.0 - gate))
    upstream[...] = dot_c(ball[8:24, :], ramp)


def paired(count, part, scratch, width=2):
    def step(group, carry):
        for p in range(width):
            part(group * width + p, *[ref.at[p] for ref in scratch])
        return carry

    lax.fori_loop(0, count // width, step, 0)


def response_kernel(begin, count, first_part, *refs):
    if first_part:
        activation, final, ball, disp, marks, first, mixed = refs[:7]
        out, site, token, upstream = refs[7:11]
        response_start(activation, final, ball, upstream)
    else:
        upstream, disp, marks, first, mixed, out, site, token = refs[:8]
    token[...] = jnp.zeros_like(token)
    bends, uppers, lowers = refs[-3:]

    def part(j, bend, upper, lower):
        at = pl.ds(pl.multiple_of((j + begin) * chunk, chunk), chunk)
        mark = marks[at, :]
        squared = disp[0, at, :] * disp[0, at, :]
        squared = squared + disp[1, at, :] * disp[1, at, :] + disp[2, at, :] * disp[2, at, :]
        basis = [jnp.exp(squared * (-1.0 / (w * w))) for w in radial_widths]
        lean = [b * (-2.0 / (w * w)) for b, w in zip(basis, radial_widths)]
        ah, al = split(jnp.concatenate(basis, axis=0))
        bh, bl = split(jnp.concatenate(lean, axis=0))
        half_pre = dot_n(first[...], jnp.concatenate([ah, al, ah], axis=0))
        bent = jnp.tanh(half_pre)
        bend[...] = (
            (1.0 + bent)
            * (1.0 + half_pre * (1.0 - bent))
            * dot_n(first[...], jnp.concatenate([bh, bl, bh], axis=0))
        )
        upper[...], lower[...] = split(bend[...])
        for m in range(chunk):
            mine = jnp.broadcast_to(mark[m : m + 1, :], (8, own))
            hits = [mine == float(s) for s in range(kinds)]
            lines = slice(m * hidden, (m + 1) * hidden)
            wide = dot_n(mixed[...], upper[lines, :])
            wide = wide[0:48] + (wide[48:96] + dot_n(mixed[0:48, :], lower[lines, :]))
            total = jnp.zeros((8, own), f32)
            for s in range(kinds):
                total = jnp.where(hits[s], wide[s * 8 : s * 8 + 8], total)
            out[j * chunk + m] = total
            total = jnp.zeros((8, own), f32)
            for n in range(0, hidden, 8):
                chosen = jnp.zeros((8, own), f32)
                for s in range(kinds):
                    row = s * hidden + n
                    chosen = jnp.where(hits[s], upstream[row : row + 8, :], chosen)
                total = total + chosen * bend[m * hidden + n : m * hidden + n + 8, :]
            line = jnp.sum(total, axis=0, keepdims=True)
            site[pl.ds(j * chunk + m, 1), :] = line

    paired(count, part, (bends, uppers, lowers))


def structure_kernel(
    core, got, waves_x, planes, after, mine, other, total, extra, lefts_high, lefts_low
):
    total[...] = jnp.zeros_like(total)
    extra[...] = jnp.zeros_like(extra)

    def part(z, left_high, left_low):
        at = pl.ds(pl.multiple_of(z * own, own), own)
        charge = jnp.concatenate([got[z, 0:8, :], got[z, 8:16, :]], axis=1)
        for f in range(0, 2 * top, 2):
            pair = jnp.concatenate(
                [charge * waves_x[f : f + 1, at], charge * waves_x[f + 1 : f + 2, at]], axis=0
            )
            upper, lower = split(pair)
            left_high[f * 8 : f * 8 + 16, :] = upper
            left_low[f * 8 : f * 8 + 16, :] = lower
        plane_high, plane_low = planes[0:waves, at], planes[waves : 2 * waves, at]
        total[...] += dot_t(plane_high, left_high[...]) + (
            dot_t(plane_low, left_high[...]) + dot_t(plane_high, left_low[...])
        )
        upper, lower = split(charge)
        extra[:, 0:waves] += dot_t(upper, plane_high) + (
            dot_t(lower, plane_high) + dot_t(upper, plane_low)
        )

    paired(ranks, part, (lefts_high, lefts_low), 8)
    first = core[0] == 0
    real, imaginary = total[0:plane_rows, :], total[plane_rows:waves, :]
    begin, rest = extra[:, 0:128], extra[:, 128:256]
    for ref, one in ((mine, first), (other, jnp.logical_not(first))):
        ref[0:plane_rows, :] = jnp.where(one, real, imaginary)
        ref[plane_rows : plane_rows + 8, 0:128] = jnp.where(one, begin, rest)
        ref[plane_rows : plane_rows + 8, 128:256] = jnp.zeros((8, 128), f32)


def weight_kernel(rank, edges, got, out, lone_out):
    counts = got[0, 16:40, :]
    for z in range(1, ranks):
        counts = counts + got[z, 16:40, :]
    main, rest = counts[0:16], counts[16:24]
    line = lax.broadcasted_iota(i32, (8, 128), 0)
    lane = lax.broadcasted_iota(i32, (8, 128), 1)
    spill = jnp.where(line < 5, rest, 0.0)
    flat = jnp.where(line == 5, 1.0, 0.0)
    row = lax.broadcasted_iota(i32, (128, 128), 0)
    wave = lax.shift_right_logical(lax.broadcasted_iota(i32, (128, 128), 1), 3)

    def pick(where):
        return jnp.where(where, 1.0, 0.0)

    halves = dot_c(main, pick(row == wave)[0:16])
    both = jnp.concatenate([halves[0:64], dot_x(spill, pick(row == wave))], axis=0)
    apart = jnp.concatenate([halves[64:128], dot_x(spill, pick(row == wave + 16))], axis=0)
    zero = jnp.concatenate([dot_c(rest, flat)[0:64], dot_x(spill, pick(row == 32))], axis=0)
    shape = (plane_rows, 128)
    ky, kz = plane_of(rank[0], shape, 0)
    kx = (lax.shift_right_logical(lax.broadcasted_iota(i32, shape, 1), 3) + 1).astype(f32)
    qx, qy, qz = (tau * k / edges[d : d + 1, 0:128] for d, k in enumerate((kx, ky, kz)))
    flat_square = qy * qy + qz * qz
    square = qx * qx + flat_square

    def weigh(q):
        return (tau / atoms_all) * jnp.exp((-0.5 * gauss_width * gauss_width) * q) / q

    weight = weigh(square)
    out[0] = both * weight
    out[1] = apart * weight
    zero = zero * jnp.where(flat_square > 0.0, weigh(jnp.maximum(flat_square, 1e-6)), 0.0)
    out[2] = zero
    lane = lax.broadcasted_iota(i32, (plane_rows, own), 1)
    row = lax.broadcasted_iota(i32, (plane_rows, own), 0)
    twice = jnp.where((lane == row) | (lane == row + plane_rows), 1.0, 0.0)
    lone_out[...] = dot_c(zero[:, 0:8], twice)


def threefold(x):
    main = x.astype(bf16).astype(f32)
    return jnp.concatenate([main, main, x - main], axis=1).astype(bf16)


def turn_table(table, blocks, lines):
    for block in range(blocks):
        at = slice(block * 128, block * 128 + 128)
        lines[at, 0 : 3 * waves] = threefold(jnp.transpose(table[:, at]))


def halves_of(core, mine, other):
    first = core[0] == 0
    real = jnp.where(first, mine[0:plane_rows, :], other[0:plane_rows, :])
    imaginary = jnp.where(first, other[0:plane_rows, :], mine[0:plane_rows, :])
    tail = slice(plane_rows, plane_rows + 8)
    begin = jnp.where(first, mine[tail, 0:128], other[tail, 0:128])
    rest = jnp.where(first, other[tail, 0:128], mine[tail, 0:128])
    return real, imaginary, jnp.concatenate([begin, rest], axis=1)


def potential_kernel(
    core, mine, other, weights, lone_weights, waves_x, planes, potential, table, lines_high, lines_low,
    results
):
    real, imaginary, lone = halves_of(core, mine, other)
    both, apart = weights[0], weights[1]
    real_c, real_s = real[:, 0:128], real[:, 128:256]
    imag_c, imag_s = imaginary[:, 0:128], imaginary[:, 128:256]
    upper, lower = slice(0, plane_rows), slice(plane_rows, waves)
    table[upper, 0:128] = both * real_c - apart * imag_s
    table[lower, 0:128] = both * imag_c + apart * real_s
    table[upper, 128:256] = both * real_s + apart * imag_c
    table[lower, 128:256] = both * imag_s - apart * real_c
    for block in range(2):
        at = slice(block * 128, block * 128 + 128)
        lines_high[at, 0:waves], lines_low[at, 0:waves] = split(jnp.transpose(table[:, at]))
    lone = (lone * lone_weights[...])[:, 0:waves]
    lone = jnp.concatenate([lone, jnp.zeros_like(lone)], axis=0)
    lines_high[256:272, 0:waves], lines_low[256:272, 0:waves] = split(lone)

    def part(z, result):
        at = pl.ds(pl.multiple_of(z * own, own), own)
        plane_high = planes[0:waves, at]
        lines = lines_high[0:272, 0:waves]
        result[...] = dot_n(lines, plane_high) + (
            dot_n(lines_low[0:272, 0:waves], plane_high)
            + dot_n(lines, planes[waves : 2 * waves, at])
        )
        total = result[256:264, :]
        for f in range(2 * top):
            total = total + waves_x[f : f + 1, at] * result[f * 8 : f * 8 + 8, :]
        potential[z] = total

    paired(ranks, part, (results,), 8)


def gradient_kernel(
    rank, core, edges, mine, other, weights, table, got, waves_x, planes, gradient, wide, lines,
    tall, results
):
    _, _, lone = halves_of(core, mine, other)
    lane = lax.broadcasted_iota(i32, (8, 128), 1)
    repeat = jnp.where((lane & 7) == lax.broadcasted_iota(i32, (8, 128), 0), 1.0, 0.0)
    lone = dot_c(lone, repeat)
    zero = weights[2]
    shape = (plane_rows, 128)
    ky, kz = plane_of(rank[0], shape, 0)
    ty, tz = tau * ky, tau * kz
    upper, lower = slice(0, plane_rows), slice(plane_rows, waves)
    for part in range(2):
        at = slice(part * 128, part * 128 + 128)
        re, im = table[upper, at], table[lower, at]
        wide[upper, at], wide[lower, at] = re, im
        for form, scale in ((1, ty), (2, tz)):
            at = slice(form * 256 + part * 128, form * 256 + part * 128 + 128)
            wide[upper, at] = scale * im
            wide[lower, at] = -(scale * re)
    re, im = zero * lone[0:plane_rows], zero * lone[plane_rows:waves]
    group = lax.shift_right_logical(lax.broadcasted_iota(i32, shape, 1), 3)
    turn = jnp.where(group == 0, ty, tz)
    wide[upper, 768:896] = turn * im
    wide[lower, 768:896] = -(turn * re)
    turn_table(wide, 7, lines)
    tall[0 : 2 * waves, :] = planes[...]
    tall[2 * waves : 3 * waves, :] = planes[0:waves, :]

    def part(z, result):
        at = pl.ds(pl.multiple_of(z * own, own), own)
        result[...] = dot_n(lines[0:784, 0 : 3 * waves], tall[:, at])
        total = [jnp.zeros((8, own), f32), result[768:776, :], result[776:784, :]]
        for f in range(2 * top):
            wave = waves_x[f : f + 1, at]
            for form in (1, 2):
                row = form * 256 + f * 8
                total[form] = total[form] + wave * result[row : row + 8, :]
        for k in range(top):
            cosine, sine = waves_x[k : k + 1, at], waves_x[top + k : top + k + 1, at]
            turn = tau * (k + 1)
            total[0] = total[0] + (turn * cosine) * result[(top + k) * 8 : (top + k) * 8 + 8, :]
            total[0] = total[0] - (turn * sine) * result[k * 8 : k * 8 + 8, :]
        charge = jnp.concatenate([got[z, 0:8, :], got[z, 8:16, :]], axis=1)
        for d in range(3):
            line = jnp.sum(charge * total[d], axis=0, keepdims=True) / edges[d : d + 1, :]
            gradient[z, 2 * d : 2 * d + 1, :] = line[:, 0:128]
            gradient[z, 2 * d + 1 : 2 * d + 2, :] = line[:, 128:256]

    paired(ranks, part, (results,))


def pair_kernel(ghosts, got, r0, e0, r1, e1, r2, e2, disp, listing, *refs):
    potential = got[0]
    for z in range(1, ranks):
        potential = potential + got[z]
    lefts, rights, total, pulled = refs[-4:]
    total[...] = jnp.zeros_like(total)
    pulled[...] = jnp.zeros_like(pulled)
    height = 8 if ghosts else 24
    row = lax.broadcasted_iota(i32, (height, own), 0)
    if ghosts:
        row_high = 16 + 4 * lax.shift_right_logical(row, 1) + 3 * (row & 1)
    else:
        middle = 17 + 12 * lax.shift_right_logical(row - 16, 1) + (row & 1)
        row_high = jnp.where(row < 16, row, jnp.where(row < 20, middle, -1))
    row_low = lax.broadcasted_iota(i32, (128, own), 0)

    def part(response, site, begin, j, left, right):
        to = pl.ds(pl.multiple_of(j * chunk, chunk), chunk)
        at = pl.ds(pl.multiple_of((j + begin) * chunk, chunk), chunk)
        lines = [
            jnp.sum(potential * response[j * chunk + m], axis=0, keepdims=True)
            for m in range(chunk)
        ]
        radial = site[to, :] + jnp.concatenate(lines, axis=0)
        pulls = [radial * disp[d, at, :] for d in range(3)]
        index = listing[at, :]
        low, high = index & 127, lax.shift_right_logical(index, 7)
        pieces = []
        for d in range(3):
            if not ghosts:
                pulled[d] += pulls[d]
            main = pulls[d].astype(bf16).astype(f32)
            pieces.append((main, pulls[d] - main))
        for m in range(chunk):
            lanes = slice(m * own, (m + 1) * own)
            hit = jnp.broadcast_to(high[m : m + 1, :], (height, own)) == row_high
            blocks = [
                jnp.where(hit, pieces[d][piece][m : m + 1, :], 0.0)
                for piece in range(2)
                for d in range(3)
            ]
            left[:, lanes] = jnp.concatenate(blocks, axis=0).astype(bf16)
            spot = jnp.broadcast_to(low[m : m + 1, :], (128, own)) == row_low
            right[:, lanes] = jnp.where(spot, 1.0, 0.0).astype(bf16)
        if ghosts:
            total[...] += dot_t(right[...], left[...])
        else:
            total[...] += dot_t(left[...], right[...])

    begin = 0
    for response, site in ((r0, e0), (r1, e1), (r2, e2)):
        count = response.shape[0] // chunk
        paired(count, functools.partial(part, response, site, begin), (lefts, rights), count)
        begin += count
    whole = jnp.transpose(total[...]) if ghosts else total[...]
    scattered = whole[0 : 3 * height, :] + whole[3 * height : 6 * height, :]
    nothing = jnp.zeros((1, 128), f32)
    if ghosts:
        cells0, cells3 = refs[:2]
        for u in range(4):
            for c in range(4):
                for side, ref in ((0, cells0), (1, cells3)):
                    spot = c * 8 + u * 2 + side
                    value = scattered[spot : spot + 1, :] if c < 3 else nothing
                    ref[u * 4 + c : u * 4 + c + 1, :] = value
        return
    lines, domain, direct, mid0, mid3 = refs[:5]
    for side, ref in ((0, mid0), (1, mid3)):
        for j in range(2):
            for c in range(4):
                spot = c * 24 + 16 + side * 2 + j
                value = scattered[spot : spot + 1, :] if c < 3 else nothing
                ref[j * 4 + c : j * 4 + c + 1, :] = value
    for z in range(ranks):
        for d in range(3):
            for half in range(2):
                spot, r = d * 24 + z * 2 + half, 2 * d + half
                domain[z, r : r + 1, :] = scattered[spot : spot + 1, :] + lines[z, r : r + 1, :]
        domain[z, 6:8, :] = jnp.zeros((2, 128), f32)
    for d in range(3):
        line = -jnp.sum(pulled[d], axis=0, keepdims=True)
        direct[2 * d : 2 * d + 1, :] = line[:, 0:128]
        direct[2 * d + 1 : 2 * d + 2, :] = line[:, 128:256]
    direct[6:8, :] = jnp.zeros((2, 128), f32)


def echo_kernel(above, below, mid0, mid3, send0, send3, inner0, inner1):
    for u, ref in ((0, send0), (1, inner0), (2, inner1), (3, send3)):
        both = jnp.concatenate([below[u * 4 : u * 4 + 4, :], above[u * 4 : u * 4 + 4, :]], axis=0)
        if u == 0:
            both = both + mid0[...]
        if u == 3:
            both = both + mid3[...]
        ref[...] = both


def border_back_kernel(inner0, inner1, from_left, from_right, rows, domain, out):
    cells = (inner0[...] + from_left[...], inner1[...] + from_right[...])
    row_high = lax.broadcasted_iota(i32, (16, 128), 0)
    row_low = lax.broadcasted_iota(i32, (128, 128), 0)
    total = jnp.zeros((96, 128), f32)
    for i in range(2):
        index = rows[i]
        low, high = index & 127, lax.shift_right_logical(index, 7)
        for j in range(2):
            hit = jnp.broadcast_to(high[j : j + 1, :], (16, 128)) == row_high
            spot = jnp.broadcast_to(low[j : j + 1, :], (128, 128)) == row_low
            left = []
            for part in range(2):
                for c in range(3):
                    value = cells[i][j * 4 + c : j * 4 + c + 1, :]
                    main = value.astype(bf16).astype(f32)
                    left.append(jnp.where(hit, main if part == 0 else value - main, 0.0))
            total = total + dot_t(
                jnp.concatenate(left, axis=0).astype(bf16),
                jnp.where(spot, 1.0, 0.0).astype(bf16),
            )
    total = total[0:48, :] + total[48:96, :]
    for z in range(ranks):
        lines = [total[d * 16 + z * 2 : d * 16 + z * 2 + 2, :] for d in range(3)]
        lines.append(jnp.zeros((2, 128), f32))
        out[z] = domain[z] + jnp.concatenate(lines, axis=0)


def step_kernel(edges, got, direct, place, speed, kind, kicks, force_out, place_out, speed_out):
    gradient = direct[...]
    for z in range(ranks):
        gradient = gradient + got[z]
    species = kind[...]
    mass = jnp.zeros((1, own), f32)
    for s in range(kinds):
        mass = jnp.where(species == s, masses_table[s], mass)
    retain = math.exp(-friction * time_step)
    spread = jnp.sqrt((1.0 - retain * retain) / mass)
    for d in range(3):
        row = slice(d, d + 1)
        force = -jnp.concatenate(
            [gradient[2 * d : 2 * d + 1, :], gradient[2 * d + 1 : 2 * d + 2, :]], axis=1
        )
        halfway = speed[row, :] + 0.5 * time_step * force / mass
        updated = retain * halfway + spread * kicks[row, :]
        force_out[row, :] = force
        speed_out[row, :] = updated
        place_out[row, :] = place[row, :] + 0.5 * time_step * (halfway + updated) / edges[row, :]


def shift(axis, by):
    count = lax.axis_size(axis)
    return [(i, (i + by) % count) for i in range(count)]


def add_kernel(after, *refs):
    total = refs[0][...]
    for ref in refs[1:-1]:
        total = total + ref[...]
    refs[-1][...] = total


def partners():
    places = [(x, y, c) for x in range(4) for y in range(4) for c in range(2)]

    def number(x, y, c):
        return (x % 4 * 2 + y % 2) * 4 + y % 4 // 2 * 2 + c

    swap = [(number(x, y, c), number(x, y, 1 - c)) for x, y, c in places]
    rings = [
        [[(number(x, y, c), number(x, y + d, c)) for x, y, c in places] for d in (1, 3, 2)],
        [[(number(x, y, c), number(x + d, y, c)) for x, y, c in places] for d in (1, 3, 2)],
    ]
    return swap, rings


def body(
    fractional_placements,
    particle_speeds,
    element_kinds,
    adjacent_padded_indices,
    adjacent_valid_tally,
    border_particle_rows,
    reciprocal_integer_triples,
    cell_edge_sizes,
    friction_random_kicks,
    element_feature_vectors,
    distance_net_initial_weights,
    distance_net_final_weights,
    message_blend_matrix,
    energy_head_initial_weights,
    energy_head_final_weights,
    hidden_electric_projection,
):
    rank = lax.axis_index("ka").astype(i32).reshape(1)
    core = (lax.axis_index("gy") % 2).astype(i32).reshape(1)
    def stay(array):
        return pltpu.with_memory_space_constraint(array, pltpu.HBM)

    packed, place, kind = call(
        pack_kernel,
        [((ranks, 8, 128), f32), ((3, own), f32), ((1, own), i32)],
        [far] * 2,
        [pltpu.SemaphoreType.DMA((2,))],
    )(stay(fractional_placements), stay(element_kinds.reshape(1, own)))
    table = lax.all_to_all(packed, "ka", 0, 0)
    edges, listing, tally, rows, counts, first, mixed, ball, base, final = call(
        prepare_kernel,
        [
            ((8, own), f32),
            ((slots, own), i32),
            ((1, own), i32),
            ((2, 2, 128), i32),
            ((ranks, 24, 128), f32),
            ((chunk * hidden, 192), bf16),
            ((2 * 8 * kinds, hidden), bf16),
            ((24, kinds * hidden), f32),
            ((24, 8), f32),
            ((16, 1), f32),
        ],
        [far] * 12,
        [
            pltpu.VMEM((3, reciprocal_integer_triples.shape[1]), i32),
            pltpu.VMEM((8, hidden), f32),
            pltpu.VMEM((hidden, 128), f32),
            pltpu.VMEM((8, 128), f32),
            pltpu.VMEM((128, 128), f32),
            pltpu.VMEM((24, 128), f32),
            pltpu.VMEM((1, 16), f32),
            pltpu.SMEM((3,), f32),
            pltpu.SemaphoreType.DMA((12,)),
        ],
        cost=work(8),
    )(
        *map(
            stay,
            (
                cell_edge_sizes,
                adjacent_padded_indices.T,
                adjacent_valid_tally.reshape(1, own),
                border_particle_rows,
                reciprocal_integer_triples,
                distance_net_initial_weights,
                distance_net_final_weights,
                element_feature_vectors,
                message_blend_matrix,
                energy_head_initial_weights.T,
                hidden_electric_projection.T,
                energy_head_final_weights.reshape(1, 16),
            ),
        )
    )
    cell0, cell1 = call(border_kernel, [((8, 128), f32)] * 2, [vmem] * 2)(table, rows)
    below = lax.ppermute(cell1, "gy", shift("gy", 1))
    above = lax.ppermute(cell0, "gy", shift("gy", -1))
    near = call(own_gather_kernel, [((4, slots, own), f32)], [vmem] * 2, cost=work(2))(
        table, listing
    )[0]
    head, tail = call(columns_kernel, [((16, 128), f32)] * 2, [vmem] * 4 + [anywhere])(
        below, cell0, cell1, above, near
    )
    left = lax.ppermute(tail, "gx", shift("gx", 1))
    right = lax.ppermute(head, "gx", shift("gx", -1))
    planes, waves_x = call(
        factor_kernel,
        [((2 * waves, ranks * own), bf16), ((2 * top, ranks * own), f32)],
        [smem, vmem],
        cost=work(2),
    )(rank, table)

    send, activation, disp, marks = call(
        message_kernel,
        [
            ((ranks, 40, 128), f32),
            ((16, own), f32),
            ((3, slots, own), f32),
            ((slots, own), f32),
        ],
        [vmem] * 14 + [anywhere],
        [
            pltpu.VMEM((64, 128), f32),
            pltpu.VMEM((kinds * hidden, own), f32),
            pltpu.VMEM((8, chunk * hidden, own), f32),
        ],
        cost=work(8),
    )(
        edges, listing, near, below, above, left, right, place, kind, tally, counts, first,
        ball, base, waves_x,
    )
    got = lax.all_to_all(send, "ka", 0, 0)
    ready = (disp, marks, first, mixed)

    def respond(begin, count, operands):
        started = begin == 0
        outs = [((count * chunk, 8, own), f32), ((count * chunk, own), f32), ((8, 128), f32)]
        outs += [((kinds * hidden, own), f32)] * started
        return call(
            functools.partial(response_kernel, begin, count, started),
            outs,
            [vmem] * len(operands),
            [
                pltpu.VMEM((2, chunk * hidden, own), f32),
                pltpu.VMEM((2, chunk * hidden, own), bf16),
                pltpu.VMEM((2, chunk * hidden, own), bf16),
            ],
            cost=work(count),
        )(*operands)

    *response0, token0, upstream = respond(0, 4, (activation, final, ball) + ready)
    *response1, token1 = respond(4, 2, (upstream,) + ready)
    *response2, token2 = respond(6, 2, (upstream,) + ready)

    mine, other = call(
        structure_kernel,
        [((plane_rows + 8, own), f32)] * 2,
        [smem] + [vmem] * 3 + [anywhere],
        [
            pltpu.VMEM((waves, own), f32),
            pltpu.VMEM((8, own), f32),
            pltpu.VMEM((8, own, own), bf16),
            pltpu.VMEM((8, own, own), bf16),
        ],
        cost=work(3),
    )(core, got, waves_x, planes, token0)
    swap, rings = partners()
    both = ("gx", "gy")

    def add(after, *parts):
        return call(
            add_kernel, [((plane_rows + 8, own), f32)], [anywhere] + [vmem] * len(parts)
        )(after, *parts)[0]

    summed = mine + lax.ppermute(other, both, swap)
    for ring, after in zip(rings, (token1, token2)):
        summed = add(after, summed, *[lax.ppermute(summed, both, turn) for turn in ring])
    opposite = lax.ppermute(summed, both, swap)
    weights, lone_weights = call(
        weight_kernel,
        [((3, plane_rows, 128), f32), ((8, own), f32)],
        [smem] + [vmem] * 2,
        cost=work(0.5),
    )(rank, edges, got)
    potential, spectrum = call(
        potential_kernel,
        [((ranks, 8, own), f32), ((waves, 256), f32)],
        [smem] + [vmem] * 6,
        [
            pltpu.VMEM((272, own), bf16),
            pltpu.VMEM((272, own), bf16),
            pltpu.VMEM((8, 272, own), f32),
        ],
        cost=work(2),
    )(core, summed, opposite, weights, lone_weights, waves_x, planes)
    shares = lax.all_to_all(potential, "ka", 0, 0)
    lines = call(
        gradient_kernel,
        [((ranks, 8, 128), f32)],
        [smem] * 2 + [vmem] * 8,
        [
            pltpu.VMEM((waves, 896), f32),
            pltpu.VMEM((896, 512), bf16),
            pltpu.VMEM((3 * waves, ranks * own), bf16),
            pltpu.VMEM((8, 784, own), f32),
        ],
        cost=work(5),
    )(rank, core, edges, summed, opposite, weights, spectrum, got, waves_x, planes)[0]
    pairs = (shares, *response0, *response1, *response2, disp, listing)

    def pull(ghosts, outs, operands):
        return call(
            functools.partial(pair_kernel, ghosts),
            outs,
            [vmem] * len(operands),
            [
                pltpu.VMEM((4, 48 if ghosts else 144, chunk * own), bf16),
                pltpu.VMEM((4, 128, chunk * own), bf16),
                pltpu.VMEM((128, 48) if ghosts else (144, 128), f32),
                pltpu.VMEM((3, chunk, own), f32),
            ],
            cost=work(2),
        )(*operands)

    cells0, cells3 = pull(True, [((16, 128), f32)] * 2, pairs)
    domain, direct, mid0, mid3 = pull(
        False, [((ranks, 8, 128), f32)] + [((8, 128), f32)] * 3, pairs + (lines,)
    )
    from_above = lax.ppermute(cells0, "gy", shift("gy", -1))
    from_below = lax.ppermute(cells3, "gy", shift("gy", 1))
    send0, send3, inner0, inner1 = call(
        echo_kernel, [((8, 128), f32)] * 4, [vmem] * 4
    )(from_above, from_below, mid0, mid3)
    from_right = lax.ppermute(send0, "gx", shift("gx", -1))
    from_left = lax.ppermute(send3, "gx", shift("gx", 1))
    reaction = call(border_back_kernel, [((ranks, 8, 128), f32)], [vmem] * 6)(
        inner0, inner1, from_left, from_right, rows, domain
    )[0]
    returned = lax.all_to_all(reaction, "ka", 0, 0)
    forces, places, speeds = call(
        step_kernel, [((3, own), f32)] * 3, [vmem] * 7
    )(
        edges, returned, direct, place, particle_speeds, kind, friction_random_kicks,
    )
    return (forces, places, speeds)


def solution(mesh):
    atoms = ("gx", "gy", "ka")
    return jax.shard_map(
        body,
        mesh=mesh,
        in_specs=(
            P(None, atoms),
            P(None, atoms),
            P(atoms),
            P(atoms, None),
            P(atoms),
            P("gx", "gy", None),
            P(None, "ka"),
            P(),
            P(None, atoms),
            P(),
            P(),
            P(),
            P(),
            P(),
            P(),
            P(),
        ),
        out_specs=(P(None, atoms), P(None, atoms), P(None, atoms)),
        check_vma=False,
    )
```
